512 devices in a mesh: dp: 32 (over x, y, core), tensor: 4 (over z_lo), replica: 4 (over z_hi).
Axes of the slice: x: 4, y: 4, z: 16 (z_hi: 4, z_lo: 4; z = z_hi * 4 + z_lo), core: 2. Of those that a mesh axis runs over, the one named last changes fastest.
Arguments:
- hidden_state: bfloat16 [128, 2, 128, 3584], P(('dp', 'replica'), None, None, 'tensor'), may hold values from -6 to 6
- attn_out: bfloat16 [128, 2, 128, 3584], P(('dp', 'replica'), None, None, 'tensor'), may hold values from -6 to 6
- o_weight: bfloat16 [3584, 3584], P('tensor', 'replica'), may hold values from -0.09375 to 0.09375
- norm_gain: float32 [3584], P('tensor'), may hold values from 0.1 to 1.9
- lengths: int32 [128, 2], P(('dp', 'replica')), may hold values from 32 to 128
- positive: int32 [128], P(('dp', 'replica')), may hold values from 0 to 31
Outputs:
- grad_hidden: bfloat16 [128, 2, 128, 3584], P(('dp', 'replica'), None, None, 'tensor')
- grad_attn: bfloat16 [128, 2, 128, 3584], P(('dp', 'replica'), None, None, 'tensor')
- grad_weight: bfloat16 [3584, 3584], P('tensor', 'replica')
- grad_gain: float32 [3584], P('tensor')
- loss: float32 [], replicated
The draws below stay inside these ranges and needn't reach their ends.
Inputs may be any that keep to these rules, and one draw needn't show every extreme that they name: positive indexes a passage of the query's own replica group, numbered as in the reference program.
All inputs are finite; a program needn't handle non-finite values.
Results may differ from the reference program's by a relative error of at most 0.002.
Values may be sent and summed in bfloat16 or wider, within the bound.
No kernel may reach another device: no remote copies, remote signals or barrier semaphores. Data moves between devices by JAX's collectives and lax.ppermute only.
A program may use at most 128 MiB of HBM per device.

```python
import jax
import jax.numpy as jnp
from jax import lax

D = 3584
PAIRS_DEV = 1
SEQ = 128
GROUP = 32
PAIRS = 128
N_DP = 32
N_REPLICA = 4


def set_ends(result, key, low, high):
    extent = result.shape
    place = [jax.random.randint(jax.random.fold_in(key, axis), (), 0, extent[axis]) for axis in range(len(extent))]
    result = result.at[tuple(place)].set(low)
    longest = extent.index(max(extent))
    place[longest] = (place[longest] + 1) % extent[longest]
    return result.at[tuple(place)].set(high)


def level_of(stream_key, extent, pieces, smallest, largest):
    factor_of, own = 1.0, jax.random.fold_in(stream_key, 6)
    for dim, parts in pieces:
        draws = jnp.exp(jax.random.uniform(jax.random.fold_in(own, dim), (parts,), jnp.float32, smallest / len(pieces), largest / len(pieces)))
        factor_of = factor_of * jnp.repeat(draws, extent[dim] // parts).reshape([-1 if axis == dim else 1 for axis in range(len(extent))])
    return factor_of


def noise(rng, shape, width, most, pieces=(), kind=jnp.bfloat16):
    entries = jax.random.normal(rng, shape, jnp.float32) * width
    if len(pieces) > 0:
        entries = level_of(rng, shape, pieces, -0.22, 0.18) * entries
    return jnp.clip(entries, min=-most, max=most).astype(kind)


def setup_inputs(seed: int = 0) -> dict:
    seeds = jax.random.split(jax.random.key(seed), 7)
    hidden_state = noise(seeds[0], (PAIRS, 2, SEQ, D), 1.0, 6.0, ((0, 128), (3, 4)))
    attn_out = noise(seeds[1], (PAIRS, 2, SEQ, D), 1.0, 6.0, ((0, 128), (3, 4)))
    o_weight = noise(seeds[2], (D, D), D ** -0.5, 0.09375, ((0, 4), (1, 4)))
    norm_gain = jnp.clip(1.0 + 0.18 * jax.random.normal(seeds[3], (D,), jnp.float32), 0.1, 1.9)
    lengths = set_ends(jax.random.randint(seeds[4], (PAIRS, 2), SEQ // 4, SEQ + 1), jax.random.fold_in(seeds[4], 1), SEQ // 4, SEQ).astype(jnp.int32)
    positive = set_ends(jax.random.randint(seeds[5], (PAIRS,), 0, PAIRS_DEV * N_DP), jax.random.fold_in(seeds[5], 1), 0, (PAIRS_DEV * N_DP) - 1).astype(jnp.int32)
    return {"hidden_state": hidden_state, "attn_out": attn_out, "o_weight": o_weight, "norm_gain": norm_gain, "lengths": lengths, "positive": positive}


logit_scale = 20.0
grad_scale = 256.0
epsilon = 1e-06

def pooled(states, gain_vec, mask_row, count_row):
    inv_rms = lax.rsqrt(lax.optimization_barrier(jnp.mean(states * states, -1, keepdims=True)) + epsilon)
    normed = states * inv_rms * gain_vec
    return lax.optimization_barrier(jnp.sum(normed * mask_row[..., None], -2)) / count_row[..., None]

def reference(hidden_state, attn_out, o_weight, norm_gain, lengths, positive):
    highest = lax.Precision.HIGHEST
    gain_vec = norm_gain.astype(jnp.float32)
    positions = jnp.arange(SEQ, dtype=jnp.int32)
    valid_mask = (positions[None, None, :] < lengths[:, :, None]).astype(jnp.float32)
    token_count = lengths.astype(jnp.float32)

    def embed_one(items):
        states, mask_row, count_row = items
        return pooled(states.astype(jnp.float32), gain_vec, mask_row, count_row)
    embeds = lax.map(embed_one, (hidden_state, valid_mask, token_count))
    inv_norm = lax.rsqrt(lax.optimization_barrier(jnp.sum(embeds * embeds, -1, keepdims=True)) + epsilon)
    unit_emb = embeds * inv_norm
    groups = unit_emb.reshape(N_DP, N_REPLICA, PAIRS_DEV, 2, D).transpose(1, 0, 2, 3, 4).reshape(N_REPLICA, GROUP, 2, D)
    targets = positive.reshape(N_DP, N_REPLICA, PAIRS_DEV).transpose(1, 0, 2).reshape(N_REPLICA, GROUP)
    queries = groups[:, :, 0]
    passages = groups[:, :, 1]
    logits = logit_scale * jnp.einsum('rqd,rpd->rqp', queries, passages, precision=highest)
    log_total = jnp.log(lax.optimization_barrier(jnp.sum(jnp.exp(logits), -1)))
    one_hot = (jnp.arange(GROUP, dtype=jnp.int32)[None, None, :] == targets[:, :, None]).astype(jnp.float32)
    chosen = lax.optimization_barrier(jnp.sum(logits * one_hot, -1))
    loss = jnp.sum(log_total - chosen)
    score_grad = grad_scale * (jnp.exp(logits - log_total[..., None]) - one_hot)
    query_grad = logit_scale * jnp.einsum('rqp,rpd->rqd', score_grad, passages, precision=highest)
    passage_grad = logit_scale * jnp.einsum('rqp,rqd->rpd', score_grad, queries, precision=highest)
    embed_grad = jnp.stack([query_grad, passage_grad], 2)
    embed_grad = embed_grad.reshape(N_REPLICA, N_DP, PAIRS_DEV, 2, D).transpose(1, 0, 2, 3, 4).reshape(PAIRS, 2, D)
    along = lax.optimization_barrier(jnp.sum(unit_emb * embed_grad, -1, keepdims=True))
    pooled_grad = (embed_grad - unit_emb * along) * inv_norm
    weight32 = o_weight.astype(jnp.float32)

    def per_pair(carry, items):
        weight_acc, gain_acc = carry
        states, attn, mask_row, count_row, pool_row = items
        states = states.astype(jnp.float32)
        inv_rms = lax.rsqrt(lax.optimization_barrier(jnp.mean(states * states, -1, keepdims=True)) + epsilon)
        normed_grad = mask_row[..., None] * (pool_row / count_row[:, None])[:, None, :]
        scaled_grad = gain_vec * normed_grad
        norm_term = lax.optimization_barrier(jnp.mean(scaled_grad * states, -1, keepdims=True))
        state_grad = inv_rms * scaled_grad - states * (inv_rms * inv_rms * inv_rms) * norm_term
        grad_rounded = state_grad.astype(jnp.bfloat16)
        flat_grad = state_grad.reshape(2 * SEQ, D)
        flat_attn = attn.reshape(2 * SEQ, D).astype(jnp.float32)
        weight_acc = weight_acc + jnp.dot(flat_attn.T, flat_grad, precision=highest)
        gain_acc = gain_acc + lax.optimization_barrier(jnp.sum(normed_grad * states * inv_rms, (0, 1)))
        attn_grad = jnp.dot(flat_grad, weight32.T, precision=highest).astype(jnp.bfloat16).reshape(2, SEQ, D)
        return ((weight_acc, gain_acc), (grad_rounded, attn_grad))
    start = (jnp.zeros((D, D), jnp.float32), jnp.zeros((D,), jnp.float32))
    (weight_acc, gain_acc), (grad_hidden, grad_attn) = lax.scan(per_pair, start, (hidden_state, attn_out, valid_mask, token_count, pooled_grad))
    return (grad_hidden, grad_attn, weight_acc.astype(jnp.bfloat16), gain_acc, loss)
```

```python
import jax
import jax.numpy as jnp
from jax import lax
from jax.sharding import Mesh, PartitionSpec as P

logit_scale = 20.0
grad_scale = 256.0
epsilon = 1e-06

f32 = jnp.float32
bf16 = jnp.bfloat16

NX, NY, NC, NT, NR = 4, 4, 2, 4, 4
PLANE = ("x", "y")
DP = ("x", "y", "c")

D = 3584
FEAT = D // NT
COLS = D // NR
SEQ = 128
TOK = 2 * SEQ
HALF = FEAT // NC
SLICE = HALF // (NX * NY)
W_ROWS = FEAT // (NY * NC)

AT_RMS = D
AT_U = D + SEQ
AT_LEN = AT_U + SLICE
AT_POS = AT_LEN + 1
WIDTH = D + 2 * SEQ


def swap_core(value):
    return lax.ppermute(value, "c", [(0, 1), (1, 0)])


def split3(value):
    high = lax.reduce_precision(value, 8, 7)
    rest = value - high
    mid = lax.reduce_precision(rest, 8, 7)
    low = rest - mid
    return high.astype(bf16), mid.astype(bf16), low.astype(bf16)


def body(hidden_state, attn_out, o_weight, norm_gain, lengths, positive):
    highest = lax.Precision.HIGHEST
    ix, iy, ic = lax.axis_index("x"), lax.axis_index("y"), lax.axis_index("c")
    it, ir = lax.axis_index("t"), lax.axis_index("r")
    dp_index = (ix * NY + iy) * NC + ic

    state = hidden_state.reshape(TOK, FEAT)
    attn = attn_out.reshape(TOK, FEAT)
    state_all = lax.all_gather(state, "t")
    w_start = (iy * NC + ic) * W_ROWS
    w_mine = lax.dynamic_slice(o_weight, (w_start, 0), (W_ROWS, COLS))
    w_moved = lax.ppermute(
        w_mine,
        ("x", "r"),
        [(i * NR + (j + i) % NR, i * NR + j) for i in range(NX) for j in range(NR)],
    )
    w_all = lax.all_gather(w_moved, DP).reshape(NX, FEAT, COLS)
    attn_keep = jnp.where(ic == 0, attn[:, :HALF], attn[:, HALF:])
    attn_give = jnp.where(ic == 0, attn[:, HALF:], attn[:, :HALF])
    attn_other = swap_core(attn_give)

    states = state.astype(f32).reshape(2, SEQ, FEAT)
    square = lax.psum(jnp.sum(states * states, -1), "t") / D
    inv_rms = lax.rsqrt(square + epsilon)
    token_count = lengths.reshape(2).astype(f32)
    valid = (jnp.arange(SEQ, dtype=jnp.int32)[None, :] < lengths.reshape(2)[:, None]).astype(f32)
    pool_weight = valid * inv_rms / token_count[:, None]
    pooled = jnp.sum(pool_weight[..., None] * states, 1)
    attn_pool = jnp.sum(pool_weight[..., None] * attn.astype(f32).reshape(2, SEQ, FEAT), 1)

    near = jnp.concatenate([pooled, norm_gain[None]], 0)
    near = lax.all_to_all(jnp.broadcast_to(near[None], (NT, 3, FEAT)), "t", 0, 0)
    pooled_row = near[:, :2].transpose(1, 0, 2).reshape(2, D)
    gain = near[:, 2].reshape(D)

    u_parts = attn_pool.reshape(2, NC, NX * NY, SLICE).transpose(2, 1, 0, 3)
    u_parts = u_parts.reshape(NX * NY * NC, 2, SLICE)
    extra = jnp.stack(
        [token_count, jnp.broadcast_to(positive.astype(f32), (2,))], -1
    )
    row = jnp.concatenate([pooled_row, inv_rms], -1)
    group = NX * NY * NC
    send = jnp.concatenate(
        [
            jnp.broadcast_to(row[None], (group, 2, D + SEQ)),
            u_parts,
            jnp.broadcast_to(extra[None], (group, 2, 2)),
            jnp.zeros((group, 2, WIDTH - AT_POS - 1), f32),
        ],
        -1,
    )
    got = lax.all_to_all(send, DP, 0, 0)

    raw = got[..., :D]
    embeds = raw * gain
    inv_norm = lax.rsqrt(jnp.sum(embeds * embeds, -1, keepdims=True) + epsilon)
    unit = embeds * inv_norm
    query, passage = unit[:, 0], unit[:, 1]
    target = got[:, 0, AT_POS].astype(jnp.int32)
    contract_last = (((1,), (1,)), ((), ()))
    contract_first = (((0,), (0,)), ((), ()))
    logits = logit_scale * lax.dot_general(query, passage, contract_last, precision=highest)
    log_total = jnp.log(jnp.sum(jnp.exp(logits), -1))
    one_hot = (jnp.arange(group, dtype=jnp.int32)[None, :] == target[:, None]).astype(f32)
    loss_part = jnp.sum(log_total - jnp.sum(logits * one_hot, -1))
    score_grad = grad_scale * (jnp.exp(logits - log_total[:, None]) - one_hot)
    query_grad = logit_scale * jnp.dot(score_grad, passage, precision=highest)
    passage_grad = logit_scale * lax.dot_general(
        score_grad, query, contract_first, precision=highest
    )
    embed_grad = jnp.stack([query_grad, passage_grad], 1)
    along = jnp.sum(unit * embed_grad, -1, keepdims=True)
    pooled_grad = (embed_grad - unit * along) * inv_norm
    gain_part = jnp.sum(pooled_grad * raw, (0, 1))
    scaled = pooled_grad * gain
    gain_mine = lax.dynamic_slice(gain_part, (it * FEAT,), (FEAT,))
    totals = lax.psum(jnp.concatenate([gain_mine, loss_part[None]]), "r")

    other_index = dp_index + 1 - 2 * ic
    state_other = swap_core(state_all)
    rows = jnp.stack([scaled[dp_index], scaled[other_index]])
    counts = jnp.stack([got[dp_index, :, AT_LEN], got[other_index, :, AT_LEN]])
    rms = jnp.stack([got[dp_index, :, AT_RMS:AT_U], got[other_index, :, AT_RMS:AT_U]])
    place = jnp.arange(SEQ, dtype=jnp.int32).astype(f32)
    first_coef = jnp.where(place < counts[..., None], rms / counts[..., None], 0.0)
    both = jnp.stack([state_all, state_other]).reshape(2, NT, 2, SEQ, FEAT)
    inner = jnp.einsum(
        "ptskf,pstf->psk",
        both.astype(f32),
        rows.reshape(2, 2, NT, FEAT),
        precision=highest,
    )
    coef = first_coef * rms * rms * inner / D

    attn_pair = jnp.stack([attn_keep, attn_other]).astype(f32)
    attn_scaled = (attn_pair * coef.reshape(2, TOK, 1)).astype(bf16).reshape(2 * TOK, HALF)
    flat_states = both.reshape(2, NT, TOK, FEAT)
    parts = []
    for block in range(NR):
        block_states = flat_states[:, block].reshape(2 * TOK, FEAT)
        part = lax.dot_general(
            attn_scaled, block_states, contract_first, preferred_element_type=f32
        )
        parts.append(part.astype(bf16).reshape(NX * NY, 1, SLICE, COLS))
    partial = jnp.concatenate(parts, 1).reshape(NX * NY, NR * SLICE, COLS)
    spread = lax.all_to_all(partial, PLANE, 0, 0)
    second = jnp.sum(spread.astype(f32), 0).reshape(NR, SLICE, COLS)

    u_all = got[..., AT_U:AT_LEN].reshape(2 * group, SLICE)
    first = lax.dot_general(
        u_all, scaled.reshape(2 * group, D), contract_first, precision=highest
    )
    mine = first.reshape(SLICE, NR, COLS).transpose(1, 0, 2) - second
    total = lax.dynamic_index_in_dim(mine, ir, 0, keepdims=False)
    for step in range(1, NR):
        outgoing = lax.dynamic_index_in_dim(mine, (ir + step) % NR, 0, keepdims=False)
        total = total + lax.ppermute(
            outgoing, "r", [(j, (j + step) % NR) for j in range(NR)]
        )
    done = jnp.broadcast_to(total.astype(bf16)[None], (NX * NY, SLICE, COLS))
    half = lax.all_to_all(done, PLANE, 0, 0).reshape(HALF, COLS)
    half_other = swap_core(half)
    grad_weight = jnp.where(
        ic == 0,
        jnp.concatenate([half, half_other], 0),
        jnp.concatenate([half_other, half], 0),
    )

    own_first = first_coef[0]
    own_coef = coef[0]
    own_rows = rows[0].reshape(2, NT, FEAT)
    row_here = lax.dynamic_index_in_dim(own_rows, it, 1, keepdims=False)
    state_grad = own_first[..., None] * row_here[:, None, :] - states * own_coef[..., None]
    grad_hidden = state_grad.astype(bf16).reshape(1, 2, SEQ, FEAT)

    pieces = jnp.stack(split3(own_rows)).reshape(6, NT, FEAT)
    token_part = jnp.zeros((TOK, FEAT), f32)
    row_part = jnp.zeros((6, FEAT), f32)
    for block in range(NX):
        which = (ir + block) % NR
        token_part = token_part + lax.dot_general(
            lax.dynamic_index_in_dim(state_all, which, 0, keepdims=False),
            w_all[block],
            contract_last,
            preferred_element_type=f32,
        )
        row_part = row_part + lax.dot_general(
            lax.dynamic_index_in_dim(pieces, which, 1, keepdims=False),
            w_all[block],
            contract_last,
            preferred_element_type=f32,
        )
    row_sum = jnp.sum(row_part.reshape(3, 2, FEAT)[::-1], 0)
    attn_grad = (
        own_first[..., None] * row_sum[:, None, :]
        - token_part.reshape(2, SEQ, FEAT) * own_coef[..., None]
    )
    grad_attn = attn_grad.astype(bf16).reshape(1, 2, SEQ, FEAT)
    return (grad_hidden, grad_attn, grad_weight, totals[:FEAT], totals[FEAT])


def solution(mesh):
    fine = Mesh(mesh.devices.reshape(NX, NY, NC, NT, NR), ("x", "y", "c", "t", "r"))
    pairs = ("x", "y", "c", "r")
    placed = (
        P(pairs, None, None, "t"),
        P(pairs, None, None, "t"),
        P("t", "r"),
        P("t"),
        P(pairs, None),
        P(pairs),
    )
    return jax.shard_map(
        body,
        mesh=fine,
        in_specs=placed,
        out_specs=(
            P(pairs, None, None, "t"),
            P(pairs, None, None, "t"),
            P("t", "r"),
            P("t"),
            P(),
        ),
        check_vma=False,
    )
```

```python
import jax
import jax.numpy as jnp
from jax import lax
from jax.experimental import pallas as pl
from jax.experimental.pallas import tpu as pltpu
from jax.sharding import Mesh, PartitionSpec as P

logit_scale = 20.0
grad_scale = 256.0
epsilon = 1e-06

f32 = jnp.float32
bf16 = jnp.bfloat16

NX, NY, NC, NT, NR = 4, 4, 2, 4, 4
PLANE = ("x", "y")
DP = ("x", "y", "c")

D = 3584
FEAT = D // NT
COLS = D // NR
SEQ = 128
TOK = 2 * SEQ
HALF = FEAT // NC
SLICE = HALF // (NX * NY)
W_ROWS = HALF // NY
PIECES = 16

AT_RMS = D
AT_U = D + SEQ
AT_LEN = AT_U + SLICE
AT_POS = AT_LEN + 1
WIDTH = D + 2 * SEQ


def swap_core(value):
    return lax.ppermute(value, "c", [(0, 1), (1, 0)])


def split3(value):
    high = lax.reduce_precision(value, 8, 7)
    rest = value - high
    mid = lax.reduce_precision(rest, 8, 7)
    low = rest - mid
    return high.astype(bf16), mid.astype(bf16), low.astype(bf16)


contract_last = (((1,), (1,)), ((), ()))
contract_first = (((0,), (0,)), ((), ()))


def dot_last(left, right):
    return lax.dot_general(left, right, contract_last, preferred_element_type=f32)


def weight_kernel(
    own_ref, other_ref, keep_ref, given_ref, pieces_ref, scale_ref, out_ref, coef_ref, acc_ref
):
    token = lax.broadcasted_iota(jnp.int32, (TOK, PIECES), 0)
    part = lax.broadcasted_iota(jnp.int32, (TOK, PIECES), 1)
    part = part - jnp.where(token < SEQ, 0, 3)
    mask = (part >= 0) & (part < 3)
    scaled = []
    for pair, (state_ref, attn_ref) in enumerate(
        ((own_ref, keep_ref), (other_ref, given_ref))
    ):
        inner = jnp.zeros((TOK, PIECES), f32)
        for block in range(NT):
            inner = inner + dot_last(state_ref[block], pieces_ref[pair, block])
        inner = jnp.sum(jnp.where(mask, inner, 0.0), -1, keepdims=True)
        coef = scale_ref[pair] * inner
        coef_ref[pair] = coef
        scaled.append((attn_ref[...].astype(f32) * coef).astype(bf16))
    for block in range(NT):
        acc_ref[block] = lax.dot_general(
            scaled[0], own_ref[block], contract_first, preferred_element_type=f32
        ) + lax.dot_general(
            scaled[1], other_ref[block], contract_first, preferred_element_type=f32
        )
    for place in range(NX * NY):
        rows = [
            acc_ref[block, place * SLICE : (place + 1) * SLICE, :] for block in range(NR)
        ]
        out_ref[place] = jnp.concatenate(rows, 0).astype(bf16)


def weight_partials(own, other, keep, given, pieces, scale):
    spec = pl.BlockSpec(memory_space=pltpu.VMEM)
    return pl.pallas_call(
        weight_kernel,
        out_shape=(
            jax.ShapeDtypeStruct((NX * NY, NR * SLICE, COLS), bf16),
            jax.ShapeDtypeStruct((NC, TOK, 1), f32),
        ),
        in_specs=[spec] * 6,
        out_specs=(spec, spec),
        scratch_shapes=[pltpu.VMEM((NR, HALF, COLS), f32)],
        compiler_params=pltpu.CompilerParams(vmem_limit_bytes=48 * 1024 * 1024),
        cost_estimate=pl.CostEstimate(
            flops=4 * TOK * HALF * D, bytes_accessed=8 * 1024 * 1024, transcendentals=0
        ),
        name="weight_partials",
    )(own, other, keep, given, pieces, scale)


def attn_kernel(
    shift_ref, own_ref, other_ref, pieces_ref, w_ref, coef_ref, first_ref, keep_ref, give_ref
):
    shift = shift_ref[0]
    for pair, (state_ref, out_ref) in enumerate(((own_ref, keep_ref), (other_ref, give_ref))):
        tokens = jnp.zeros((TOK, HALF), f32)
        rows = jnp.zeros((PIECES, HALF), f32)
        for block in range(NX):
            which = lax.rem(shift + block, NR)
            tokens = tokens + dot_last(state_ref[which], w_ref[block])
            rows = rows + dot_last(pieces_ref[pair, which], w_ref[block])
        for side in range(2):
            row = rows[3 * side + 2 : 3 * side + 3] + rows[3 * side + 1 : 3 * side + 2]
            row = row + rows[3 * side : 3 * side + 1]
            here = slice(side * SEQ, (side + 1) * SEQ)
            out_ref[here, :] = (
                first_ref[pair, here, :] * row - coef_ref[pair, here, :] * tokens[here]
            ).astype(bf16)


def attn_grads(shift, own, other, pieces, w_all, coef, first):
    spec = pl.BlockSpec(memory_space=pltpu.VMEM)
    out = jax.ShapeDtypeStruct((TOK, HALF), bf16)
    return pl.pallas_call(
        attn_kernel,
        out_shape=(out, out),
        in_specs=[pl.BlockSpec(memory_space=pltpu.SMEM)] + [spec] * 6,
        out_specs=(spec, spec),
        compiler_params=pltpu.CompilerParams(vmem_limit_bytes=48 * 1024 * 1024),
        cost_estimate=pl.CostEstimate(
            flops=4 * TOK * HALF * D, bytes_accessed=8 * 1024 * 1024, transcendentals=0
        ),
        name="attn_grads",
    )(shift, own, other, pieces, w_all, coef, first)


def body(hidden_state, attn_out, o_weight, norm_gain, lengths, positive):
    highest = lax.Precision.HIGHEST
    ix, iy, ic = lax.axis_index("x"), lax.axis_index("y"), lax.axis_index("c")
    it, ir = lax.axis_index("t"), lax.axis_index("r")
    dp_index = (ix * NY + iy) * NC + ic

    state = hidden_state.reshape(TOK, FEAT)
    attn = attn_out.reshape(TOK, FEAT)
    state_all = lax.all_to_all(jnp.broadcast_to(state[None], (NT, TOK, FEAT)), "t", 0, 0)
    w_start = (ic * NY + iy) * W_ROWS
    w_mine = lax.dynamic_slice(o_weight, (w_start, 0), (W_ROWS, COLS))
    w_moved = lax.ppermute(
        w_mine,
        ("x", "r"),
        [(i * NR + (j + i) % NR, i * NR + j) for i in range(NX) for j in range(NR)],
    )
    w_all = lax.all_gather(w_moved, PLANE).reshape(NX, HALF, COLS)
    attn_keep = jnp.where(ic == 0, attn[:, :HALF], attn[:, HALF:])
    attn_give = jnp.where(ic == 0, attn[:, HALF:], attn[:, :HALF])
    attn_other = swap_core(attn_give)

    states = state.astype(f32).reshape(2, SEQ, FEAT)
    square = lax.psum(jnp.sum(states * states, -1), "t") / D
    inv_rms = lax.rsqrt(square + epsilon)
    token_count = lengths.reshape(2).astype(f32)
    valid = (jnp.arange(SEQ, dtype=jnp.int32)[None, :] < lengths.reshape(2)[:, None]).astype(f32)
    pool_weight = valid * inv_rms / token_count[:, None]
    pooled = jnp.sum(pool_weight[..., None] * states, 1)
    attn_pool = jnp.sum(pool_weight[..., None] * attn.astype(f32).reshape(2, SEQ, FEAT), 1)

    near = jnp.concatenate([pooled, norm_gain[None]], 0)
    near = lax.all_to_all(jnp.broadcast_to(near[None], (NT, 3, FEAT)), "t", 0, 0)
    pooled_row = near[:, :2].transpose(1, 0, 2).reshape(2, D)
    gain = near[:, 2].reshape(D)

    u_parts = attn_pool.reshape(2, NC, NX * NY, SLICE).transpose(2, 1, 0, 3)
    u_parts = u_parts.reshape(NX * NY * NC, 2, SLICE)
    extra = jnp.stack(
        [token_count, jnp.broadcast_to(positive.astype(f32), (2,))], -1
    )
    row = jnp.concatenate([pooled_row, inv_rms], -1)
    group = NX * NY * NC
    send = jnp.concatenate(
        [
            jnp.broadcast_to(row[None], (group, 2, D + SEQ)),
            u_parts,
            jnp.broadcast_to(extra[None], (group, 2, 2)),
            jnp.zeros((group, 2, WIDTH - AT_POS - 1), f32),
        ],
        -1,
    )
    got = lax.all_to_all(send, DP, 0, 0)

    raw = got[..., :D]
    embeds = raw * gain
    inv_norm = lax.rsqrt(jnp.sum(embeds * embeds, -1, keepdims=True) + epsilon)
    unit = embeds * inv_norm
    query, passage = unit[:, 0], unit[:, 1]
    target = got[:, 0, AT_POS].astype(jnp.int32)
    logits = logit_scale * lax.dot_general(query, passage, contract_last, precision=highest)
    log_total = jnp.log(jnp.sum(jnp.exp(logits), -1))
    one_hot = (jnp.arange(group, dtype=jnp.int32)[None, :] == target[:, None]).astype(f32)
    loss_part = jnp.sum(log_total - jnp.sum(logits * one_hot, -1))
    score_grad = grad_scale * (jnp.exp(logits - log_total[:, None]) - one_hot)
    query_grad = logit_scale * jnp.dot(score_grad, passage, precision=highest)
    passage_grad = logit_scale * lax.dot_general(
        score_grad, query, contract_first, precision=highest
    )
    embed_grad = jnp.stack([query_grad, passage_grad], 1)
    along = jnp.sum(unit * embed_grad, -1, keepdims=True)
    pooled_grad = (embed_grad - unit * along) * inv_norm
    gain_part = jnp.sum(pooled_grad * raw, (0, 1))
    scaled = pooled_grad * gain
    gain_mine = lax.dynamic_slice(gain_part, (it * FEAT,), (FEAT,))

    other_index = dp_index + 1 - 2 * ic
    state_other = swap_core(state_all)
    rows = jnp.stack([scaled[dp_index], scaled[other_index]])
    counts = jnp.stack([got[dp_index, :, AT_LEN], got[other_index, :, AT_LEN]])
    rms = jnp.stack([got[dp_index, :, AT_RMS:AT_U], got[other_index, :, AT_RMS:AT_U]])
    place = jnp.arange(SEQ, dtype=jnp.int32).astype(f32)
    first_coef = jnp.where(place < counts[..., None], rms / counts[..., None], 0.0)
    scale = (first_coef * rms * rms / D).reshape(NC, TOK, 1)
    first_col = first_coef.reshape(NC, TOK, 1)
    pieces = jnp.stack(split3(rows), 2).reshape(NC, 6, NT, FEAT).transpose(0, 2, 1, 3)
    pieces = jnp.pad(pieces, ((0, 0), (0, 0), (0, PIECES - 6), (0, 0)))

    partial, coef = weight_partials(
        state_all, state_other, attn_keep, attn_other, pieces, scale
    )
    spread = lax.all_to_all(partial, PLANE, 0, 0)
    second = jnp.sum(spread.astype(f32), 0).reshape(NR, SLICE, COLS)

    u_all = got[..., AT_U:AT_LEN].reshape(2 * group, SLICE)
    first = lax.dot_general(
        u_all, scaled.reshape(2 * group, D), contract_first, precision=highest
    )
    first = first.reshape(SLICE, NR, COLS).transpose(1, 0, 2)
    tail = jnp.stack([gain_mine, jnp.broadcast_to(loss_part, (FEAT,))])
    tails = [tail]
    first_sum = lax.dynamic_index_in_dim(first, ir, 0, keepdims=False)
    for step in range(1, NR):
        outgoing = lax.dynamic_index_in_dim(first, (ir + step) % NR, 0, keepdims=False)
        arrived = lax.ppermute(
            jnp.concatenate([outgoing, tail], 0),
            "r",
            [(j, (j + step) % NR) for j in range(NR)],
        )
        first_sum = first_sum + arrived[:SLICE]
        tails.append(arrived[SLICE:])
    tails = jnp.stack(tails)
    totals = jnp.zeros((2, FEAT), f32)
    for source in range(NR):
        totals = totals + lax.dynamic_index_in_dim(
            tails, (ir - source) % NR, 0, keepdims=False
        )

    second_sum = lax.dynamic_index_in_dim(second, ir, 0, keepdims=False)
    second_cut = second.astype(bf16)
    for step in range(1, NR):
        outgoing = lax.dynamic_index_in_dim(second_cut, (ir + step) % NR, 0, keepdims=False)
        second_sum = second_sum + lax.ppermute(
            outgoing, "r", [(j, (j + step) % NR) for j in range(NR)]
        ).astype(f32)
    total = first_sum - second_sum
    done = jnp.broadcast_to(total.astype(bf16)[None], (NX * NY, SLICE, COLS))
    half = lax.all_to_all(done, PLANE, 0, 0).reshape(HALF, COLS)
    half_other = swap_core(half)
    grad_weight = jnp.where(
        ic == 0,
        jnp.concatenate([half, half_other], 0),
        jnp.concatenate([half_other, half], 0),
    )

    row_here = lax.dynamic_index_in_dim(
        rows[0].reshape(2, NT, FEAT), it, 1, keepdims=False
    )
    state_grad = first_coef[0][..., None] * row_here[:, None, :] - states * coef[0].reshape(
        2, SEQ, 1
    )
    grad_hidden = state_grad.astype(bf16).reshape(1, 2, SEQ, FEAT)

    keep, give = attn_grads(
        ir.reshape(1), state_all, state_other, pieces, w_all, coef, first_col
    )
    arrived = swap_core(give)
    grad_attn = jnp.where(
        ic == 0, jnp.concatenate([keep, arrived], 1), jnp.concatenate([arrived, keep], 1)
    ).reshape(1, 2, SEQ, FEAT)
    return (grad_hidden, grad_attn, grad_weight, totals[0], totals[1, 0])


def solution(mesh):
    fine = Mesh(mesh.devices.reshape(NX, NY, NC, NT, NR), ("x", "y", "c", "t", "r"))
    pairs = ("x", "y", "c", "r")
    placed = (
        P(pairs, None, None, "t"),
        P(pairs, None, None, "t"),
        P("t", "r"),
        P("t"),
        P(pairs, None),
        P(pairs),
    )
    return jax.shard_map(
        body,
        mesh=fine,
        in_specs=placed,
        out_specs=(
            P(pairs, None, None, "t"),
            P(pairs, None, None, "t"),
            P("t", "r"),
            P("t"),
            P(),
        ),
        check_vma=False,
    )
```

```python
import jax
import jax.numpy as jnp
from jax import lax
from jax.experimental import pallas as pl
from jax.experimental.pallas import tpu as pltpu
from jax.sharding import Mesh, PartitionSpec as P

logit_scale = 20.0
grad_scale = 256.0
epsilon = 1e-06

f32 = jnp.float32
bf16 = jnp.bfloat16

NX, NY, NC, NT, NR = 4, 4, 2, 4, 4
PLANE = ("x", "y")
DP = ("x", "y", "c")

D = 3584
FEAT = D // NT
COLS = D // NR
SEQ = 128
TOK = 2 * SEQ
HALF = FEAT // NC
SLICE = HALF // (NX * NY)
W_ROWS = HALF // NY
PIECES = 16
GROUP = NX * NY * NC

AT_RMS = D
AT_U = D + SEQ
AT_LEN = AT_U + SLICE
AT_POS = AT_LEN + 1
WIDTH = D + 2 * SEQ


def swap_core(value):
    return lax.ppermute(value, "c", [(0, 1), (1, 0)])


contract_last = (((1,), (1,)), ((), ()))
contract_first = (((0,), (0,)), ((), ()))


def dot_last(left, right):
    return lax.dot_general(left, right, contract_last, preferred_element_type=f32)


def dot_exact(left, right, dims):
    return lax.dot_general(
        left, right, dims, precision=lax.Precision.HIGHEST, preferred_element_type=f32
    )


def group_kernel(
    index_ref, got_ref, gain_ref,
    scaled_ref, first_ref, gain_out_ref, loss_ref, pieces_ref, scale_ref, column_ref,
):
    gain = gain_ref[...]
    raw, unit, inv_norm = [], [], []
    for side in range(2):
        raw.append(got_ref[side, :, :D])
        embeds = raw[side] * gain
        square = jnp.sum(embeds * embeds, -1, keepdims=True)
        inv_norm.append(lax.rsqrt(square + epsilon))
        unit.append(embeds * inv_norm[side])
    logits = logit_scale * dot_exact(unit[0], unit[1], contract_last)
    log_total = jnp.log(jnp.sum(jnp.exp(logits), -1, keepdims=True))
    target = got_ref[0, :, AT_POS : AT_POS + 1]
    passage = lax.broadcasted_iota(jnp.int32, (GROUP, GROUP), 1).astype(f32)
    one_hot = jnp.where(passage == target, 1.0, 0.0)
    chosen = jnp.sum(logits * one_hot, -1, keepdims=True)
    loss = jnp.sum(log_total - chosen, 0, keepdims=True)
    loss_ref[...] = jnp.broadcast_to(loss, (8, 128))
    score_grad = grad_scale * (jnp.exp(logits - log_total) - one_hot)
    grads = (
        dot_exact(score_grad, unit[1], (((1,), (0,)), ((), ()))),
        dot_exact(score_grad, unit[0], contract_first),
    )
    gain_sum = jnp.zeros((1, D), f32)
    first = jnp.zeros((SLICE, D), f32)
    for side in range(2):
        grad = logit_scale * grads[side]
        along = jnp.sum(unit[side] * grad, -1, keepdims=True)
        pooled_grad = (grad - unit[side] * along) * inv_norm[side]
        gain_sum = gain_sum + jnp.sum(pooled_grad * raw[side], 0, keepdims=True)
        scaled = pooled_grad * gain
        scaled_ref[side] = scaled
        first = first + dot_exact(got_ref[side, :, AT_U:AT_LEN], scaled, contract_first)
    for block in range(NR):
        columns = slice(block * COLS, (block + 1) * COLS)
        first_ref[block] = first[:, columns]
        gain_out_ref[block] = gain_sum[:, columns]

    token = lax.broadcasted_iota(jnp.int32, (SEQ, SEQ), 0)
    lane = lax.broadcasted_iota(jnp.int32, (SEQ, SEQ), 1)
    position = lax.broadcasted_iota(jnp.int32, (SEQ, 1), 0).astype(f32)
    for pair in range(NC):
        index = index_ref[pair]
        chosen_row = lax.broadcasted_iota(jnp.int32, (GROUP, 1), 0) == index
        parts = []
        for side in range(2):
            row = jnp.sum(jnp.where(chosen_row, scaled_ref[side], 0.0), 0, keepdims=True)
            high = row.astype(bf16).astype(f32)
            mid = (row - high).astype(bf16).astype(f32)
            parts += [high, mid, row - high - mid]
            rest = jnp.where(chosen_row, got_ref[side, :, AT_RMS:WIDTH], 0.0)
            rest = jnp.sum(rest, 0, keepdims=True)
            rms_row = rest[:, :SEQ]
            count = rest[:, AT_LEN - AT_RMS : AT_LEN - AT_RMS + 1]
            rms = jnp.sum(jnp.where(token == lane, rms_row, 0.0), -1, keepdims=True)
            column = jnp.where(position < count, rms / count, 0.0)
            here = slice(side * SEQ, (side + 1) * SEQ)
            column_ref[pair, here, :] = column
            scale_ref[pair, here, :] = column * rms * rms * (1.0 / D)
        parts.append(jnp.zeros((PIECES - 6, D), f32))
        piece = jnp.concatenate(parts, 0).astype(bf16)
        for block in range(NR):
            pieces_ref[pair, block] = piece[:, block * COLS : (block + 1) * COLS]


def group_math(index, got, gain):
    spec = pl.BlockSpec(memory_space=pltpu.VMEM)
    return pl.pallas_call(
        group_kernel,
        out_shape=(
            jax.ShapeDtypeStruct((2, GROUP, D), f32),
            jax.ShapeDtypeStruct((NR, SLICE, COLS), f32),
            jax.ShapeDtypeStruct((NR, 1, COLS), f32),
            jax.ShapeDtypeStruct((8, 128), f32),
            jax.ShapeDtypeStruct((NC, NR, PIECES, COLS), bf16),
            jax.ShapeDtypeStruct((NC, TOK, 1), f32),
            jax.ShapeDtypeStruct((NC, TOK, 1), f32),
        ),
        in_specs=[pl.BlockSpec(memory_space=pltpu.SMEM), spec, spec],
        out_specs=(spec,) * 7,
        compiler_params=pltpu.CompilerParams(vmem_limit_bytes=32 * 1024 * 1024),
        cost_estimate=pl.CostEstimate(
            flops=50 * GROUP * GROUP * D, bytes_accessed=3 * 1024 * 1024, transcendentals=4096
        ),
        name="group_math",
    )(index, got, gain)


def weight_kernel(
    own_ref, other_ref, keep_ref, given_ref, pieces_ref, scale_ref, out_ref, coef_ref, acc_ref
):
    token = lax.broadcasted_iota(jnp.int32, (TOK, PIECES), 0)
    part = lax.broadcasted_iota(jnp.int32, (TOK, PIECES), 1)
    part = part - jnp.where(token < SEQ, 0, 3)
    mask = (part >= 0) & (part < 3)
    scaled = []
    for pair, (state_ref, attn_ref) in enumerate(
        ((own_ref, keep_ref), (other_ref, given_ref))
    ):
        inner = jnp.zeros((TOK, PIECES), f32)
        for block in range(NT):
            inner = inner + dot_last(state_ref[block], pieces_ref[pair, block])
        inner = jnp.sum(jnp.where(mask, inner, 0.0), -1, keepdims=True)
        coef = scale_ref[pair] * inner
        coef_ref[pair] = coef
        scaled.append((attn_ref[...].astype(f32) * coef).astype(bf16))
    for block in range(NT):
        acc_ref[block] = lax.dot_general(
            scaled[0], own_ref[block], contract_first, preferred_element_type=f32
        ) + lax.dot_general(
            scaled[1], other_ref[block], contract_first, preferred_element_type=f32
        )
    for place in range(NX * NY):
        rows = [
            acc_ref[block, place * SLICE : (place + 1) * SLICE, :] for block in range(NR)
        ]
        out_ref[place] = jnp.concatenate(rows, 0).astype(bf16)


def weight_partials(own, other, keep, given, pieces, scale):
    spec = pl.BlockSpec(memory_space=pltpu.VMEM)
    return pl.pallas_call(
        weight_kernel,
        out_shape=(
            jax.ShapeDtypeStruct((NX * NY, NR * SLICE, COLS), bf16),
            jax.ShapeDtypeStruct((NC, TOK, 1), f32),
        ),
        in_specs=[spec] * 6,
        out_specs=(spec, spec),
        scratch_shapes=[pltpu.VMEM((NR, HALF, COLS), f32)],
        compiler_params=pltpu.CompilerParams(vmem_limit_bytes=48 * 1024 * 1024),
        cost_estimate=pl.CostEstimate(
            flops=4 * TOK * HALF * D, bytes_accessed=8 * 1024 * 1024, transcendentals=0
        ),
        name="weight_partials",
    )(own, other, keep, given, pieces, scale)


def attn_kernel(
    shift_ref, own_ref, other_ref, pieces_ref, w_ref, coef_ref, first_ref, keep_ref, give_ref
):
    shift = shift_ref[0]
    for pair, (state_ref, out_ref) in enumerate(((own_ref, keep_ref), (other_ref, give_ref))):
        tokens = jnp.zeros((TOK, HALF), f32)
        rows = jnp.zeros((PIECES, HALF), f32)
        for block in range(NX):
            which = lax.rem(shift + block, NR)
            tokens = tokens + dot_last(state_ref[which], w_ref[block])
            rows = rows + dot_last(pieces_ref[pair, which], w_ref[block])
        for side in range(2):
            row = rows[3 * side + 2 : 3 * side + 3] + rows[3 * side + 1 : 3 * side + 2]
            row = row + rows[3 * side : 3 * side + 1]
            here = slice(side * SEQ, (side + 1) * SEQ)
            out_ref[here, :] = (
                first_ref[pair, here, :] * row - coef_ref[pair, here, :] * tokens[here]
            ).astype(bf16)


def attn_grads(shift, own, other, pieces, w_all, coef, first):
    spec = pl.BlockSpec(memory_space=pltpu.VMEM)
    out = jax.ShapeDtypeStruct((TOK, HALF), bf16)
    return pl.pallas_call(
        attn_kernel,
        out_shape=(out, out),
        in_specs=[pl.BlockSpec(memory_space=pltpu.SMEM)] + [spec] * 6,
        out_specs=(spec, spec),
        compiler_params=pltpu.CompilerParams(vmem_limit_bytes=48 * 1024 * 1024),
        cost_estimate=pl.CostEstimate(
            flops=4 * TOK * HALF * D, bytes_accessed=8 * 1024 * 1024, transcendentals=0
        ),
        name="attn_grads",
    )(shift, own, other, pieces, w_all, coef, first)


def body(hidden_state, attn_out, o_weight, norm_gain, lengths, positive):
    ix, iy, ic = lax.axis_index("x"), lax.axis_index("y"), lax.axis_index("c")
    it, ir = lax.axis_index("t"), lax.axis_index("r")
    dp_index = (ix * NY + iy) * NC + ic

    state = hidden_state.reshape(TOK, FEAT)
    attn = attn_out.reshape(TOK, FEAT)
    state_all = lax.all_gather(state, "t")
    w_start = (ic * NY + iy) * W_ROWS
    w_mine = lax.dynamic_slice(o_weight, (w_start, 0), (W_ROWS, COLS))
    w_moved = lax.ppermute(
        w_mine,
        ("x", "r"),
        [(i * NR + (j + i) % NR, i * NR + j) for i in range(NX) for j in range(NR)],
    )
    attn_keep = jnp.where(ic == 0, attn[:, :HALF], attn[:, HALF:])
    attn_give = jnp.where(ic == 0, attn[:, HALF:], attn[:, :HALF])
    attn_other = swap_core(attn_give)

    states = state.astype(f32).reshape(2, SEQ, FEAT)
    square = lax.psum(jnp.sum(states * states, -1), "t") / D
    inv_rms = lax.rsqrt(square + epsilon)
    token_count = lengths.reshape(2).astype(f32)
    valid = (jnp.arange(SEQ, dtype=jnp.int32)[None, :] < lengths.reshape(2)[:, None]).astype(f32)
    pool_weight = valid * inv_rms / token_count[:, None]
    pooled = jnp.sum(pool_weight[..., None] * states, 1)
    attn_pool = jnp.sum(pool_weight[..., None] * attn.astype(f32).reshape(2, SEQ, FEAT), 1)

    near = jnp.concatenate([pooled, norm_gain[None]], 0)
    near = lax.all_to_all(jnp.broadcast_to(near[None], (NT, 3, FEAT)), "t", 0, 0)
    pooled_row = near[:, :2].transpose(1, 0, 2).reshape(2, D)
    gain = near[:, 2].reshape(1, D)

    u_parts = attn_pool.reshape(2, NC, NX * NY, SLICE).transpose(2, 1, 0, 3)
    u_parts = u_parts.reshape(GROUP, 2, SLICE)
    extra = jnp.stack(
        [token_count, jnp.broadcast_to(positive.astype(f32), (2,))], -1
    )
    row = jnp.concatenate([pooled_row, inv_rms], -1)
    send = jnp.concatenate(
        [
            jnp.broadcast_to(row[None], (GROUP, 2, D + SEQ)),
            u_parts,
            jnp.broadcast_to(extra[None], (GROUP, 2, 2)),
            jnp.zeros((GROUP, 2, WIDTH - AT_POS - 1), f32),
        ],
        -1,
    )
    got = lax.all_to_all(send, DP, 0, 0)
    got, state_all, w_moved = lax.optimization_barrier((got, state_all, w_moved))
    w_all = lax.all_gather(w_moved, PLANE).reshape(NX, HALF, COLS)

    other_index = dp_index + 1 - 2 * ic
    state_other = swap_core(state_all)
    scaled, first, gain_part, loss_part, pieces, scale, first_col = group_math(
        jnp.stack([dp_index, other_index]), got.transpose(1, 0, 2), gain
    )

    partial, coef = weight_partials(
        state_all, state_other, attn_keep, attn_other, pieces, scale
    )
    partial, first = lax.optimization_barrier((partial, first))
    spread = lax.all_to_all(partial, PLANE, 0, 0)

    gain_mine = lax.dynamic_index_in_dim(gain_part, it, 0, keepdims=False)
    tail = jnp.concatenate([gain_mine, jnp.broadcast_to(loss_part[:1, :1], (1, FEAT))], 0)
    tails = [tail]
    first_sum = lax.dynamic_index_in_dim(first, ir, 0, keepdims=False)
    for step in range(1, NR):
        outgoing = lax.dynamic_index_in_dim(first, (ir + step) % NR, 0, keepdims=False)
        arrived = lax.ppermute(
            jnp.concatenate([outgoing, tail], 0),
            "r",
            [(j, (j + step) % NR) for j in range(NR)],
        )
        first_sum = first_sum + arrived[:SLICE]
        tails.append(arrived[SLICE:])
    tails = jnp.stack(tails)
    totals = jnp.zeros((2, FEAT), f32)
    for source in range(NR):
        totals = totals + lax.dynamic_index_in_dim(
            tails, (ir - source) % NR, 0, keepdims=False
        )

    spread, first_sum, totals = lax.optimization_barrier((spread, first_sum, totals))
    second = jnp.sum(spread.astype(f32), 0).reshape(NR, SLICE, COLS)
    second_sum = jnp.sum(
        lax.all_to_all(second.astype(bf16), "r", 0, 0).astype(f32), 0
    )
    total = first_sum - second_sum
    done = jnp.broadcast_to(total.astype(bf16)[None], (NX * NY, SLICE, COLS))
    half = lax.all_to_all(done, PLANE, 0, 0).reshape(HALF, COLS)
    row_here = lax.dynamic_slice(scaled, (0, dp_index, it * FEAT), (2, 1, FEAT))
    state_grad = first_col[0].reshape(2, SEQ, 1) * row_here - states * coef[0].reshape(2, SEQ, 1)
    grad_hidden = state_grad.astype(bf16).reshape(1, 2, SEQ, FEAT)
    keep, give = attn_grads(
        ir.reshape(1), state_all, state_other, pieces, w_all, coef, first_col
    )
    half, keep, give = lax.optimization_barrier((half, keep, give))
    half_other = swap_core(half)
    grad_weight = jnp.where(
        ic == 0,
        jnp.concatenate([half, half_other], 0),
        jnp.concatenate([half_other, half], 0),
    )

    arrived = swap_core(give)
    grad_attn = jnp.where(
        ic == 0, jnp.concatenate([keep, arrived], 1), jnp.concatenate([arrived, keep], 1)
    ).reshape(1, 2, SEQ, FEAT)
    return (grad_hidden, grad_attn, grad_weight, totals[0], totals[1, 0])


def solution(mesh):
    fine = Mesh(mesh.devices.reshape(NX, NY, NC, NT, NR), ("x", "y", "c", "t", "r"))
    pairs = ("x", "y", "c", "r")
    placed = (
        P(pairs, None, None, "t"),
        P(pairs, None, None, "t"),
        P("t", "r"),
        P("t"),
        P(pairs, None),
        P(pairs),
    )
    return jax.shard_map(
        body,
        mesh=fine,
        in_specs=placed,
        out_specs=(
            P(pairs, None, None, "t"),
            P(pairs, None, None, "t"),
            P("t", "r"),
            P("t"),
            P(),
        ),
        check_vma=False,
    )
```

```python
import jax
import jax.numpy as jnp
from jax import lax
from jax.experimental import pallas as pl
from jax.experimental.pallas import tpu as pltpu
from jax.sharding import Mesh, PartitionSpec as P

logit_scale = 20.0
grad_scale = 256.0
epsilon = 1e-06

f32 = jnp.float32
bf16 = jnp.bfloat16

NX, NY, NC, NT, NR = 4, 4, 2, 4, 4
PLANE = ("x", "y")
DP = ("x", "y", "c")

D = 3584
FEAT = D // NT
COLS = D // NR
SEQ = 128
TOK = 2 * SEQ
HALF = FEAT // NC
SLICE = HALF // (NX * NY)
W_ROWS = HALF // NY
PIECES = 16
GROUP = NX * NY * NC

AT_RMS = D
AT_U = D + SEQ
AT_LEN = AT_U + SLICE
AT_POS = AT_LEN + 1
WIDTH = D + 2 * SEQ


def swap_core(value):
    return lax.ppermute(value, "c", [(0, 1), (1, 0)])


contract_last = (((1,), (1,)), ((), ()))
contract_first = (((0,), (0,)), ((), ()))


def dot_last(left, right):
    return lax.dot_general(left, right, contract_last, preferred_element_type=f32)


def dot_exact(left, right, dims):
    return lax.dot_general(
        left, right, dims, precision=lax.Precision.HIGHEST, preferred_element_type=f32
    )


def group_kernel(
    index_ref, got_ref, gain_ref,
    scaled_ref, first_ref, gain_out_ref, loss_ref, pieces_ref, scale_ref, column_ref,
):
    gain = gain_ref[...]
    raw, unit, inv_norm = [], [], []
    for side in range(2):
        raw.append(got_ref[side, :, :D])
        embeds = raw[side] * gain
        square = jnp.sum(embeds * embeds, -1, keepdims=True)
        inv_norm.append(lax.rsqrt(square + epsilon))
        unit.append(embeds * inv_norm[side])
    logits = logit_scale * dot_exact(unit[0], unit[1], contract_last)
    log_total = jnp.log(jnp.sum(jnp.exp(logits), -1, keepdims=True))
    target = got_ref[0, :, AT_POS : AT_POS + 1]
    passage = lax.broadcasted_iota(jnp.int32, (GROUP, GROUP), 1).astype(f32)
    one_hot = jnp.where(passage == target, 1.0, 0.0)
    chosen = jnp.sum(logits * one_hot, -1, keepdims=True)
    loss = jnp.sum(log_total - chosen, 0, keepdims=True)
    loss_ref[...] = jnp.broadcast_to(loss, (8, 128))
    score_grad = grad_scale * (jnp.exp(logits - log_total) - one_hot)
    grads = (
        dot_exact(score_grad, unit[1], (((1,), (0,)), ((), ()))),
        dot_exact(score_grad, unit[0], contract_first),
    )
    gain_sum = jnp.zeros((1, D), f32)
    first = jnp.zeros((SLICE, D), f32)
    for side in range(2):
        grad = logit_scale * grads[side]
        along = jnp.sum(unit[side] * grad, -1, keepdims=True)
        pooled_grad = (grad - unit[side] * along) * inv_norm[side]
        gain_sum = gain_sum + jnp.sum(pooled_grad * raw[side], 0, keepdims=True)
        scaled = pooled_grad * gain
        scaled_ref[side] = scaled
        first = first + dot_exact(got_ref[side, :, AT_U:AT_LEN], scaled, contract_first)
    for block in range(NR):
        columns = slice(block * COLS, (block + 1) * COLS)
        first_ref[block] = first[:, columns]
        gain_out_ref[block] = gain_sum[:, columns]

    token = lax.broadcasted_iota(jnp.int32, (SEQ, SEQ), 0)
    lane = lax.broadcasted_iota(jnp.int32, (SEQ, SEQ), 1)
    position = lax.broadcasted_iota(jnp.int32, (SEQ, 1), 0).astype(f32)
    for pair in range(NC):
        index = index_ref[pair]
        chosen_row = lax.broadcasted_iota(jnp.int32, (GROUP, 1), 0) == index
        parts = []
        for side in range(2):
            row = jnp.sum(jnp.where(chosen_row, scaled_ref[side], 0.0), 0, keepdims=True)
            high = row.astype(bf16).astype(f32)
            mid = (row - high).astype(bf16).astype(f32)
            parts += [high, mid, row - high - mid]
            rest = jnp.where(chosen_row, got_ref[side, :, AT_RMS:WIDTH], 0.0)
            rest = jnp.sum(rest, 0, keepdims=True)
            rms_row = rest[:, :SEQ]
            count = rest[:, AT_LEN - AT_RMS : AT_LEN - AT_RMS + 1]
            rms = jnp.sum(jnp.where(token == lane, rms_row, 0.0), -1, keepdims=True)
            column = jnp.where(position < count, rms / count, 0.0)
            here = slice(side * SEQ, (side + 1) * SEQ)
            column_ref[pair, here, :] = column
            scale_ref[pair, here, :] = column * rms * rms * (1.0 / D)
        parts.append(jnp.zeros((PIECES - 6, D), f32))
        piece = jnp.concatenate(parts, 0).astype(bf16)
        for block in range(NR):
            pieces_ref[pair, block] = piece[:, block * COLS : (block + 1) * COLS]


def group_math(index, got, gain):
    spec = pl.BlockSpec(memory_space=pltpu.VMEM)
    return pl.pallas_call(
        group_kernel,
        out_shape=(
            jax.ShapeDtypeStruct((2, GROUP, D), f32),
            jax.ShapeDtypeStruct((NR, SLICE, COLS), f32),
            jax.ShapeDtypeStruct((NR, 1, COLS), f32),
            jax.ShapeDtypeStruct((8, 128), f32),
            jax.ShapeDtypeStruct((NC, NR, PIECES, COLS), bf16),
            jax.ShapeDtypeStruct((NC, TOK, 1), f32),
            jax.ShapeDtypeStruct((NC, TOK, 1), f32),
        ),
        in_specs=[pl.BlockSpec(memory_space=pltpu.SMEM), spec, spec],
        out_specs=(spec,) * 7,
        compiler_params=pltpu.CompilerParams(vmem_limit_bytes=16 * 1024 * 1024),
        cost_estimate=pl.CostEstimate(
            flops=50 * GROUP * GROUP * D, bytes_accessed=3 * 1024 * 1024, transcendentals=4096
        ),
        name="group_math",
    )(index, got, gain)


def weight_kernel(
    own_ref, other_ref, keep_ref, given_ref, pieces_ref, scale_ref, out_ref, coef_ref, acc_ref
):
    token = lax.broadcasted_iota(jnp.int32, (TOK, PIECES), 0)
    part = lax.broadcasted_iota(jnp.int32, (TOK, PIECES), 1)
    part = part - jnp.where(token < SEQ, 0, 3)
    mask = (part >= 0) & (part < 3)
    scaled = []
    for pair, (state_ref, attn_ref) in enumerate(
        ((own_ref, keep_ref), (other_ref, given_ref))
    ):
        inner = jnp.zeros((TOK, PIECES), f32)
        for block in range(NT):
            inner = inner + dot_last(state_ref[block], pieces_ref[pair, block])
        inner = jnp.sum(jnp.where(mask, inner, 0.0), -1, keepdims=True)
        coef = scale_ref[pair] * inner
        coef_ref[pair] = coef
        scaled.append((attn_ref[...].astype(f32) * coef).astype(bf16))
    for block in range(NT):
        acc_ref[block] = lax.dot_general(
            scaled[0], own_ref[block], contract_first, preferred_element_type=f32
        ) + lax.dot_general(
            scaled[1], other_ref[block], contract_first, preferred_element_type=f32
        )
    for place in range(NX * NY):
        rows = [
            acc_ref[block, place * SLICE : (place + 1) * SLICE, :] for block in range(NR)
        ]
        out_ref[place] = jnp.concatenate(rows, 0).astype(bf16)


def weight_partials(own, other, keep, given, pieces, scale):
    spec = pl.BlockSpec(memory_space=pltpu.VMEM)
    return pl.pallas_call(
        weight_kernel,
        out_shape=(
            jax.ShapeDtypeStruct((NX * NY, NR * SLICE, COLS), bf16),
            jax.ShapeDtypeStruct((NC, TOK, 1), f32),
        ),
        in_specs=[spec] * 6,
        out_specs=(spec, spec),
        scratch_shapes=[pltpu.VMEM((NR, HALF, COLS), f32)],
        compiler_params=pltpu.CompilerParams(vmem_limit_bytes=24 * 1024 * 1024),
        cost_estimate=pl.CostEstimate(
            flops=4 * TOK * HALF * D, bytes_accessed=8 * 1024 * 1024, transcendentals=0
        ),
        name="weight_partials",
    )(own, other, keep, given, pieces, scale)


def attn_kernel(
    shift_ref, own_ref, other_ref, pieces_ref, w_ref, coef_ref, first_ref, keep_ref, give_ref
):
    shift = shift_ref[0]
    for pair, (state_ref, out_ref) in enumerate(((own_ref, keep_ref), (other_ref, give_ref))):
        tokens = jnp.zeros((TOK, HALF), f32)
        rows = jnp.zeros((PIECES, HALF), f32)
        for block in range(NX):
            which = lax.rem(shift + block, NR)
            tokens = tokens + dot_last(state_ref[which], w_ref[block])
            rows = rows + dot_last(pieces_ref[pair, which], w_ref[block])
        for side in range(2):
            row = rows[3 * side + 2 : 3 * side + 3] + rows[3 * side + 1 : 3 * side + 2]
            row = row + rows[3 * side : 3 * side + 1]
            here = slice(side * SEQ, (side + 1) * SEQ)
            out_ref[here, :] = (
                first_ref[pair, here, :] * row - coef_ref[pair, here, :] * tokens[here]
            ).astype(bf16)


def attn_grads(shift, own, other, pieces, w_all, coef, first):
    spec = pl.BlockSpec(memory_space=pltpu.VMEM)
    out = jax.ShapeDtypeStruct((TOK, HALF), bf16)
    return pl.pallas_call(
        attn_kernel,
        out_shape=(out, out),
        in_specs=[pl.BlockSpec(memory_space=pltpu.SMEM)] + [spec] * 6,
        out_specs=(spec, spec),
        compiler_params=pltpu.CompilerParams(vmem_limit_bytes=24 * 1024 * 1024),
        cost_estimate=pl.CostEstimate(
            flops=4 * TOK * HALF * D, bytes_accessed=8 * 1024 * 1024, transcendentals=0
        ),
        name="attn_grads",
    )(shift, own, other, pieces, w_all, coef, first)


def body(hidden_state, attn_out, o_weight, norm_gain, lengths, positive):
    ix, iy, ic = lax.axis_index("x"), lax.axis_index("y"), lax.axis_index("c")
    it, ir = lax.axis_index("t"), lax.axis_index("r")
    dp_index = (ix * NY + iy) * NC + ic

    state = hidden_state.reshape(TOK, FEAT)
    attn = attn_out.reshape(TOK, FEAT)
    state_all = lax.all_gather(state, "t")
    w_start = (ic * NY + iy) * W_ROWS
    w_mine = lax.dynamic_slice(o_weight, (w_start, 0), (W_ROWS, COLS))
    w_moved = lax.ppermute(
        w_mine,
        ("x", "r"),
        [(i * NR + (j + i) % NR, i * NR + j) for i in range(NX) for j in range(NR)],
    )
    attn_keep = jnp.where(ic == 0, attn[:, :HALF], attn[:, HALF:])
    attn_give = jnp.where(ic == 0, attn[:, HALF:], attn[:, :HALF])
    attn_other = swap_core(attn_give)

    states = state.astype(f32).reshape(2, SEQ, FEAT)
    square = lax.psum(jnp.sum(states * states, -1), "t") / D
    inv_rms = lax.rsqrt(square + epsilon)
    token_count = lengths.reshape(2).astype(f32)
    valid = (jnp.arange(SEQ, dtype=jnp.int32)[None, :] < lengths.reshape(2)[:, None]).astype(f32)
    pool_weight = valid * inv_rms / token_count[:, None]
    pooled = jnp.sum(pool_weight[..., None] * states, 1)
    attn_pool = jnp.sum(pool_weight[..., None] * attn.astype(f32).reshape(2, SEQ, FEAT), 1)

    near = jnp.concatenate([pooled, norm_gain[None]], 0)
    near, w_moved = lax.optimization_barrier((near, w_moved))
    near = lax.all_to_all(jnp.broadcast_to(near[None], (NT, 3, FEAT)), "t", 0, 0)
    pooled_row = near[:, :2].transpose(1, 0, 2).reshape(2, D)
    gain = near[:, 2].reshape(1, D)

    u_parts = attn_pool.reshape(2, NC, NX * NY, SLICE).transpose(2, 1, 0, 3)
    u_parts = u_parts.reshape(GROUP, 2, SLICE)
    extra = jnp.stack(
        [token_count, jnp.broadcast_to(positive.astype(f32), (2,))], -1
    )
    row = jnp.concatenate([pooled_row, inv_rms], -1)
    send = jnp.concatenate(
        [
            jnp.broadcast_to(row[None], (GROUP, 2, D + SEQ)),
            u_parts,
            jnp.broadcast_to(extra[None], (GROUP, 2, 2)),
            jnp.zeros((GROUP, 2, WIDTH - AT_POS - 1), f32),
        ],
        -1,
    )
    got = lax.all_to_all(send, DP, 0, 0)
    got, state_all, w_moved, attn_other = lax.optimization_barrier(
        (got, state_all, w_moved, attn_other)
    )
    w_all = lax.all_gather(w_moved, PLANE).reshape(NX, HALF, COLS)

    other_index = dp_index + 1 - 2 * ic
    state_other = swap_core(state_all)
    scaled, first, gain_part, loss_part, pieces, scale, first_col = group_math(
        jnp.stack([dp_index, other_index]), got.transpose(1, 0, 2), gain
    )

    partial, coef = weight_partials(
        state_all, state_other, attn_keep, attn_other, pieces, scale
    )
    partial, first = lax.optimization_barrier((partial, first))
    spread = lax.all_to_all(partial, PLANE, 0, 0)

    gain_mine = lax.dynamic_index_in_dim(gain_part, it, 0, keepdims=False)
    tail = jnp.concatenate([gain_mine, jnp.broadcast_to(loss_part[:1, :1], (1, FEAT))], 0)
    tails = [tail]
    first_sum = lax.dynamic_index_in_dim(first, ir, 0, keepdims=False)
    for step in range(1, NR):
        outgoing = lax.dynamic_index_in_dim(first, (ir + step) % NR, 0, keepdims=False)
        arrived = lax.ppermute(
            jnp.concatenate([outgoing, tail], 0),
            "r",
            [(j, (j + step) % NR) for j in range(NR)],
        )
        first_sum = first_sum + arrived[:SLICE]
        tails.append(arrived[SLICE:])
    tails = jnp.stack(tails)
    totals = jnp.zeros((2, FEAT), f32)
    for source in range(NR):
        totals = totals + lax.dynamic_index_in_dim(
            tails, (ir - source) % NR, 0, keepdims=False
        )

    spread, first_sum, totals = lax.optimization_barrier((spread, first_sum, totals))
    second = jnp.sum(spread.astype(f32), 0).reshape(NR, SLICE, COLS)
    second = lax.all_to_all(second.astype(bf16), "r", 0, 0)

    row_here = lax.dynamic_slice(scaled, (0, dp_index, it * FEAT), (2, 1, FEAT))
    state_grad = first_col[0].reshape(2, SEQ, 1) * row_here - states * coef[0].reshape(2, SEQ, 1)
    grad_hidden = state_grad.astype(bf16).reshape(1, 2, SEQ, FEAT)
    keep, give = attn_grads(
        ir.reshape(1), state_all, state_other, pieces, w_all, coef, first_col
    )

    second, keep, give = lax.optimization_barrier((second, keep, give))
    second_sum = jnp.sum(second.astype(f32), 0)
    total = first_sum - second_sum
    done = jnp.broadcast_to(total.astype(bf16)[None], (NX * NY, SLICE, COLS))
    half = lax.all_to_all(done, PLANE, 0, 0).reshape(HALF, COLS)
    arrived = swap_core(give)
    grad_attn = jnp.where(
        ic == 0, jnp.concatenate([keep, arrived], 1), jnp.concatenate([arrived, keep], 1)
    ).reshape(1, 2, SEQ, FEAT)
    half, grad_attn, grad_hidden, totals = lax.optimization_barrier(
        (half, grad_attn, grad_hidden, totals)
    )
    half_other = swap_core(half)
    grad_weight = jnp.where(
        ic == 0,
        jnp.concatenate([half, half_other], 0),
        jnp.concatenate([half_other, half], 0),
    )

    return (grad_hidden, grad_attn, grad_weight, totals[0], totals[1, 0])


def solution(mesh):
    fine = Mesh(mesh.devices.reshape(NX, NY, NC, NT, NR), ("x", "y", "c", "t", "r"))
    pairs = ("x", "y", "c", "r")
    placed = (
        P(pairs, None, None, "t"),
        P(pairs, None, None, "t"),
        P("t", "r"),
        P("t"),
        P(pairs, None),
        P(pairs),
    )
    return jax.shard_map(
        body,
        mesh=fine,
        in_specs=placed,
        out_specs=(
            P(pairs, None, None, "t"),
            P(pairs, None, None, "t"),
            P("t", "r"),
            P("t"),
            P(),
        ),
        check_vma=False,
    )
```

```python
import jax
import jax.numpy as jnp
from jax import lax
from jax.experimental import pallas as pl
from jax.experimental.pallas import tpu as pltpu
from jax.sharding import Mesh, PartitionSpec as P

logit_scale = 20.0
grad_scale = 256.0
epsilon = 1e-06

f32 = jnp.float32
bf16 = jnp.bfloat16

NX, NY, NC, NT, NR = 4, 4, 2, 4, 4
PLANE = ("x", "y")
DP = ("x", "y", "c")

D = 3584
FEAT = D // NT
COLS = D // NR
SEQ = 128
TOK = 2 * SEQ
HALF = FEAT // NC
SLICE = HALF // (NX * NY)
W_ROWS = HALF // NY
PIECES = 16
GROUP = NX * NY * NC

LANES = 1024
ROWS = 8
LAST = D - 3 * LANES
AT_RMS = LAST
AT_U = AT_RMS + SEQ
AT_LEN = AT_U + SLICE
AT_POS = AT_LEN + 1


def swap_core(value):
    return lax.ppermute(value, "c", [(0, 1), (1, 0)])


contract_last = (((1,), (1,)), ((), ()))
contract_first = (((0,), (0,)), ((), ()))


def dot_last(left, right):
    return lax.dot_general(left, right, contract_last, preferred_element_type=f32)


def dot_exact(left, right, dims):
    return lax.dot_general(
        left, right, dims, precision=lax.Precision.HIGHEST, preferred_element_type=f32
    )


def front_kernel(length_ref, target_ref, state_ref, attn_ref, send_ref, base_ref):
    square = jnp.zeros((TOK, FEAT), f32)
    for block in range(NT):
        part = state_ref[block].astype(f32)
        square = square + part * part
    square = jnp.sum(square, -1, keepdims=True)
    inv_rms = lax.rsqrt(square * (1.0 / D) + epsilon)
    token = lax.broadcasted_iota(jnp.int32, (SEQ, SEQ), 0)
    lane = lax.broadcasted_iota(jnp.int32, (SEQ, SEQ), 1)
    position = lax.broadcasted_iota(jnp.int32, (SEQ, 1), 0)
    pools = []
    for side in range(2):
        here = slice(side * SEQ, (side + 1) * SEQ)
        length = length_ref[side]
        count = jnp.full((1, 1), length, jnp.int32).astype(f32)
        rms = inv_rms[here]
        weight = jnp.where(position < length, rms, 0.0) / count
        pooled = [
            jnp.sum(weight * state_ref[block, here, :].astype(f32), 0, keepdims=True)
            for block in range(NT)
        ]
        rms_row = jnp.sum(jnp.where(token == lane, rms, 0.0), 0, keepdims=True)
        row = jnp.concatenate(
            pooled + [rms_row, jnp.zeros((1, LANES - AT_U), f32)], 1
        )
        for part in range(4):
            base_ref[4 * side + part : 4 * side + part + 1, :] = row[
                :, part * LANES : (part + 1) * LANES
            ]
        pools.append(
            jnp.sum(weight * attn_ref[here, :].astype(f32), 0, keepdims=True)
        )
    base = base_ref[...]
    fixed = base[:, AT_U : AT_U + 128]
    row_index = lax.broadcasted_iota(jnp.int32, (ROWS, 128), 0)
    lane_index = lax.broadcasted_iota(jnp.int32, (ROWS, 128), 1)
    both = jnp.concatenate([pools[0]] * 4 + [pools[1]] * 4, 0)
    first_side = row_index < 4
    count = jnp.where(first_side, length_ref[0], length_ref[1]).astype(f32)
    target = jnp.full((ROWS, 128), target_ref[0], jnp.int32).astype(f32)
    last_row = (row_index == 3) | (row_index == 7)
    for device in range(GROUP):
        at = (device % NC) * HALF + (device // NC) * SLICE
        moved = both if at == 0 else pltpu.roll(both, FEAT - at, 1)
        extra = jnp.where(lane_index < SLICE, moved[:, :128], 0.0)
        extra = jnp.where(lane_index == SLICE, count, extra)
        extra = jnp.where(lane_index == SLICE + 1, target, extra)
        send_ref[device] = base
        send_ref[device, :, AT_U : AT_U + 128] = jnp.where(last_row, extra, fixed)


def front(lengths, target, state_all, attn):
    spec = pl.BlockSpec(memory_space=pltpu.VMEM)
    scalars = pl.BlockSpec(memory_space=pltpu.SMEM)
    return pl.pallas_call(
        front_kernel,
        out_shape=jax.ShapeDtypeStruct((GROUP, ROWS, LANES), f32),
        in_specs=[scalars, scalars, spec, spec],
        out_specs=spec,
        scratch_shapes=[pltpu.VMEM((ROWS, LANES), f32)],
        compiler_params=pltpu.CompilerParams(vmem_limit_bytes=16 * 1024 * 1024),
        cost_estimate=pl.CostEstimate(
            flops=8 * TOK * D, bytes_accessed=4 * 1024 * 1024, transcendentals=TOK
        ),
        name="front",
    )(lengths, target, state_all, attn)


def group_kernel(
    index_ref, got_ref, gain_ref,
    scaled_ref, first_ref, gain_out_ref, loss_ref, pieces_ref, scale_ref, column_ref,
):
    gain = gain_ref[...]
    raw, unit, inv_norm = [], [], []
    for side in range(2):
        parts = [got_ref[4 * side + part] for part in range(4)]
        raw.append(jnp.concatenate(parts, 1)[:, :D])
        embeds = raw[side] * gain
        square = jnp.sum(embeds * embeds, -1, keepdims=True)
        inv_norm.append(lax.rsqrt(square + epsilon))
        unit.append(embeds * inv_norm[side])
    logits = logit_scale * dot_exact(unit[0], unit[1], contract_last)
    log_total = jnp.log(jnp.sum(jnp.exp(logits), -1, keepdims=True))
    target = got_ref[3, :, AT_POS : AT_POS + 1]
    passage = lax.broadcasted_iota(jnp.int32, (GROUP, GROUP), 1).astype(f32)
    one_hot = jnp.where(passage == target, 1.0, 0.0)
    chosen = jnp.sum(logits * one_hot, -1, keepdims=True)
    loss = jnp.sum(log_total - chosen, 0, keepdims=True)
    loss_ref[...] = jnp.broadcast_to(loss, (8, 128))
    score_grad = grad_scale * (jnp.exp(logits - log_total) - one_hot)
    grads = (
        dot_exact(score_grad, unit[1], (((1,), (0,)), ((), ()))),
        dot_exact(score_grad, unit[0], contract_first),
    )
    gain_sum = jnp.zeros((1, D), f32)
    first = jnp.zeros((SLICE, D), f32)
    for side in range(2):
        grad = logit_scale * grads[side]
        along = jnp.sum(unit[side] * grad, -1, keepdims=True)
        pooled_grad = (grad - unit[side] * along) * inv_norm[side]
        gain_sum = gain_sum + jnp.sum(pooled_grad * raw[side], 0, keepdims=True)
        scaled = pooled_grad * gain
        scaled_ref[side] = scaled
        first = first + dot_exact(got_ref[4 * side + 3, :, AT_U:AT_LEN], scaled, contract_first)
    for block in range(NR):
        columns = slice(block * COLS, (block + 1) * COLS)
        first_ref[block] = first[:, columns]
        gain_out_ref[block] = gain_sum[:, columns]

    token = lax.broadcasted_iota(jnp.int32, (SEQ, SEQ), 0)
    lane = lax.broadcasted_iota(jnp.int32, (SEQ, SEQ), 1)
    position = lax.broadcasted_iota(jnp.int32, (SEQ, 1), 0).astype(f32)
    for pair in range(NC):
        index = index_ref[pair]
        chosen_row = lax.broadcasted_iota(jnp.int32, (GROUP, 1), 0) == index
        parts = []
        for side in range(2):
            row = jnp.sum(jnp.where(chosen_row, scaled_ref[side], 0.0), 0, keepdims=True)
            high = row.astype(bf16).astype(f32)
            mid = (row - high).astype(bf16).astype(f32)
            parts += [high, mid, row - high - mid]
            rest = jnp.where(chosen_row, got_ref[4 * side + 3, :, AT_RMS:], 0.0)
            rest = jnp.sum(rest, 0, keepdims=True)
            rms_row = rest[:, :SEQ]
            count = rest[:, AT_LEN - AT_RMS : AT_LEN - AT_RMS + 1]
            rms = jnp.sum(jnp.where(token == lane, rms_row, 0.0), -1, keepdims=True)
            column = jnp.where(position < count, rms / count, 0.0)
            here = slice(side * SEQ, (side + 1) * SEQ)
            column_ref[pair, here, :] = column
            scale_ref[pair, here, :] = column * rms * rms * (1.0 / D)
        parts.append(jnp.zeros((PIECES - 6, D), f32))
        piece = jnp.concatenate(parts, 0).astype(bf16)
        for block in range(NR):
            pieces_ref[pair, block] = piece[:, block * COLS : (block + 1) * COLS]


def group_math(index, got, gain):
    spec = pl.BlockSpec(memory_space=pltpu.VMEM)
    return pl.pallas_call(
        group_kernel,
        out_shape=(
            jax.ShapeDtypeStruct((2, GROUP, D), f32),
            jax.ShapeDtypeStruct((NR, SLICE, COLS), f32),
            jax.ShapeDtypeStruct((NR, 1, COLS), f32),
            jax.ShapeDtypeStruct((8, 128), f32),
            jax.ShapeDtypeStruct((NC, NR, PIECES, COLS), bf16),
            jax.ShapeDtypeStruct((NC, TOK, 1), f32),
            jax.ShapeDtypeStruct((NC, TOK, 1), f32),
        ),
        in_specs=[pl.BlockSpec(memory_space=pltpu.SMEM), spec, spec],
        out_specs=(spec,) * 7,
        compiler_params=pltpu.CompilerParams(vmem_limit_bytes=16 * 1024 * 1024),
        cost_estimate=pl.CostEstimate(
            flops=50 * GROUP * GROUP * D, bytes_accessed=3 * 1024 * 1024, transcendentals=4096
        ),
        name="group_math",
    )(index, got, gain)


def weight_kernel(
    own_ref, other_ref, keep_ref, given_ref, pieces_ref, scale_ref, out_ref, coef_ref, acc_ref
):
    token = lax.broadcasted_iota(jnp.int32, (TOK, PIECES), 0)
    part = lax.broadcasted_iota(jnp.int32, (TOK, PIECES), 1)
    part = part - jnp.where(token < SEQ, 0, 3)
    mask = (part >= 0) & (part < 3)
    scaled = []
    for pair, (state_ref, attn_ref) in enumerate(
        ((own_ref, keep_ref), (other_ref, given_ref))
    ):
        inner = jnp.zeros((TOK, PIECES), f32)
        for block in range(NT):
            inner = inner + dot_last(state_ref[block], pieces_ref[pair, block])
        inner = jnp.sum(jnp.where(mask, inner, 0.0), -1, keepdims=True)
        coef = scale_ref[pair] * inner
        coef_ref[pair] = coef
        scaled.append((attn_ref[...].astype(f32) * coef).astype(bf16))
    for block in range(NT):
        acc_ref[block] = lax.dot_general(
            scaled[0], own_ref[block], contract_first, preferred_element_type=f32
        ) + lax.dot_general(
            scaled[1], other_ref[block], contract_first, preferred_element_type=f32
        )
    for place in range(NX * NY):
        rows = [
            acc_ref[block, place * SLICE : (place + 1) * SLICE, :] for block in range(NR)
        ]
        out_ref[place] = jnp.concatenate(rows, 0).astype(bf16)


def weight_partials(own, other, keep, given, pieces, scale):
    spec = pl.BlockSpec(memory_space=pltpu.VMEM)
    return pl.pallas_call(
        weight_kernel,
        out_shape=(
            jax.ShapeDtypeStruct((NX * NY, NR * SLICE, COLS), bf16),
            jax.ShapeDtypeStruct((NC, TOK, 1), f32),
        ),
        in_specs=[spec] * 6,
        out_specs=(spec, spec),
        scratch_shapes=[pltpu.VMEM((NR, HALF, COLS), f32)],
        compiler_params=pltpu.CompilerParams(vmem_limit_bytes=24 * 1024 * 1024),
        cost_estimate=pl.CostEstimate(
            flops=4 * TOK * HALF * D, bytes_accessed=8 * 1024 * 1024, transcendentals=0
        ),
        name="weight_partials",
    )(own, other, keep, given, pieces, scale)


def attn_kernel(
    shift_ref, own_ref, other_ref, pieces_ref, w_ref, coef_ref, first_ref, keep_ref, give_ref
):
    shift = shift_ref[0]
    for pair, (state_ref, out_ref) in enumerate(((own_ref, keep_ref), (other_ref, give_ref))):
        tokens = jnp.zeros((TOK, HALF), f32)
        rows = jnp.zeros((PIECES, HALF), f32)
        for block in range(NX):
            which = lax.rem(shift + block, NR)
            tokens = tokens + dot_last(state_ref[which], w_ref[block])
            rows = rows + dot_last(pieces_ref[pair, which], w_ref[block])
        for side in range(2):
            row = rows[3 * side + 2 : 3 * side + 3] + rows[3 * side + 1 : 3 * side + 2]
            row = row + rows[3 * side : 3 * side + 1]
            here = slice(side * SEQ, (side + 1) * SEQ)
            out_ref[here, :] = (
                first_ref[pair, here, :] * row - coef_ref[pair, here, :] * tokens[here]
            ).astype(bf16)


def attn_grads(shift, own, other, pieces, w_all, coef, first):
    spec = pl.BlockSpec(memory_space=pltpu.VMEM)
    out = jax.ShapeDtypeStruct((TOK, HALF), bf16)
    return pl.pallas_call(
        attn_kernel,
        out_shape=(out, out),
        in_specs=[pl.BlockSpec(memory_space=pltpu.SMEM)] + [spec] * 6,
        out_specs=(spec, spec),
        compiler_params=pltpu.CompilerParams(vmem_limit_bytes=24 * 1024 * 1024),
        cost_estimate=pl.CostEstimate(
            flops=4 * TOK * HALF * D, bytes_accessed=8 * 1024 * 1024, transcendentals=0
        ),
        name="attn_grads",
    )(shift, own, other, pieces, w_all, coef, first)


def body(hidden_state, attn_out, o_weight, norm_gain, lengths, positive):
    ix, iy, ic = lax.axis_index("x"), lax.axis_index("y"), lax.axis_index("c")
    it, ir = lax.axis_index("t"), lax.axis_index("r")
    dp_index = (ix * NY + iy) * NC + ic

    state = hidden_state.reshape(TOK, FEAT)
    states = state.astype(f32).reshape(2, SEQ, FEAT)
    attn = attn_out.reshape(TOK, FEAT)
    state_all = lax.all_to_all(jnp.broadcast_to(state[None], (NT, TOK, FEAT)), "t", 0, 0)
    w_start = (ic * NY + iy) * W_ROWS
    w_mine = lax.dynamic_slice(o_weight, (w_start, 0), (W_ROWS, COLS))
    w_moved = lax.ppermute(
        w_mine,
        ("x", "r"),
        [(i * NR + (j + i) % NR, i * NR + j) for i in range(NX) for j in range(NR)],
    )
    attn_keep = jnp.where(ic == 0, attn[:, :HALF], attn[:, HALF:])
    attn_give = jnp.where(ic == 0, attn[:, HALF:], attn[:, :HALF])
    attn_other = swap_core(attn_give)
    gains = [norm_gain.reshape(1, FEAT)]
    for step in range(1, NT):
        gains.append(
            lax.ppermute(gains[0], "t", [(j, (j + step) % NT) for j in range(NT)])
        )
    gains = jnp.stack(gains)
    gain = jnp.concatenate(
        [
            lax.dynamic_index_in_dim(gains, (it - source) % NT, 0, keepdims=False)
            for source in range(NT)
        ],
        1,
    )
    state_all, attn_other, gain = lax.optimization_barrier((state_all, attn_other, gain))

    send = front(lengths.reshape(2), positive, state_all, attn)
    send, w_moved = lax.optimization_barrier((send, w_moved))
    w_all = lax.all_gather(w_moved, PLANE).reshape(NX, HALF, COLS)
    got = lax.all_to_all(send, DP, 0, 0)

    other_index = dp_index + 1 - 2 * ic
    state_other = swap_core(state_all)
    scaled, first, gain_part, loss_part, pieces, scale, first_col = group_math(
        jnp.stack([dp_index, other_index]), got.transpose(1, 0, 2), gain
    )

    partial, coef = weight_partials(
        state_all, state_other, attn_keep, attn_other, pieces, scale
    )
    partial, first = lax.optimization_barrier((partial, first))
    spread = lax.all_to_all(partial, PLANE, 0, 0)

    gain_mine = lax.dynamic_index_in_dim(gain_part, it, 0, keepdims=False)
    tail = jnp.concatenate([gain_mine, jnp.broadcast_to(loss_part[:1, :1], (1, FEAT))], 0)
    tails = [tail]
    first_sum = lax.dynamic_index_in_dim(first, ir, 0, keepdims=False)
    for step in range(1, NR):
        outgoing = lax.dynamic_index_in_dim(first, (ir + step) % NR, 0, keepdims=False)
        arrived = lax.ppermute(
            jnp.concatenate([outgoing, tail], 0),
            "r",
            [(j, (j + step) % NR) for j in range(NR)],
        )
        first_sum = first_sum + arrived[:SLICE]
        tails.append(arrived[SLICE:])
    tails = jnp.stack(tails)
    totals = jnp.zeros((2, FEAT), f32)
    for source in range(NR):
        totals = totals + lax.dynamic_index_in_dim(
            tails, (ir - source) % NR, 0, keepdims=False
        )

    row_here = lax.dynamic_slice(scaled, (0, dp_index, it * FEAT), (2, 1, FEAT))
    state_grad = first_col[0].reshape(2, SEQ, 1) * row_here - states * coef[0].reshape(2, SEQ, 1)
    grad_hidden = state_grad.astype(bf16).reshape(1, 2, SEQ, FEAT)
    keep, give = attn_grads(
        ir.reshape(1), state_all, state_other, pieces, w_all, coef, first_col
    )

    arrived = swap_core(give)
    grad_attn = jnp.where(
        ic == 0, jnp.concatenate([keep, arrived], 1), jnp.concatenate([arrived, keep], 1)
    ).reshape(1, 2, SEQ, FEAT)
    spread, first_sum, totals, grad_attn, grad_hidden = lax.optimization_barrier(
        (spread, first_sum, totals, grad_attn, grad_hidden)
    )
    second = jnp.sum(spread.astype(f32), 0).reshape(NR, SLICE, COLS)
    second = lax.all_to_all(second.astype(bf16), "r", 0, 0)

    second_sum = jnp.sum(second.astype(f32), 0)
    total = first_sum - second_sum
    done = jnp.broadcast_to(total.astype(bf16)[None], (NX * NY, SLICE, COLS))
    half = lax.all_to_all(done, PLANE, 0, 0).reshape(HALF, COLS)
    half_other = swap_core(half)
    grad_weight = jnp.where(
        ic == 0,
        jnp.concatenate([half, half_other], 0),
        jnp.concatenate([half_other, half], 0),
    )

    return (grad_hidden, grad_attn, grad_weight, totals[0], totals[1, 0])


def solution(mesh):
    fine = Mesh(mesh.devices.reshape(NX, NY, NC, NT, NR), ("x", "y", "c", "t", "r"))
    pairs = ("x", "y", "c", "r")
    placed = (
        P(pairs, None, None, "t"),
        P(pairs, None, None, "t"),
        P("t", "r"),
        P("t"),
        P(pairs, None),
        P(pairs),
    )
    return jax.shard_map(
        body,
        mesh=fine,
        in_specs=placed,
        out_specs=(
            P(pairs, None, None, "t"),
            P(pairs, None, None, "t"),
            P("t", "r"),
            P("t"),
            P(),
        ),
        check_vma=False,
    )
```

```python
import jax
import jax.numpy as jnp
from jax import lax
from jax.experimental import pallas as pl
from jax.experimental.pallas import tpu as pltpu
from jax.sharding import Mesh, PartitionSpec as P

logit_scale = 20.0
grad_scale = 256.0
epsilon = 1e-06

f32 = jnp.float32
bf16 = jnp.bfloat16

NX, NY, NC, NT, NR = 4, 4, 2, 4, 4
PLANE = ("x", "y")
DP = ("x", "y", "c")

D = 3584
FEAT = D // NT
COLS = D // NR
SEQ = 128
TOK = 2 * SEQ
HALF = FEAT // NC
SLICE = HALF // (NX * NY)
W_ROWS = HALF // NY
PIECES = 16
GROUP = NX * NY * NC

AT_RMS = D
AT_U = D + SEQ
AT_LEN = AT_U + SLICE
AT_POS = AT_LEN + 1
WIDTH = D + 2 * SEQ


def swap_core(value):
    return lax.ppermute(value, "c", [(0, 1), (1, 0)])


contract_last = (((1,), (1,)), ((), ()))
contract_first = (((0,), (0,)), ((), ()))


def dot_last(left, right):
    return lax.dot_general(left, right, contract_last, preferred_element_type=f32)


def dot_exact(left, right, dims):
    return lax.dot_general(
        left, right, dims, precision=lax.Precision.HIGHEST, preferred_element_type=f32
    )


def group_kernel(
    index_ref, got_ref, gain_ref,
    scaled_ref, first_ref, gain_out_ref, loss_ref, pieces_ref, scale_ref, column_ref,
):
    gain = gain_ref[...]
    raw, unit, inv_norm = [], [], []
    for side in range(2):
        raw.append(got_ref[side, :, :D])
        embeds = raw[side] * gain
        square = jnp.sum(embeds * embeds, -1, keepdims=True)
        inv_norm.append(lax.rsqrt(square + epsilon))
        unit.append(embeds * inv_norm[side])
    logits = logit_scale * dot_exact(unit[0], unit[1], contract_last)
    log_total = jnp.log(jnp.sum(jnp.exp(logits), -1, keepdims=True))
    target = got_ref[0, :, AT_POS : AT_POS + 1]
    passage = lax.broadcasted_iota(jnp.int32, (GROUP, GROUP), 1).astype(f32)
    one_hot = jnp.where(passage == target, 1.0, 0.0)
    chosen = jnp.sum(logits * one_hot, -1, keepdims=True)
    loss = jnp.sum(log_total - chosen, 0, keepdims=True)
    loss_ref[...] = jnp.broadcast_to(loss, (8, 128))
    score_grad = grad_scale * (jnp.exp(logits - log_total) - one_hot)
    grads = (
        dot_exact(score_grad, unit[1], (((1,), (0,)), ((), ()))),
        dot_exact(score_grad, unit[0], contract_first),
    )
    gain_sum = jnp.zeros((1, D), f32)
    first = jnp.zeros((SLICE, D), f32)
    for side in range(2):
        grad = logit_scale * grads[side]
        along = jnp.sum(unit[side] * grad, -1, keepdims=True)
        pooled_grad = (grad - unit[side] * along) * inv_norm[side]
        gain_sum = gain_sum + jnp.sum(pooled_grad * raw[side], 0, keepdims=True)
        scaled = pooled_grad * gain
        scaled_ref[side] = scaled
        first = first + dot_exact(got_ref[side, :, AT_U:AT_LEN], scaled, contract_first)
    for block in range(NR):
        columns = slice(block * COLS, (block + 1) * COLS)
        first_ref[block] = first[:, columns]
        gain_out_ref[block] = gain_sum[:, columns]

    token = lax.broadcasted_iota(jnp.int32, (SEQ, SEQ), 0)
    lane = lax.broadcasted_iota(jnp.int32, (SEQ, SEQ), 1)
    position = lax.broadcasted_iota(jnp.int32, (SEQ, 1), 0).astype(f32)
    for pair in range(NC):
        index = index_ref[pair]
        chosen_row = lax.broadcasted_iota(jnp.int32, (GROUP, 1), 0) == index
        parts = []
        for side in range(2):
            row = jnp.sum(jnp.where(chosen_row, scaled_ref[side], 0.0), 0, keepdims=True)
            high = row.astype(bf16).astype(f32)
            mid = (row - high).astype(bf16).astype(f32)
            parts += [high, mid, row - high - mid]
            rest = jnp.where(chosen_row, got_ref[side, :, AT_RMS:WIDTH], 0.0)
            rest = jnp.sum(rest, 0, keepdims=True)
            rms_row = rest[:, :SEQ]
            count = rest[:, AT_LEN - AT_RMS : AT_LEN - AT_RMS + 1]
            rms = jnp.sum(jnp.where(token == lane, rms_row, 0.0), -1, keepdims=True)
            column = jnp.where(position < count, rms / count, 0.0)
            here = slice(side * SEQ, (side + 1) * SEQ)
            column_ref[pair, here, :] = column
            scale_ref[pair, here, :] = column * rms * rms * (1.0 / D)
        parts.append(jnp.zeros((PIECES - 6, D), f32))
        piece = jnp.concatenate(parts, 0).astype(bf16)
        for block in range(NR):
            pieces_ref[pair, block] = piece[:, block * COLS : (block + 1) * COLS]


def group_math(index, got, gain):
    spec = pl.BlockSpec(memory_space=pltpu.VMEM)
    return pl.pallas_call(
        group_kernel,
        out_shape=(
            jax.ShapeDtypeStruct((2, GROUP, D), f32),
            jax.ShapeDtypeStruct((NR, SLICE, COLS), f32),
            jax.ShapeDtypeStruct((NR, 1, COLS), f32),
            jax.ShapeDtypeStruct((8, 128), f32),
            jax.ShapeDtypeStruct((NC, NR, PIECES, COLS), bf16),
            jax.ShapeDtypeStruct((NC, TOK, 1), f32),
            jax.ShapeDtypeStruct((NC, TOK, 1), f32),
        ),
        in_specs=[pl.BlockSpec(memory_space=pltpu.SMEM), spec, spec],
        out_specs=(spec,) * 7,
        compiler_params=pltpu.CompilerParams(vmem_limit_bytes=16 * 1024 * 1024),
        cost_estimate=pl.CostEstimate(
            flops=50 * GROUP * GROUP * D, bytes_accessed=3 * 1024 * 1024, transcendentals=4096
        ),
        name="group_math",
    )(index, got, gain)


def weight_kernel(
    own_ref, other_ref, keep_ref, given_ref, pieces_ref, scale_ref, out_ref, coef_ref, acc_ref
):
    token = lax.broadcasted_iota(jnp.int32, (TOK, PIECES), 0)
    part = lax.broadcasted_iota(jnp.int32, (TOK, PIECES), 1)
    part = part - jnp.where(token < SEQ, 0, 3)
    mask = (part >= 0) & (part < 3)
    scaled = []
    for pair, (state_ref, attn_ref) in enumerate(
        ((own_ref, keep_ref), (other_ref, given_ref))
    ):
        inner = jnp.zeros((TOK, PIECES), f32)
        for block in range(NT):
            inner = inner + dot_last(state_ref[block], pieces_ref[pair, block])
        inner = jnp.sum(jnp.where(mask, inner, 0.0), -1, keepdims=True)
        coef = scale_ref[pair] * inner
        coef_ref[pair] = coef
        scaled.append((attn_ref[...].astype(f32) * coef).astype(bf16))
    for block in range(NT):
        acc_ref[block] = lax.dot_general(
            scaled[0], own_ref[block], contract_first, preferred_element_type=f32
        ) + lax.dot_general(
            scaled[1], other_ref[block], contract_first, preferred_element_type=f32
        )
    for place in range(NX * NY):
        rows = [
            acc_ref[block, place * SLICE : (place + 1) * SLICE, :] for block in range(NR)
        ]
        out_ref[place] = jnp.concatenate(rows, 0).astype(bf16)


def weight_partials(own, other, keep, given, pieces, scale):
    spec = pl.BlockSpec(memory_space=pltpu.VMEM)
    return pl.pallas_call(
        weight_kernel,
        out_shape=(
            jax.ShapeDtypeStruct((NX * NY, NR * SLICE, COLS), bf16),
            jax.ShapeDtypeStruct((NC, TOK, 1), f32),
        ),
        in_specs=[spec] * 6,
        out_specs=(spec, spec),
        scratch_shapes=[pltpu.VMEM((NR, HALF, COLS), f32)],
        compiler_params=pltpu.CompilerParams(vmem_limit_bytes=24 * 1024 * 1024),
        cost_estimate=pl.CostEstimate(
            flops=4 * TOK * HALF * D, bytes_accessed=8 * 1024 * 1024, transcendentals=0
        ),
        name="weight_partials",
    )(own, other, keep, given, pieces, scale)


def sum_kernel(spread_ref, out_ref, acc_ref):
    step = pl.program_id(0)
    part = spread_ref[0].astype(f32)
    for place in range(1, spread_ref.shape[0]):
        part = part + spread_ref[place].astype(f32)

    @pl.when(step == 0)
    def _():
        acc_ref[...] = part

    @pl.when(step > 0)
    def _():
        acc_ref[...] += part

    @pl.when(step == NX - 1)
    def _():
        for block in range(NR):
            out_ref[block] = acc_ref[block * SLICE : (block + 1) * SLICE, :].astype(bf16)


def sum_senders(spread):
    return pl.pallas_call(
        sum_kernel,
        grid=(NX,),
        out_shape=jax.ShapeDtypeStruct((NR, SLICE, COLS), bf16),
        in_specs=[pl.BlockSpec((NY, NR * SLICE, COLS), lambda step: (step, 0, 0))],
        out_specs=pl.BlockSpec((NR, SLICE, COLS), lambda step: (0, 0, 0)),
        scratch_shapes=[pltpu.VMEM((NR * SLICE, COLS), f32)],
        compiler_params=pltpu.CompilerParams(vmem_limit_bytes=16 * 1024 * 1024),
        cost_estimate=pl.CostEstimate(
            flops=NX * NY * NR * SLICE * COLS, bytes_accessed=4 * 1024 * 1024, transcendentals=0
        ),
        name="sum_senders",
    )(spread)


def join_kernel(core_ref, mine_ref, other_ref, out_ref):
    core = core_ref[0]
    for which, ref in ((core, mine_ref), (1 - core, other_ref)):
        rows = [ref[place].astype(f32) for place in range(NX * NY)]
        out_ref[pl.ds(pl.multiple_of(which * HALF, HALF), HALF), :] = jnp.concatenate(
            rows, 0
        ).astype(bf16)


def join_halves(core, mine, other):
    spec = pl.BlockSpec(memory_space=pltpu.VMEM)
    return pl.pallas_call(
        join_kernel,
        out_shape=jax.ShapeDtypeStruct((FEAT, COLS), bf16),
        in_specs=[pl.BlockSpec(memory_space=pltpu.SMEM), spec, spec],
        out_specs=spec,
        compiler_params=pltpu.CompilerParams(vmem_limit_bytes=16 * 1024 * 1024),
        cost_estimate=pl.CostEstimate(
            flops=0, bytes_accessed=4 * 1024 * 1024, transcendentals=0
        ),
        name="join_halves",
    )(core, mine, other)


def attn_kernel(
    shift_ref, own_ref, other_ref, pieces_ref, w_ref, coef_ref, first_ref, keep_ref, give_ref
):
    shift = shift_ref[0]
    for pair, (state_ref, out_ref) in enumerate(((own_ref, keep_ref), (other_ref, give_ref))):
        tokens = jnp.zeros((TOK, HALF), f32)
        rows = jnp.zeros((PIECES, HALF), f32)
        for block in range(NX):
            which = lax.rem(shift + block, NR)
            tokens = tokens + dot_last(state_ref[which], w_ref[block])
            rows = rows + dot_last(pieces_ref[pair, which], w_ref[block])
        for side in range(2):
            row = rows[3 * side + 2 : 3 * side + 3] + rows[3 * side + 1 : 3 * side + 2]
            row = row + rows[3 * side : 3 * side + 1]
            here = slice(side * SEQ, (side + 1) * SEQ)
            out_ref[here, :] = (
                first_ref[pair, here, :] * row - coef_ref[pair, here, :] * tokens[here]
            ).astype(bf16)


def attn_grads(shift, own, other, pieces, w_all, coef, first):
    spec = pl.BlockSpec(memory_space=pltpu.VMEM)
    out = jax.ShapeDtypeStruct((TOK, HALF), bf16)
    return pl.pallas_call(
        attn_kernel,
        out_shape=(out, out),
        in_specs=[pl.BlockSpec(memory_space=pltpu.SMEM)] + [spec] * 6,
        out_specs=(spec, spec),
        compiler_params=pltpu.CompilerParams(vmem_limit_bytes=24 * 1024 * 1024),
        cost_estimate=pl.CostEstimate(
            flops=4 * TOK * HALF * D, bytes_accessed=8 * 1024 * 1024, transcendentals=0
        ),
        name="attn_grads",
    )(shift, own, other, pieces, w_all, coef, first)


def body(hidden_state, attn_out, o_weight, norm_gain, lengths, positive):
    ix, iy, ic = lax.axis_index("x"), lax.axis_index("y"), lax.axis_index("c")
    it, ir = lax.axis_index("t"), lax.axis_index("r")
    dp_index = (ix * NY + iy) * NC + ic

    state = hidden_state.reshape(TOK, FEAT)
    attn = attn_out.reshape(TOK, FEAT)
    state_all = lax.all_gather(state, "t")
    w_start = (ic * NY + iy) * W_ROWS
    w_mine = lax.dynamic_slice(o_weight, (w_start, 0), (W_ROWS, COLS))
    w_moved = lax.ppermute(
        w_mine,
        ("x", "r"),
        [(i * NR + (j + i) % NR, i * NR + j) for i in range(NX) for j in range(NR)],
    )
    attn_keep = jnp.where(ic == 0, attn[:, :HALF], attn[:, HALF:])
    attn_give = jnp.where(ic == 0, attn[:, HALF:], attn[:, :HALF])
    attn_other = swap_core(attn_give)

    states = state.astype(f32).reshape(2, SEQ, FEAT)
    square = lax.psum(jnp.sum(states * states, -1), "t") / D
    inv_rms = lax.rsqrt(square + epsilon)
    token_count = lengths.reshape(2).astype(f32)
    valid = (jnp.arange(SEQ, dtype=jnp.int32)[None, :] < lengths.reshape(2)[:, None]).astype(f32)
    pool_weight = valid * inv_rms / token_count[:, None]
    pooled = jnp.sum(pool_weight[..., None] * states, 1)
    attn_pool = jnp.sum(pool_weight[..., None] * attn.astype(f32).reshape(2, SEQ, FEAT), 1)

    near = jnp.concatenate([pooled, norm_gain[None]], 0)
    near = lax.all_to_all(jnp.broadcast_to(near[None], (NT, 3, FEAT)), "t", 0, 0)
    pooled_row = near[:, :2].transpose(1, 0, 2).reshape(2, D)
    gain = near[:, 2].reshape(1, D)

    u_parts = attn_pool.reshape(2, NC, NX * NY, SLICE).transpose(2, 1, 0, 3)
    u_parts = u_parts.reshape(GROUP, 2, SLICE)
    extra = jnp.stack(
        [token_count, jnp.broadcast_to(positive.astype(f32), (2,))], -1
    )
    row = jnp.concatenate([pooled_row, inv_rms], -1)
    send = jnp.concatenate(
        [
            jnp.broadcast_to(row[None], (GROUP, 2, D + SEQ)),
            u_parts,
            jnp.broadcast_to(extra[None], (GROUP, 2, 2)),
            jnp.zeros((GROUP, 2, WIDTH - AT_POS - 1), f32),
        ],
        -1,
    )
    got = lax.all_to_all(send, DP, 0, 0)
    got, state_all, attn_other = lax.optimization_barrier((got, state_all, attn_other))

    other_index = dp_index + 1 - 2 * ic
    state_other = swap_core(state_all)
    scaled, first, gain_part, loss_part, pieces, scale, first_col = group_math(
        jnp.stack([dp_index, other_index]), got.transpose(1, 0, 2), gain
    )

    partial, coef = weight_partials(
        state_all, state_other, attn_keep, attn_other, pieces, scale
    )
    partial, first, w_moved = lax.optimization_barrier((partial, first, w_moved))
    w_all = lax.all_gather(w_moved, PLANE).reshape(NX, HALF, COLS)
    spread = lax.all_to_all(partial, PLANE, 0, 0)

    gain_mine = lax.dynamic_index_in_dim(gain_part, it, 0, keepdims=False)
    tail = jnp.concatenate([gain_mine, jnp.broadcast_to(loss_part[:1, :1], (1, FEAT))], 0)
    tails = [tail]
    first_sum = lax.dynamic_index_in_dim(first, ir, 0, keepdims=False)
    for step in range(1, NR):
        outgoing = lax.dynamic_index_in_dim(first, (ir + step) % NR, 0, keepdims=False)
        arrived = lax.ppermute(
            jnp.concatenate([outgoing, tail], 0),
            "r",
            [(j, (j + step) % NR) for j in range(NR)],
        )
        first_sum = first_sum + arrived[:SLICE]
        tails.append(arrived[SLICE:])
    tails = jnp.stack(tails)
    totals = jnp.zeros((2, FEAT), f32)
    for source in range(NR):
        totals = totals + lax.dynamic_index_in_dim(
            tails, (ir - source) % NR, 0, keepdims=False
        )

    spread, first_sum, totals = lax.optimization_barrier((spread, first_sum, totals))
    second = lax.all_to_all(sum_senders(spread), "r", 0, 0)

    row_here = lax.dynamic_slice(scaled, (0, dp_index, it * FEAT), (2, 1, FEAT))
    state_grad = first_col[0].reshape(2, SEQ, 1) * row_here - states * coef[0].reshape(2, SEQ, 1)
    grad_hidden = state_grad.astype(bf16).reshape(1, 2, SEQ, FEAT)
    keep, give = attn_grads(
        ir.reshape(1), state_all, state_other, pieces, w_all, coef, first_col
    )

    second_sum = jnp.sum(second.astype(f32), 0)
    total = first_sum - second_sum
    done = jnp.broadcast_to(total.astype(bf16)[None], (NX * NY, SLICE, COLS))
    half = lax.all_to_all(done, PLANE, 0, 0)
    half, keep, give, grad_hidden, totals = lax.optimization_barrier(
        (half, keep, give, grad_hidden, totals)
    )
    half_other = swap_core(half)
    arrived = swap_core(give)
    grad_attn = jnp.where(
        ic == 0, jnp.concatenate([keep, arrived], 1), jnp.concatenate([arrived, keep], 1)
    ).reshape(1, 2, SEQ, FEAT)
    grad_weight = join_halves(ic.reshape(1), half, half_other)
    return (grad_hidden, grad_attn, grad_weight, totals[0], totals[1, 0])


def solution(mesh):
    fine = Mesh(mesh.devices.reshape(NX, NY, NC, NT, NR), ("x", "y", "c", "t", "r"))
    pairs = ("x", "y", "c", "r")
    placed = (
        P(pairs, None, None, "t"),
        P(pairs, None, None, "t"),
        P("t", "r"),
        P("t"),
        P(pairs, None),
        P(pairs),
    )
    return jax.shard_map(
        body,
        mesh=fine,
        in_specs=placed,
        out_specs=(
            P(pairs, None, None, "t"),
            P(pairs, None, None, "t"),
            P("t", "r"),
            P("t"),
            P(),
        ),
        check_vma=False,
    )
```

```python
import jax
import jax.numpy as jnp
from jax import lax
from jax.experimental import pallas as pl
from jax.experimental.pallas import tpu as pltpu
from jax.sharding import Mesh, PartitionSpec as P

logit_scale = 20.0
grad_scale = 256.0
epsilon = 1e-06

f32 = jnp.float32
bf16 = jnp.bfloat16

NX, NY, NC, NT, NR = 4, 4, 2, 4, 4
PLANE = ("x", "y")
DP = ("x", "y", "c")

D = 3584
FEAT = D // NT
COLS = D // NR
SEQ = 128
TOK = 2 * SEQ
HALF = FEAT // NC
SLICE = HALF // (NX * NY)
W_ROWS = HALF // NY
PIECES = 16
GROUP = NX * NY * NC

AT_RMS = D
AT_U = D + SEQ
AT_LEN = AT_U + SLICE
AT_POS = AT_LEN + 1
WIDTH = D + 2 * SEQ


def swap_core(value):
    return lax.ppermute(value, "c", [(0, 1), (1, 0)])


contract_last = (((1,), (1,)), ((), ()))
contract_first = (((0,), (0,)), ((), ()))


def dot_last(left, right):
    return lax.dot_general(left, right, contract_last, preferred_element_type=f32)


def dot_exact(left, right, dims):
    return lax.dot_general(
        left, right, dims, precision=lax.Precision.HIGHEST, preferred_element_type=f32
    )


def group_kernel(
    index_ref, got_ref, gain_ref,
    scaled_ref, first_ref, gain_out_ref, loss_ref, pieces_ref, scale_ref, column_ref,
):
    gain = gain_ref[...]
    raw, unit, inv_norm = [], [], []
    for side in range(2):
        raw.append(got_ref[side, :, :D])
        embeds = raw[side] * gain
        square = jnp.sum(embeds * embeds, -1, keepdims=True)
        inv_norm.append(lax.rsqrt(square + epsilon))
        unit.append(embeds * inv_norm[side])
    logits = logit_scale * dot_exact(unit[0], unit[1], contract_last)
    log_total = jnp.log(jnp.sum(jnp.exp(logits), -1, keepdims=True))
    target = got_ref[0, :, AT_POS : AT_POS + 1]
    passage = lax.broadcasted_iota(jnp.int32, (GROUP, GROUP), 1).astype(f32)
    one_hot = jnp.where(passage == target, 1.0, 0.0)
    chosen = jnp.sum(logits * one_hot, -1, keepdims=True)
    loss = jnp.sum(log_total - chosen, 0, keepdims=True)
    loss_ref[...] = jnp.broadcast_to(loss, (8, 128))
    score_grad = grad_scale * (jnp.exp(logits - log_total) - one_hot)
    grads = (
        dot_exact(score_grad, unit[1], (((1,), (0,)), ((), ()))),
        dot_exact(score_grad, unit[0], contract_first),
    )
    gain_sum = jnp.zeros((1, D), f32)
    first = jnp.zeros((SLICE, D), f32)
    for side in range(2):
        grad = logit_scale * grads[side]
        along = jnp.sum(unit[side] * grad, -1, keepdims=True)
        pooled_grad = (grad - unit[side] * along) * inv_norm[side]
        gain_sum = gain_sum + jnp.sum(pooled_grad * raw[side], 0, keepdims=True)
        scaled = pooled_grad * gain
        scaled_ref[side] = scaled
        first = first + dot_exact(got_ref[side, :, AT_U:AT_LEN], scaled, contract_first)
    for block in range(NR):
        columns = slice(block * COLS, (block + 1) * COLS)
        first_ref[block] = first[:, columns]
        gain_out_ref[block] = gain_sum[:, columns]

    token = lax.broadcasted_iota(jnp.int32, (SEQ, SEQ), 0)
    lane = lax.broadcasted_iota(jnp.int32, (SEQ, SEQ), 1)
    position = lax.broadcasted_iota(jnp.int32, (SEQ, 1), 0).astype(f32)
    for pair in range(NC):
        index = index_ref[pair]
        chosen_row = lax.broadcasted_iota(jnp.int32, (GROUP, 1), 0) == index
        parts = []
        for side in range(2):
            row = jnp.sum(jnp.where(chosen_row, scaled_ref[side], 0.0), 0, keepdims=True)
            high = row.astype(bf16).astype(f32)
            mid = (row - high).astype(bf16).astype(f32)
            parts += [high, mid, row - high - mid]
            rest = jnp.where(chosen_row, got_ref[side, :, AT_RMS:WIDTH], 0.0)
            rest = jnp.sum(rest, 0, keepdims=True)
            rms_row = rest[:, :SEQ]
            count = rest[:, AT_LEN - AT_RMS : AT_LEN - AT_RMS + 1]
            rms = jnp.sum(jnp.where(token == lane, rms_row, 0.0), -1, keepdims=True)
            column = jnp.where(position < count, rms / count, 0.0)
            here = slice(side * SEQ, (side + 1) * SEQ)
            column_ref[pair, here, :] = column
            scale_ref[pair, here, :] = column * rms * rms * (1.0 / D)
        parts.append(jnp.zeros((PIECES - 6, D), f32))
        piece = jnp.concatenate(parts, 0).astype(bf16)
        for block in range(NR):
            pieces_ref[pair, block] = piece[:, block * COLS : (block + 1) * COLS]


def group_math(index, got, gain):
    spec = pl.BlockSpec(memory_space=pltpu.VMEM)
    return pl.pallas_call(
        group_kernel,
        out_shape=(
            jax.ShapeDtypeStruct((2, GROUP, D), f32),
            jax.ShapeDtypeStruct((NR, SLICE, COLS), f32),
            jax.ShapeDtypeStruct((NR, 1, COLS), f32),
            jax.ShapeDtypeStruct((8, 128), f32),
            jax.ShapeDtypeStruct((NC, NR, PIECES, COLS), bf16),
            jax.ShapeDtypeStruct((NC, TOK, 1), f32),
            jax.ShapeDtypeStruct((NC, TOK, 1), f32),
        ),
        in_specs=[pl.BlockSpec(memory_space=pltpu.SMEM), spec, spec],
        out_specs=(spec,) * 7,
        compiler_params=pltpu.CompilerParams(vmem_limit_bytes=16 * 1024 * 1024),
        cost_estimate=pl.CostEstimate(
            flops=50 * GROUP * GROUP * D, bytes_accessed=3 * 1024 * 1024, transcendentals=4096
        ),
        name="group_math",
    )(index, got, gain)


def weight_kernel(
    own_ref, other_ref, keep_ref, given_ref, pieces_ref, scale_ref, out_ref, coef_ref, acc_ref
):
    token = lax.broadcasted_iota(jnp.int32, (TOK, PIECES), 0)
    part = lax.broadcasted_iota(jnp.int32, (TOK, PIECES), 1)
    part = part - jnp.where(token < SEQ, 0, 3)
    mask = (part >= 0) & (part < 3)
    scaled = []
    for pair, (state_ref, attn_ref) in enumerate(
        ((own_ref, keep_ref), (other_ref, given_ref))
    ):
        inner = jnp.zeros((TOK, PIECES), f32)
        for block in range(NT):
            inner = inner + dot_last(state_ref[block], pieces_ref[pair, block])
        inner = jnp.sum(jnp.where(mask, inner, 0.0), -1, keepdims=True)
        coef = scale_ref[pair] * inner
        coef_ref[pair] = coef
        scaled.append((attn_ref[...].astype(f32) * coef).astype(bf16))
    for block in range(NT):
        acc_ref[block] = lax.dot_general(
            scaled[0], own_ref[block], contract_first, preferred_element_type=f32
        ) + lax.dot_general(
            scaled[1], other_ref[block], contract_first, preferred_element_type=f32
        )
    for place in range(NX * NY):
        rows = [
            acc_ref[block, place * SLICE : (place + 1) * SLICE, :] for block in range(NR)
        ]
        out_ref[place] = jnp.concatenate(rows, 0).astype(bf16)


def weight_partials(own, other, keep, given, pieces, scale):
    spec = pl.BlockSpec(memory_space=pltpu.VMEM)
    return pl.pallas_call(
        weight_kernel,
        out_shape=(
            jax.ShapeDtypeStruct((NX * NY, NR * SLICE, COLS), bf16),
            jax.ShapeDtypeStruct((NC, TOK, 1), f32),
        ),
        in_specs=[spec] * 6,
        out_specs=(spec, spec),
        scratch_shapes=[pltpu.VMEM((NR, HALF, COLS), f32)],
        compiler_params=pltpu.CompilerParams(vmem_limit_bytes=24 * 1024 * 1024),
        cost_estimate=pl.CostEstimate(
            flops=4 * TOK * HALF * D, bytes_accessed=8 * 1024 * 1024, transcendentals=0
        ),
        name="weight_partials",
    )(own, other, keep, given, pieces, scale)


def sum_kernel(spread_ref, out_ref, acc_ref):
    step = pl.program_id(0)
    part = spread_ref[0].astype(f32)
    for place in range(1, spread_ref.shape[0]):
        part = part + spread_ref[place].astype(f32)

    @pl.when(step == 0)
    def _():
        acc_ref[...] = part

    @pl.when(step > 0)
    def _():
        acc_ref[...] += part

    @pl.when(step == NX - 1)
    def _():
        for block in range(NR):
            out_ref[block] = acc_ref[block * SLICE : (block + 1) * SLICE, :].astype(bf16)


def sum_senders(spread):
    return pl.pallas_call(
        sum_kernel,
        grid=(NX,),
        out_shape=jax.ShapeDtypeStruct((NR, SLICE, COLS), bf16),
        in_specs=[pl.BlockSpec((NY, NR * SLICE, COLS), lambda step: (step, 0, 0))],
        out_specs=pl.BlockSpec((NR, SLICE, COLS), lambda step: (0, 0, 0)),
        scratch_shapes=[pltpu.VMEM((NR * SLICE, COLS), f32)],
        compiler_params=pltpu.CompilerParams(vmem_limit_bytes=16 * 1024 * 1024),
        cost_estimate=pl.CostEstimate(
            flops=NX * NY * NR * SLICE * COLS, bytes_accessed=4 * 1024 * 1024, transcendentals=0
        ),
        name="sum_senders",
    )(spread)


def join_kernel(core_ref, mine_ref, other_ref, out_ref):
    core = core_ref[0]
    for which, ref in ((core, mine_ref), (1 - core, other_ref)):
        rows = [ref[place].astype(f32) for place in range(NX * NY)]
        out_ref[pl.ds(pl.multiple_of(which * HALF, HALF), HALF), :] = jnp.concatenate(
            rows, 0
        ).astype(bf16)


def join_halves(core, mine, other):
    spec = pl.BlockSpec(memory_space=pltpu.VMEM)
    return pl.pallas_call(
        join_kernel,
        out_shape=jax.ShapeDtypeStruct((FEAT, COLS), bf16),
        in_specs=[pl.BlockSpec(memory_space=pltpu.SMEM), spec, spec],
        out_specs=spec,
        compiler_params=pltpu.CompilerParams(vmem_limit_bytes=16 * 1024 * 1024),
        cost_estimate=pl.CostEstimate(
            flops=0, bytes_accessed=4 * 1024 * 1024, transcendentals=0
        ),
        name="join_halves",
    )(core, mine, other)


def attn_kernel(
    shift_ref, own_ref, other_ref, pieces_ref, w_ref, coef_ref, first_ref, keep_ref, give_ref
):
    shift = shift_ref[0]
    for pair, (state_ref, out_ref) in enumerate(((own_ref, keep_ref), (other_ref, give_ref))):
        tokens = jnp.zeros((TOK, HALF), f32)
        rows = jnp.zeros((PIECES, HALF), f32)
        for block in range(NX):
            which = lax.rem(shift + block, NR)
            tokens = tokens + dot_last(state_ref[which], w_ref[block])
            rows = rows + dot_last(pieces_ref[pair, which], w_ref[block])
        for side in range(2):
            row = rows[3 * side + 2 : 3 * side + 3] + rows[3 * side + 1 : 3 * side + 2]
            row = row + rows[3 * side : 3 * side + 1]
            here = slice(side * SEQ, (side + 1) * SEQ)
            out_ref[here, :] = (
                first_ref[pair, here, :] * row - coef_ref[pair, here, :] * tokens[here]
            ).astype(bf16)


def attn_grads(shift, own, other, pieces, w_all, coef, first):
    spec = pl.BlockSpec(memory_space=pltpu.VMEM)
    out = jax.ShapeDtypeStruct((TOK, HALF), bf16)
    return pl.pallas_call(
        attn_kernel,
        out_shape=(out, out),
        in_specs=[pl.BlockSpec(memory_space=pltpu.SMEM)] + [spec] * 6,
        out_specs=(spec, spec),
        compiler_params=pltpu.CompilerParams(vmem_limit_bytes=24 * 1024 * 1024),
        cost_estimate=pl.CostEstimate(
            flops=4 * TOK * HALF * D, bytes_accessed=8 * 1024 * 1024, transcendentals=0
        ),
        name="attn_grads",
    )(shift, own, other, pieces, w_all, coef, first)


def body(hidden_state, attn_out, o_weight, norm_gain, lengths, positive):
    ix, iy, ic = lax.axis_index("x"), lax.axis_index("y"), lax.axis_index("c")
    it, ir = lax.axis_index("t"), lax.axis_index("r")
    dp_index = (ix * NY + iy) * NC + ic

    state = hidden_state.reshape(TOK, FEAT)
    attn = attn_out.reshape(TOK, FEAT)
    state_all = lax.all_gather(state, "t")
    w_start = (ic * NY + iy) * W_ROWS
    w_mine = lax.dynamic_slice(o_weight, (w_start, 0), (W_ROWS, COLS))
    w_moved = lax.ppermute(
        w_mine,
        ("x", "c", "r"),
        [
            ((i * NC + k) * NR + (j + i + 2 * k) % NR, (i * NC + k) * NR + j)
            for i in range(NX)
            for k in range(NC)
            for j in range(NR)
        ],
    )
    attn_keep = jnp.where(ic == 0, attn[:, :HALF], attn[:, HALF:])
    attn_give = jnp.where(ic == 0, attn[:, HALF:], attn[:, :HALF])
    attn_other = swap_core(attn_give)

    states = state.astype(f32).reshape(2, SEQ, FEAT)
    square = lax.psum(jnp.sum(states * states, -1), "t") / D
    inv_rms = lax.rsqrt(square + epsilon)
    token_count = lengths.reshape(2).astype(f32)
    valid = (jnp.arange(SEQ, dtype=jnp.int32)[None, :] < lengths.reshape(2)[:, None]).astype(f32)
    pool_weight = valid * inv_rms / token_count[:, None]
    pooled = jnp.sum(pool_weight[..., None] * states, 1)
    attn_pool = jnp.sum(pool_weight[..., None] * attn.astype(f32).reshape(2, SEQ, FEAT), 1)

    near = jnp.concatenate([pooled, norm_gain[None]], 0)
    near = lax.all_to_all(jnp.broadcast_to(near[None], (NT, 3, FEAT)), "t", 0, 0)
    pooled_row = near[:, :2].transpose(1, 0, 2).reshape(2, D)
    gain = near[:, 2].reshape(1, D)

    u_parts = attn_pool.reshape(2, NC, NX * NY, SLICE).transpose(2, 1, 0, 3)
    u_parts = u_parts.reshape(GROUP, 2, SLICE)
    extra = jnp.stack(
        [token_count, jnp.broadcast_to(positive.astype(f32), (2,))], -1
    )
    row = jnp.concatenate([pooled_row, inv_rms], -1)
    send = jnp.concatenate(
        [
            jnp.broadcast_to(row[None], (GROUP, 2, D + SEQ)),
            u_parts,
            jnp.broadcast_to(extra[None], (GROUP, 2, 2)),
            jnp.zeros((GROUP, 2, WIDTH - AT_POS - 1), f32),
        ],
        -1,
    )
    got = lax.all_to_all(send, DP, 0, 0)
    got, state_all, attn_other = lax.optimization_barrier((got, state_all, attn_other))

    other_index = dp_index + 1 - 2 * ic
    state_other = swap_core(state_all)
    got, w_moved = lax.optimization_barrier((got, w_moved))
    w_all = lax.all_gather(w_moved, PLANE).reshape(NX, HALF, COLS)
    scaled, first, gain_part, loss_part, pieces, scale, first_col = group_math(
        jnp.stack([dp_index, other_index]), got.transpose(1, 0, 2), gain
    )

    partial, coef = weight_partials(
        state_all, state_other, attn_keep, attn_other, pieces, scale
    )
    partial, first = lax.optimization_barrier((partial, first))
    spread = lax.all_to_all(partial, PLANE, 0, 0)

    gain_mine = lax.dynamic_index_in_dim(gain_part, it, 0, keepdims=False)
    tail = jnp.concatenate([gain_mine, jnp.broadcast_to(loss_part[:1, :1], (1, FEAT))], 0)
    tails = [tail]
    first_sum = lax.dynamic_index_in_dim(first, ir, 0, keepdims=False)
    for step in range(1, NR):
        outgoing = lax.dynamic_index_in_dim(first, (ir + step) % NR, 0, keepdims=False)
        arrived = lax.ppermute(
            jnp.concatenate([outgoing, tail], 0),
            "r",
            [(j, (j + step) % NR) for j in range(NR)],
        )
        first_sum = first_sum + arrived[:SLICE]
        tails.append(arrived[SLICE:])
    tails = jnp.stack(tails)
    totals = jnp.zeros((2, FEAT), f32)
    for source in range(NR):
        totals = totals + lax.dynamic_index_in_dim(
            tails, (ir - source) % NR, 0, keepdims=False
        )

    spread, first_sum, totals = lax.optimization_barrier((spread, first_sum, totals))
    second = lax.all_to_all(sum_senders(spread), "r", 0, 0)

    row_here = lax.dynamic_slice(scaled, (0, dp_index, it * FEAT), (2, 1, FEAT))
    state_grad = first_col[0].reshape(2, SEQ, 1) * row_here - states * coef[0].reshape(2, SEQ, 1)
    grad_hidden = state_grad.astype(bf16).reshape(1, 2, SEQ, FEAT)
    keep, give = attn_grads(
        (ir + 2 * ic).reshape(1), state_all, state_other, pieces, w_all, coef, first_col
    )

    second, keep, give = lax.optimization_barrier((second, keep, give))
    second_sum = jnp.sum(second.astype(f32), 0)
    total = first_sum - second_sum
    done = jnp.broadcast_to(total.astype(bf16)[None], (NX * NY, SLICE, COLS))
    half = lax.all_to_all(done, PLANE, 0, 0)
    arrived = swap_core(give)
    grad_attn = jnp.where(
        ic == 0, jnp.concatenate([keep, arrived], 1), jnp.concatenate([arrived, keep], 1)
    ).reshape(1, 2, SEQ, FEAT)
    half, grad_attn, grad_hidden, totals = lax.optimization_barrier(
        (half, grad_attn, grad_hidden, totals)
    )
    half_other = swap_core(half)
    grad_weight = join_halves(ic.reshape(1), half, half_other)
    return (grad_hidden, grad_attn, grad_weight, totals[0], totals[1, 0])


def solution(mesh):
    fine = Mesh(mesh.devices.reshape(NX, NY, NC, NT, NR), ("x", "y", "c", "t", "r"))
    pairs = ("x", "y", "c", "r")
    placed = (
        P(pairs, None, None, "t"),
        P(pairs, None, None, "t"),
        P("t", "r"),
        P("t"),
        P(pairs, None),
        P(pairs),
    )
    return jax.shard_map(
        body,
        mesh=fine,
        in_specs=placed,
        out_specs=(
            P(pairs, None, None, "t"),
            P(pairs, None, None, "t"),
            P("t", "r"),
            P("t"),
            P(),
        ),
        check_vma=False,
    )
```

```python
import jax
import jax.numpy as jnp
from jax import lax
from jax.experimental import pallas as pl
from jax.experimental.pallas import tpu as pltpu
from jax.sharding import Mesh, PartitionSpec as P

logit_scale = 20.0
grad_scale = 256.0
epsilon = 1e-06

f32 = jnp.float32
bf16 = jnp.bfloat16

NX, NY, NC, NT, NR = 4, 4, 2, 4, 4
PLANE = ("x", "y")
DP = ("x", "y", "c")

D = 3584
FEAT = D // NT
COLS = D // NR
SEQ = 128
TOK = 2 * SEQ
HALF = FEAT // NC
SLICE = HALF // (NX * NY)
W_ROWS = HALF // NY
PIECES = 16
GROUP = NX * NY * NC

AT_RMS = D
AT_U = D + SEQ
AT_LEN = AT_U + SLICE
AT_POS = AT_LEN + 1
WIDTH = D + 2 * SEQ


def swap_core(value):
    return lax.ppermute(value, "c", [(0, 1), (1, 0)])


contract_last = (((1,), (1,)), ((), ()))
contract_first = (((0,), (0,)), ((), ()))


def dot_last(left, right):
    return lax.dot_general(left, right, contract_last, preferred_element_type=f32)


def dot_exact(left, right, dims):
    return lax.dot_general(
        left, right, dims, precision=lax.Precision.HIGHEST, preferred_element_type=f32
    )


def group_kernel(
    index_ref, got_ref, gain_ref,
    scaled_ref, first_ref, gain_out_ref, loss_ref, pieces_ref, scale_ref, column_ref,
):
    gain = gain_ref[...]
    raw, unit, inv_norm = [], [], []
    for side in range(2):
        raw.append(got_ref[side, :, :D])
        embeds = raw[side] * gain
        square = jnp.sum(embeds * embeds, -1, keepdims=True)
        inv_norm.append(lax.rsqrt(square + epsilon))
        unit.append(embeds * inv_norm[side])
    logits = logit_scale * dot_exact(unit[0], unit[1], contract_last)
    log_total = jnp.log(jnp.sum(jnp.exp(logits), -1, keepdims=True))
    target = got_ref[0, :, AT_POS : AT_POS + 1]
    passage = lax.broadcasted_iota(jnp.int32, (GROUP, GROUP), 1).astype(f32)
    one_hot = jnp.where(passage == target, 1.0, 0.0)
    chosen = jnp.sum(logits * one_hot, -1, keepdims=True)
    loss = jnp.sum(log_total - chosen, 0, keepdims=True)
    loss_ref[...] = jnp.broadcast_to(loss, (8, 128))
    score_grad = grad_scale * (jnp.exp(logits - log_total) - one_hot)
    grads = (
        dot_exact(score_grad, unit[1], (((1,), (0,)), ((), ()))),
        dot_exact(score_grad, unit[0], contract_first),
    )
    gain_sum = jnp.zeros((1, D), f32)
    first = jnp.zeros((SLICE, D), f32)
    for side in range(2):
        grad = logit_scale * grads[side]
        along = jnp.sum(unit[side] * grad, -1, keepdims=True)
        pooled_grad = (grad - unit[side] * along) * inv_norm[side]
        gain_sum = gain_sum + jnp.sum(pooled_grad * raw[side], 0, keepdims=True)
        scaled = pooled_grad * gain
        scaled_ref[side] = scaled
        first = first + dot_exact(got_ref[side, :, AT_U:AT_LEN], scaled, contract_first)
    for block in range(NR):
        columns = slice(block * COLS, (block + 1) * COLS)
        first_ref[block] = first[:, columns]
        gain_out_ref[block] = gain_sum[:, columns]

    token = lax.broadcasted_iota(jnp.int32, (SEQ, SEQ), 0)
    lane = lax.broadcasted_iota(jnp.int32, (SEQ, SEQ), 1)
    position = lax.broadcasted_iota(jnp.int32, (SEQ, 1), 0).astype(f32)
    for pair in range(NC):
        index = index_ref[pair]
        chosen_row = lax.broadcasted_iota(jnp.int32, (GROUP, 1), 0) == index
        parts = []
        for side in range(2):
            row = jnp.sum(jnp.where(chosen_row, scaled_ref[side], 0.0), 0, keepdims=True)
            high = row.astype(bf16).astype(f32)
            mid = (row - high).astype(bf16).astype(f32)
            parts += [high, mid, row - high - mid]
            rest = jnp.where(chosen_row, got_ref[side, :, AT_RMS:WIDTH], 0.0)
            rest = jnp.sum(rest, 0, keepdims=True)
            rms_row = rest[:, :SEQ]
            count = rest[:, AT_LEN - AT_RMS : AT_LEN - AT_RMS + 1]
            rms = jnp.sum(jnp.where(token == lane, rms_row, 0.0), -1, keepdims=True)
            column = jnp.where(position < count, rms / count, 0.0)
            here = slice(side * SEQ, (side + 1) * SEQ)
            column_ref[pair, here, :] = column
            scale_ref[pair, here, :] = column * rms * rms * (1.0 / D)
        parts.append(jnp.zeros((PIECES - 6, D), f32))
        piece = jnp.concatenate(parts, 0).astype(bf16)
        for block in range(NR):
            pieces_ref[pair, block] = piece[:, block * COLS : (block + 1) * COLS]


def group_math(index, got, gain):
    spec = pl.BlockSpec(memory_space=pltpu.VMEM)
    return pl.pallas_call(
        group_kernel,
        out_shape=(
            jax.ShapeDtypeStruct((2, GROUP, D), f32),
            jax.ShapeDtypeStruct((NR, SLICE, COLS), f32),
            jax.ShapeDtypeStruct((NR, 1, COLS), f32),
            jax.ShapeDtypeStruct((8, 128), f32),
            jax.ShapeDtypeStruct((NC, NR, PIECES, COLS), bf16),
            jax.ShapeDtypeStruct((NC, TOK, 1), f32),
            jax.ShapeDtypeStruct((NC, TOK, 1), f32),
        ),
        in_specs=[pl.BlockSpec(memory_space=pltpu.SMEM), spec, spec],
        out_specs=(spec,) * 7,
        compiler_params=pltpu.CompilerParams(vmem_limit_bytes=16 * 1024 * 1024),
        cost_estimate=pl.CostEstimate(
            flops=50 * GROUP * GROUP * D, bytes_accessed=3 * 1024 * 1024, transcendentals=4096
        ),
        name="group_math",
    )(index, got, gain)


def weight_kernel(index_ref, *refs):
    states, (keep_ref, given_ref, pieces_ref, scale_ref) = refs[: 2 * NT], refs[2 * NT : 2 * NT + 4]
    out_ref, coef_ref, acc_ref = refs[2 * NT + 4 :]
    blocks = [lax.rem(index_ref[0] + NT - step, NT) for step in range(NT)]
    token = lax.broadcasted_iota(jnp.int32, (TOK, PIECES), 0)
    part = lax.broadcasted_iota(jnp.int32, (TOK, PIECES), 1)
    part = part - jnp.where(token < SEQ, 0, 3)
    mask = (part >= 0) & (part < 3)
    scaled = []
    for pair, attn_ref in enumerate((keep_ref, given_ref)):
        inner = jnp.zeros((TOK, PIECES), f32)
        for step in range(NT):
            inner = inner + dot_last(
                states[pair * NT + step][...], pieces_ref[pair, blocks[step]]
            )
        inner = jnp.sum(jnp.where(mask, inner, 0.0), -1, keepdims=True)
        coef = scale_ref[pair] * inner
        coef_ref[pair] = coef
        scaled.append((attn_ref[...].astype(f32) * coef).astype(bf16))
    for step in range(NT):
        acc_ref[blocks[step]] = lax.dot_general(
            scaled[0], states[step][...], contract_first, preferred_element_type=f32
        ) + lax.dot_general(
            scaled[1], states[NT + step][...], contract_first, preferred_element_type=f32
        )
    for place in range(NX * NY):
        rows = [
            acc_ref[block, place * SLICE : (place + 1) * SLICE, :] for block in range(NR)
        ]
        out_ref[place] = jnp.concatenate(rows, 0).astype(bf16)


def weight_partials(index, states, keep, given, pieces, scale):
    spec = pl.BlockSpec(memory_space=pltpu.VMEM)
    return pl.pallas_call(
        weight_kernel,
        out_shape=(
            jax.ShapeDtypeStruct((NX * NY, NR * SLICE, COLS), bf16),
            jax.ShapeDtypeStruct((NC, TOK, 1), f32),
        ),
        in_specs=[pl.BlockSpec(memory_space=pltpu.SMEM)] + [spec] * (2 * NT + 4),
        out_specs=(spec, spec),
        scratch_shapes=[pltpu.VMEM((NR, HALF, COLS), f32)],
        compiler_params=pltpu.CompilerParams(vmem_limit_bytes=24 * 1024 * 1024),
        cost_estimate=pl.CostEstimate(
            flops=4 * TOK * HALF * D, bytes_accessed=8 * 1024 * 1024, transcendentals=0
        ),
        name="weight_partials",
    )(index, *states, keep, given, pieces, scale)


def sum_kernel(spread_ref, out_ref, acc_ref):
    step = pl.program_id(0)
    part = spread_ref[0].astype(f32)
    for place in range(1, spread_ref.shape[0]):
        part = part + spread_ref[place].astype(f32)

    @pl.when(step == 0)
    def _():
        acc_ref[...] = part

    @pl.when(step > 0)
    def _():
        acc_ref[...] += part

    @pl.when(step == NX - 1)
    def _():
        for block in range(NR):
            out_ref[block] = acc_ref[block * SLICE : (block + 1) * SLICE, :].astype(bf16)


def sum_senders(spread):
    return pl.pallas_call(
        sum_kernel,
        grid=(NX,),
        out_shape=jax.ShapeDtypeStruct((NR, SLICE, COLS), bf16),
        in_specs=[pl.BlockSpec((NY, NR * SLICE, COLS), lambda step: (step, 0, 0))],
        out_specs=pl.BlockSpec((NR, SLICE, COLS), lambda step: (0, 0, 0)),
        scratch_shapes=[pltpu.VMEM((NR * SLICE, COLS), f32)],
        compiler_params=pltpu.CompilerParams(vmem_limit_bytes=16 * 1024 * 1024),
        cost_estimate=pl.CostEstimate(
            flops=NX * NY * NR * SLICE * COLS, bytes_accessed=4 * 1024 * 1024, transcendentals=0
        ),
        name="sum_senders",
    )(spread)


def join_kernel(core_ref, mine_ref, other_ref, out_ref):
    core = core_ref[0]
    for which, ref in ((core, mine_ref), (1 - core, other_ref)):
        rows = [ref[place].astype(f32) for place in range(NX * NY)]
        out_ref[pl.ds(pl.multiple_of(which * HALF, HALF), HALF), :] = jnp.concatenate(
            rows, 0
        ).astype(bf16)


def join_halves(core, mine, other):
    spec = pl.BlockSpec(memory_space=pltpu.VMEM)
    return pl.pallas_call(
        join_kernel,
        out_shape=jax.ShapeDtypeStruct((FEAT, COLS), bf16),
        in_specs=[pl.BlockSpec(memory_space=pltpu.SMEM), spec, spec],
        out_specs=spec,
        compiler_params=pltpu.CompilerParams(vmem_limit_bytes=16 * 1024 * 1024),
        cost_estimate=pl.CostEstimate(
            flops=0, bytes_accessed=4 * 1024 * 1024, transcendentals=0
        ),
        name="join_halves",
    )(core, mine, other)


def attn_kernel(index_ref, *refs):
    states, (pieces_ref, w_ref, coef_ref, first_ref) = refs[: 2 * NT], refs[2 * NT : 2 * NT + 4]
    blocks = [lax.rem(index_ref[0] + NT - step, NT) for step in range(NT)]
    places = [lax.rem(blocks[step] + 2 * NR - index_ref[1], NR) for step in range(NT)]
    for pair, out_ref in enumerate(refs[2 * NT + 4 :]):
        tokens = jnp.zeros((TOK, HALF), f32)
        rows = jnp.zeros((PIECES, HALF), f32)
        for step in range(NT):
            weight = w_ref[places[step]]
            tokens = tokens + dot_last(states[pair * NT + step][...], weight)
            rows = rows + dot_last(pieces_ref[pair, blocks[step]], weight)
        for side in range(2):
            row = rows[3 * side + 2 : 3 * side + 3] + rows[3 * side + 1 : 3 * side + 2]
            row = row + rows[3 * side : 3 * side + 1]
            here = slice(side * SEQ, (side + 1) * SEQ)
            out_ref[here, :] = (
                first_ref[pair, here, :] * row - coef_ref[pair, here, :] * tokens[here]
            ).astype(bf16)


def attn_grads(index, states, pieces, w_all, coef, first):
    spec = pl.BlockSpec(memory_space=pltpu.VMEM)
    out = jax.ShapeDtypeStruct((TOK, HALF), bf16)
    return pl.pallas_call(
        attn_kernel,
        out_shape=(out, out),
        in_specs=[pl.BlockSpec(memory_space=pltpu.SMEM)] + [spec] * (2 * NT + 4),
        out_specs=(spec, spec),
        compiler_params=pltpu.CompilerParams(vmem_limit_bytes=24 * 1024 * 1024),
        cost_estimate=pl.CostEstimate(
            flops=4 * TOK * HALF * D, bytes_accessed=8 * 1024 * 1024, transcendentals=0
        ),
        name="attn_grads",
    )(index, *states, pieces, w_all, coef, first)


def body(hidden_state, attn_out, o_weight, norm_gain, lengths, positive):
    ix, iy, ic = lax.axis_index("x"), lax.axis_index("y"), lax.axis_index("c")
    it, ir = lax.axis_index("t"), lax.axis_index("r")
    dp_index = (ix * NY + iy) * NC + ic

    state = hidden_state.reshape(TOK, FEAT)
    attn = attn_out.reshape(TOK, FEAT)
    w_start = (ic * NY + iy) * W_ROWS
    w_mine = lax.dynamic_slice(o_weight, (w_start, 0), (W_ROWS, COLS))
    w_moved = lax.ppermute(
        w_mine,
        ("x", "c", "r"),
        [
            ((i * NC + k) * NR + (j + i + 2 * k) % NR, (i * NC + k) * NR + j)
            for i in range(NX)
            for k in range(NC)
            for j in range(NR)
        ],
    )
    attn_keep = jnp.where(ic == 0, attn[:, :HALF], attn[:, HALF:])
    attn_give = jnp.where(ic == 0, attn[:, HALF:], attn[:, :HALF])
    attn_other = swap_core(attn_give)

    states = state.astype(f32).reshape(2, SEQ, FEAT)
    square = lax.psum(jnp.sum(states * states, -1), "t") / D
    inv_rms = lax.rsqrt(square + epsilon)
    token_count = lengths.reshape(2).astype(f32)
    valid = (jnp.arange(SEQ, dtype=jnp.int32)[None, :] < lengths.reshape(2)[:, None]).astype(f32)
    pool_weight = valid * inv_rms / token_count[:, None]
    pooled = jnp.sum(pool_weight[..., None] * states, 1)
    attn_pool = jnp.sum(pool_weight[..., None] * attn.astype(f32).reshape(2, SEQ, FEAT), 1)

    near = jnp.concatenate([pooled, norm_gain[None]], 0)
    near, w_moved = lax.optimization_barrier((near, w_moved))
    w_all = lax.all_gather(w_moved, PLANE).reshape(NX, HALF, COLS)
    near = lax.all_to_all(jnp.broadcast_to(near[None], (NT, 3, FEAT)), "t", 0, 0)
    near, later = lax.optimization_barrier((near, state))
    own = [state]
    for step in range(1, NT):
        own.append(lax.ppermute(later, "t", [(j, (j + step) % NT) for j in range(NT)]))
    pooled_row = near[:, :2].transpose(1, 0, 2).reshape(2, D)
    gain = near[:, 2].reshape(1, D)

    u_parts = attn_pool.reshape(2, NC, NX * NY, SLICE).transpose(2, 1, 0, 3)
    u_parts = u_parts.reshape(GROUP, 2, SLICE)
    extra = jnp.stack(
        [token_count, jnp.broadcast_to(positive.astype(f32), (2,))], -1
    )
    row = jnp.concatenate([pooled_row, inv_rms], -1)
    send = jnp.concatenate(
        [
            jnp.broadcast_to(row[None], (GROUP, 2, D + SEQ)),
            u_parts,
            jnp.broadcast_to(extra[None], (GROUP, 2, 2)),
            jnp.zeros((GROUP, 2, WIDTH - AT_POS - 1), f32),
        ],
        -1,
    )
    got = lax.all_to_all(send, DP, 0, 0)
    got, attn_other = lax.optimization_barrier((got, attn_other))

    other_index = dp_index + 1 - 2 * ic
    scaled, first, gain_part, loss_part, pieces, scale, first_col = group_math(
        jnp.stack([dp_index, other_index]), got.transpose(1, 0, 2), gain
    )

    for step in range(NT - 1, 0, -1):
        scale, own[step] = lax.optimization_barrier((scale, own[step]))
    other = [swap_core(block) for block in own]
    partial, coef = weight_partials(
        it.reshape(1), own + other, attn_keep, attn_other, pieces, scale
    )
    partial, first = lax.optimization_barrier((partial, first))
    spread = lax.all_to_all(partial, PLANE, 0, 0)

    gain_mine = lax.dynamic_index_in_dim(gain_part, it, 0, keepdims=False)
    tail = jnp.concatenate([gain_mine, jnp.broadcast_to(loss_part[:1, :1], (1, FEAT))], 0)
    tails = [tail]
    first_sum = lax.dynamic_index_in_dim(first, ir, 0, keepdims=False)
    for step in range(1, NR):
        outgoing = lax.dynamic_index_in_dim(first, (ir + step) % NR, 0, keepdims=False)
        arrived = lax.ppermute(
            jnp.concatenate([outgoing, tail], 0),
            "r",
            [(j, (j + step) % NR) for j in range(NR)],
        )
        first_sum = first_sum + arrived[:SLICE]
        tails.append(arrived[SLICE:])
    tails = jnp.stack(tails)
    totals = jnp.zeros((2, FEAT), f32)
    for source in range(NR):
        totals = totals + lax.dynamic_index_in_dim(
            tails, (ir - source) % NR, 0, keepdims=False
        )

    row_here = lax.dynamic_slice(scaled, (0, dp_index, it * FEAT), (2, 1, FEAT))
    state_grad = first_col[0].reshape(2, SEQ, 1) * row_here - states * coef[0].reshape(2, SEQ, 1)
    grad_hidden = state_grad.astype(bf16).reshape(1, 2, SEQ, FEAT)
    keep, give = attn_grads(
        jnp.stack([it, ir + 2 * ic]), own + other, pieces, w_all, coef, first_col
    )
    arrived = swap_core(give)
    grad_attn = jnp.where(
        ic == 0, jnp.concatenate([keep, arrived], 1), jnp.concatenate([arrived, keep], 1)
    ).reshape(1, 2, SEQ, FEAT)
    spread, first_sum, totals, grad_attn, grad_hidden = lax.optimization_barrier(
        (spread, first_sum, totals, grad_attn, grad_hidden)
    )
    second = lax.all_to_all(sum_senders(spread), "r", 0, 0)

    second_sum = jnp.sum(second.astype(f32), 0)
    total = first_sum - second_sum
    done = jnp.broadcast_to(total.astype(bf16)[None], (NX * NY, SLICE, COLS))
    half = lax.all_to_all(done, PLANE, 0, 0)
    half_other = swap_core(half)
    grad_weight = join_halves(ic.reshape(1), half, half_other)
    return (grad_hidden, grad_attn, grad_weight, totals[0], totals[1, 0])


def solution(mesh):
    fine = Mesh(mesh.devices.reshape(NX, NY, NC, NT, NR), ("x", "y", "c", "t", "r"))
    pairs = ("x", "y", "c", "r")
    placed = (
        P(pairs, None, None, "t"),
        P(pairs, None, None, "t"),
        P("t", "r"),
        P("t"),
        P(pairs, None),
        P(pairs),
    )
    return jax.shard_map(
        body,
        mesh=fine,
        in_specs=placed,
        out_specs=(
            P(pairs, None, None, "t"),
            P(pairs, None, None, "t"),
            P("t", "r"),
            P("t"),
            P(),
        ),
        check_vma=False,
    )
```

```python
import jax
import jax.numpy as jnp
from jax import lax
from jax.experimental import pallas as pl
from jax.experimental.pallas import tpu as pltpu
from jax.sharding import Mesh, PartitionSpec as P

logit_scale = 20.0
grad_scale = 256.0
epsilon = 1e-06

f32 = jnp.float32
bf16 = jnp.bfloat16

NX, NY, NC, NT, NR = 4, 4, 2, 4, 4
PLANE = ("x", "y")
DP = ("x", "y", "c")

D = 3584
FEAT = D // NT
COLS = D // NR
SEQ = 128
TOK = 2 * SEQ
HALF = FEAT // NC
SLICE = HALF // (NX * NY)
W_ROWS = HALF // NY
PIECES = 16
GROUP = NX * NY * NC

AT_RMS = D
AT_U = D + SEQ
AT_LEN = AT_U + SLICE
AT_POS = AT_LEN + 1
WIDTH = D + 2 * SEQ


def swap_core(value):
    return lax.ppermute(value, "c", [(0, 1), (1, 0)])


contract_last = (((1,), (1,)), ((), ()))
contract_first = (((0,), (0,)), ((), ()))


def dot_last(left, right):
    return lax.dot_general(left, right, contract_last, preferred_element_type=f32)


def dot_exact(left, right, dims):
    return lax.dot_general(
        left, right, dims, precision=lax.Precision.HIGHEST, preferred_element_type=f32
    )


def group_kernel(
    index_ref, got_ref, gain_ref,
    scaled_ref, first_ref, gain_out_ref, loss_ref, pieces_ref, scale_ref, column_ref,
):
    gain = gain_ref[...]
    raw, unit, inv_norm = [], [], []
    for side in range(2):
        raw.append(got_ref[side, :, :D])
        embeds = raw[side] * gain
        square = jnp.sum(embeds * embeds, -1, keepdims=True)
        inv_norm.append(lax.rsqrt(square + epsilon))
        unit.append(embeds * inv_norm[side])
    logits = logit_scale * dot_exact(unit[0], unit[1], contract_last)
    log_total = jnp.log(jnp.sum(jnp.exp(logits), -1, keepdims=True))
    target = got_ref[0, :, AT_POS : AT_POS + 1]
    passage = lax.broadcasted_iota(jnp.int32, (GROUP, GROUP), 1).astype(f32)
    one_hot = jnp.where(passage == target, 1.0, 0.0)
    chosen = jnp.sum(logits * one_hot, -1, keepdims=True)
    loss = jnp.sum(log_total - chosen, 0, keepdims=True)
    loss_ref[...] = jnp.broadcast_to(loss, (8, 128))
    score_grad = grad_scale * (jnp.exp(logits - log_total) - one_hot)
    grads = (
        dot_exact(score_grad, unit[1], (((1,), (0,)), ((), ()))),
        dot_exact(score_grad, unit[0], contract_first),
    )
    gain_sum = jnp.zeros((1, D), f32)
    first = jnp.zeros((SLICE, D), f32)
    for side in range(2):
        grad = logit_scale * grads[side]
        along = jnp.sum(unit[side] * grad, -1, keepdims=True)
        pooled_grad = (grad - unit[side] * along) * inv_norm[side]
        gain_sum = gain_sum + jnp.sum(pooled_grad * raw[side], 0, keepdims=True)
        scaled = pooled_grad * gain
        scaled_ref[side] = scaled
        first = first + dot_exact(got_ref[side, :, AT_U:AT_LEN], scaled, contract_first)
    for block in range(NR):
        columns = slice(block * COLS, (block + 1) * COLS)
        first_ref[block] = first[:, columns]
        gain_out_ref[block] = gain_sum[:, columns]

    token = lax.broadcasted_iota(jnp.int32, (SEQ, SEQ), 0)
    lane = lax.broadcasted_iota(jnp.int32, (SEQ, SEQ), 1)
    position = lax.broadcasted_iota(jnp.int32, (SEQ, 1), 0).astype(f32)
    for pair in range(NC):
        index = index_ref[pair]
        chosen_row = lax.broadcasted_iota(jnp.int32, (GROUP, 1), 0) == index
        parts = []
        for side in range(2):
            row = jnp.sum(jnp.where(chosen_row, scaled_ref[side], 0.0), 0, keepdims=True)
            high = row.astype(bf16).astype(f32)
            mid = (row - high).astype(bf16).astype(f32)
            parts += [high, mid, row - high - mid]
            rest = jnp.where(chosen_row, got_ref[side, :, AT_RMS:WIDTH], 0.0)
            rest = jnp.sum(rest, 0, keepdims=True)
            rms_row = rest[:, :SEQ]
            count = rest[:, AT_LEN - AT_RMS : AT_LEN - AT_RMS + 1]
            rms = jnp.sum(jnp.where(token == lane, rms_row, 0.0), -1, keepdims=True)
            column = jnp.where(position < count, rms / count, 0.0)
            here = slice(side * SEQ, (side + 1) * SEQ)
            column_ref[pair, here, :] = column
            scale_ref[pair, here, :] = column * rms * rms * (1.0 / D)
        parts.append(jnp.zeros((PIECES - 6, D), f32))
        piece = jnp.concatenate(parts, 0).astype(bf16)
        for block in range(NR):
            pieces_ref[pair, block] = piece[:, block * COLS : (block + 1) * COLS]


def group_math(index, got, gain):
    spec = pl.BlockSpec(memory_space=pltpu.VMEM)
    return pl.pallas_call(
        group_kernel,
        out_shape=(
            jax.ShapeDtypeStruct((2, GROUP, D), f32),
            jax.ShapeDtypeStruct((NR, SLICE, COLS), f32),
            jax.ShapeDtypeStruct((NR, 1, COLS), f32),
            jax.ShapeDtypeStruct((8, 128), f32),
            jax.ShapeDtypeStruct((NC, NR, PIECES, COLS), bf16),
            jax.ShapeDtypeStruct((NC, TOK, 1), f32),
            jax.ShapeDtypeStruct((NC, TOK, 1), f32),
        ),
        in_specs=[pl.BlockSpec(memory_space=pltpu.SMEM), spec, spec],
        out_specs=(spec,) * 7,
        compiler_params=pltpu.CompilerParams(vmem_limit_bytes=16 * 1024 * 1024),
        cost_estimate=pl.CostEstimate(
            flops=50 * GROUP * GROUP * D, bytes_accessed=3 * 1024 * 1024, transcendentals=4096
        ),
        name="group_math",
    )(index, got, gain)


def weight_kernel(
    core_ref, state_ref, keep_ref, given_ref, pieces_ref, scale_ref, out_ref, coef_ref, acc_ref
):
    bases = (NT * core_ref[0], NT * (1 - core_ref[0]))
    token = lax.broadcasted_iota(jnp.int32, (TOK, PIECES), 0)
    part = lax.broadcasted_iota(jnp.int32, (TOK, PIECES), 1)
    part = part - jnp.where(token < SEQ, 0, 3)
    mask = (part >= 0) & (part < 3)
    scaled = []
    for pair, attn_ref in enumerate((keep_ref, given_ref)):
        inner = jnp.zeros((TOK, PIECES), f32)
        for block in range(NT):
            inner = inner + dot_last(state_ref[bases[pair] + block], pieces_ref[pair, block])
        inner = jnp.sum(jnp.where(mask, inner, 0.0), -1, keepdims=True)
        coef = scale_ref[pair] * inner
        coef_ref[pair] = coef
        scaled.append((attn_ref[...].astype(f32) * coef).astype(bf16))
    for block in range(NT):
        acc_ref[block] = lax.dot_general(
            scaled[0], state_ref[bases[0] + block], contract_first, preferred_element_type=f32
        ) + lax.dot_general(
            scaled[1], state_ref[bases[1] + block], contract_first, preferred_element_type=f32
        )
    for place in range(NX * NY):
        rows = [
            acc_ref[block, place * SLICE : (place + 1) * SLICE, :] for block in range(NR)
        ]
        out_ref[place] = jnp.concatenate(rows, 0).astype(bf16)


def weight_partials(core, states, keep, given, pieces, scale):
    spec = pl.BlockSpec(memory_space=pltpu.VMEM)
    return pl.pallas_call(
        weight_kernel,
        out_shape=(
            jax.ShapeDtypeStruct((NX * NY, NR * SLICE, COLS), bf16),
            jax.ShapeDtypeStruct((NC, TOK, 1), f32),
        ),
        in_specs=[pl.BlockSpec(memory_space=pltpu.SMEM)] + [spec] * 5,
        out_specs=(spec, spec),
        scratch_shapes=[pltpu.VMEM((NR, HALF, COLS), f32)],
        compiler_params=pltpu.CompilerParams(vmem_limit_bytes=24 * 1024 * 1024),
        cost_estimate=pl.CostEstimate(
            flops=4 * TOK * HALF * D, bytes_accessed=8 * 1024 * 1024, transcendentals=0
        ),
        name="weight_partials",
    )(core, states, keep, given, pieces, scale)


def sum_kernel(spread_ref, out_ref, acc_ref):
    step = pl.program_id(0)
    part = spread_ref[0].astype(f32)
    for place in range(1, spread_ref.shape[0]):
        part = part + spread_ref[place].astype(f32)

    @pl.when(step == 0)
    def _():
        acc_ref[...] = part

    @pl.when(step > 0)
    def _():
        acc_ref[...] += part

    @pl.when(step == NX - 1)
    def _():
        for block in range(NR):
            out_ref[block] = acc_ref[block * SLICE : (block + 1) * SLICE, :].astype(bf16)


def sum_senders(spread):
    return pl.pallas_call(
        sum_kernel,
        grid=(NX,),
        out_shape=jax.ShapeDtypeStruct((NR, SLICE, COLS), bf16),
        in_specs=[pl.BlockSpec((NY, NR * SLICE, COLS), lambda step: (step, 0, 0))],
        out_specs=pl.BlockSpec((NR, SLICE, COLS), lambda step: (0, 0, 0)),
        scratch_shapes=[pltpu.VMEM((NR * SLICE, COLS), f32)],
        compiler_params=pltpu.CompilerParams(vmem_limit_bytes=16 * 1024 * 1024),
        cost_estimate=pl.CostEstimate(
            flops=NX * NY * NR * SLICE * COLS, bytes_accessed=4 * 1024 * 1024, transcendentals=0
        ),
        name="sum_senders",
    )(spread)


def join_kernel(core_ref, mine_ref, other_ref, out_ref):
    core = core_ref[0]
    for which, ref in ((core, mine_ref), (1 - core, other_ref)):
        rows = [ref[place].astype(f32) for place in range(NX * NY)]
        out_ref[pl.ds(pl.multiple_of(which * HALF, HALF), HALF), :] = jnp.concatenate(
            rows, 0
        ).astype(bf16)


def join_halves(core, mine, other):
    spec = pl.BlockSpec(memory_space=pltpu.VMEM)
    return pl.pallas_call(
        join_kernel,
        out_shape=jax.ShapeDtypeStruct((FEAT, COLS), bf16),
        in_specs=[pl.BlockSpec(memory_space=pltpu.SMEM), spec, spec],
        out_specs=spec,
        compiler_params=pltpu.CompilerParams(vmem_limit_bytes=16 * 1024 * 1024),
        cost_estimate=pl.CostEstimate(
            flops=0, bytes_accessed=4 * 1024 * 1024, transcendentals=0
        ),
        name="join_halves",
    )(core, mine, other)


def attn_kernel(
    index_ref, state_ref, pieces_ref, w_ref, coef_ref, first_ref, keep_ref, give_ref
):
    core, shift = index_ref[0], index_ref[1]
    bases = (NT * core, NT * (1 - core))
    for pair, out_ref in enumerate((keep_ref, give_ref)):
        tokens = jnp.zeros((TOK, HALF), f32)
        rows = jnp.zeros((PIECES, HALF), f32)
        for block in range(NX):
            which = lax.rem(shift + block, NR)
            tokens = tokens + dot_last(state_ref[bases[pair] + which], w_ref[block])
            rows = rows + dot_last(pieces_ref[pair, which], w_ref[block])
        for side in range(2):
            row = rows[3 * side + 2 : 3 * side + 3] + rows[3 * side + 1 : 3 * side + 2]
            row = row + rows[3 * side : 3 * side + 1]
            here = slice(side * SEQ, (side + 1) * SEQ)
            out_ref[here, :] = (
                first_ref[pair, here, :] * row - coef_ref[pair, here, :] * tokens[here]
            ).astype(bf16)


def attn_grads(index, states, pieces, w_all, coef, first):
    spec = pl.BlockSpec(memory_space=pltpu.VMEM)
    out = jax.ShapeDtypeStruct((TOK, HALF), bf16)
    return pl.pallas_call(
        attn_kernel,
        out_shape=(out, out),
        in_specs=[pl.BlockSpec(memory_space=pltpu.SMEM)] + [spec] * 5,
        out_specs=(spec, spec),
        compiler_params=pltpu.CompilerParams(vmem_limit_bytes=24 * 1024 * 1024),
        cost_estimate=pl.CostEstimate(
            flops=4 * TOK * HALF * D, bytes_accessed=8 * 1024 * 1024, transcendentals=0
        ),
        name="attn_grads",
    )(index, states, pieces, w_all, coef, first)


def body(hidden_state, attn_out, o_weight, norm_gain, lengths, positive):
    ix, iy, ic = lax.axis_index("x"), lax.axis_index("y"), lax.axis_index("c")
    it, ir = lax.axis_index("t"), lax.axis_index("r")
    dp_index = (ix * NY + iy) * NC + ic

    state = hidden_state.reshape(TOK, FEAT)
    attn = attn_out.reshape(TOK, FEAT)
    state_all = lax.all_gather(state, ("c", "t"))
    w_start = (ic * NY + iy) * W_ROWS
    w_mine = lax.dynamic_slice(o_weight, (w_start, 0), (W_ROWS, COLS))
    w_moved = lax.ppermute(
        w_mine,
        ("x", "c", "r"),
        [
            ((i * NC + k) * NR + (j + i + 2 * k) % NR, (i * NC + k) * NR + j)
            for i in range(NX)
            for k in range(NC)
            for j in range(NR)
        ],
    )
    attn_keep = jnp.where(ic == 0, attn[:, :HALF], attn[:, HALF:])
    attn_give = jnp.where(ic == 0, attn[:, HALF:], attn[:, :HALF])
    attn_other = swap_core(attn_give)

    states = state.astype(f32).reshape(2, SEQ, FEAT)
    square = lax.psum(jnp.sum(states * states, -1), "t") / D
    inv_rms = lax.rsqrt(square + epsilon)
    token_count = lengths.reshape(2).astype(f32)
    valid = (jnp.arange(SEQ, dtype=jnp.int32)[None, :] < lengths.reshape(2)[:, None]).astype(f32)
    pool_weight = valid * inv_rms / token_count[:, None]
    pooled = jnp.sum(pool_weight[..., None] * states, 1)
    attn_pool = jnp.sum(pool_weight[..., None] * attn.astype(f32).reshape(2, SEQ, FEAT), 1)

    near = jnp.concatenate([pooled, norm_gain[None]], 0)
    near = lax.all_to_all(jnp.broadcast_to(near[None], (NT, 3, FEAT)), "t", 0, 0)
    pooled_row = near[:, :2].transpose(1, 0, 2).reshape(2, D)
    gain = near[:, 2].reshape(1, D)

    u_parts = attn_pool.reshape(2, NC, NX * NY, SLICE).transpose(2, 1, 0, 3)
    u_parts = u_parts.reshape(GROUP, 2, SLICE)
    extra = jnp.stack(
        [token_count, jnp.broadcast_to(positive.astype(f32), (2,))], -1
    )
    row = jnp.concatenate([pooled_row, inv_rms], -1)
    send = jnp.concatenate(
        [
            jnp.broadcast_to(row[None], (GROUP, 2, D + SEQ)),
            u_parts,
            jnp.broadcast_to(extra[None], (GROUP, 2, 2)),
            jnp.zeros((GROUP, 2, WIDTH - AT_POS - 1), f32),
        ],
        -1,
    )
    got = lax.all_to_all(send, DP, 0, 0)
    got, attn_other = lax.optimization_barrier((got, attn_other))

    other_index = dp_index + 1 - 2 * ic
    scaled, first, gain_part, loss_part, pieces, scale, first_col = group_math(
        jnp.stack([dp_index, other_index]), got.transpose(1, 0, 2), gain
    )

    scale, w_moved = lax.optimization_barrier((scale, w_moved))
    w_all = lax.all_gather(w_moved, PLANE).reshape(NX, HALF, COLS)
    partial, coef = weight_partials(
        ic.reshape(1), state_all, attn_keep, attn_other, pieces, scale
    )
    partial, first = lax.optimization_barrier((partial, first))
    spread = lax.all_to_all(partial, PLANE, 0, 0)

    gain_mine = lax.dynamic_index_in_dim(gain_part, it, 0, keepdims=False)
    tail = jnp.concatenate([gain_mine, jnp.broadcast_to(loss_part[:1, :1], (1, FEAT))], 0)
    tails = [tail]
    first_sum = lax.dynamic_index_in_dim(first, ir, 0, keepdims=False)
    for step in range(1, NR):
        outgoing = lax.dynamic_index_in_dim(first, (ir + step) % NR, 0, keepdims=False)
        arrived = lax.ppermute(
            jnp.concatenate([outgoing, tail], 0),
            "r",
            [(j, (j + step) % NR) for j in range(NR)],
        )
        first_sum = first_sum + arrived[:SLICE]
        tails.append(arrived[SLICE:])
    tails = jnp.stack(tails)
    totals = jnp.zeros((2, FEAT), f32)
    for source in range(NR):
        totals = totals + lax.dynamic_index_in_dim(
            tails, (ir - source) % NR, 0, keepdims=False
        )

    spread, first_sum, totals = lax.optimization_barrier((spread, first_sum, totals))
    second = lax.all_to_all(sum_senders(spread), "r", 0, 0)

    row_here = lax.dynamic_slice(scaled, (0, dp_index, it * FEAT), (2, 1, FEAT))
    state_grad = first_col[0].reshape(2, SEQ, 1) * row_here - states * coef[0].reshape(2, SEQ, 1)
    grad_hidden = state_grad.astype(bf16).reshape(1, 2, SEQ, FEAT)
    keep, give = attn_grads(
        jnp.stack([ic, ir + 2 * ic]), state_all, pieces, w_all, coef, first_col
    )

    second_sum = jnp.sum(second.astype(f32), 0)
    total = first_sum - second_sum
    done = jnp.broadcast_to(total.astype(bf16)[None], (NX * NY, SLICE, COLS))
    half = lax.all_to_all(done, PLANE, 0, 0)
    half, keep, give, grad_hidden, totals = lax.optimization_barrier(
        (half, keep, give, grad_hidden, totals)
    )
    half_other = swap_core(half)
    arrived = swap_core(give)
    grad_attn = jnp.where(
        ic == 0, jnp.concatenate([keep, arrived], 1), jnp.concatenate([arrived, keep], 1)
    ).reshape(1, 2, SEQ, FEAT)
    grad_weight = join_halves(ic.reshape(1), half, half_other)
    return (grad_hidden, grad_attn, grad_weight, totals[0], totals[1, 0])


def solution(mesh):
    fine = Mesh(mesh.devices.reshape(NX, NY, NC, NT, NR), ("x", "y", "c", "t", "r"))
    pairs = ("x", "y", "c", "r")
    placed = (
        P(pairs, None, None, "t"),
        P(pairs, None, None, "t"),
        P("t", "r"),
        P("t"),
        P(pairs, None),
        P(pairs),
    )
    return jax.shard_map(
        body,
        mesh=fine,
        in_specs=placed,
        out_specs=(
            P(pairs, None, None, "t"),
            P(pairs, None, None, "t"),
            P("t", "r"),
            P("t"),
            P(),
        ),
        check_vma=False,
    )
```

```python
import jax
import jax.numpy as jnp
from jax import lax
from jax.experimental import pallas as pl
from jax.experimental.pallas import tpu as pltpu
from jax.sharding import Mesh, PartitionSpec as P

logit_scale = 20.0
grad_scale = 256.0
epsilon = 1e-06

f32 = jnp.float32
bf16 = jnp.bfloat16

NX, NY, NC, NT, NR = 4, 4, 2, 4, 4
PLANE = ("x", "y")
DP = ("x", "y", "c")

D = 3584
FEAT = D // NT
COLS = D // NR
SEQ = 128
TOK = 2 * SEQ
HALF = FEAT // NC
SLICE = HALF // (NX * NY)
W_ROWS = HALF // NY
PIECES = 16
GROUP = NX * NY * NC

AT_RMS = D
AT_U = D + SEQ
AT_LEN = AT_U + SLICE
AT_POS = AT_LEN + 1
WIDTH = D + 2 * SEQ


def swap_core(value):
    return lax.ppermute(value, "c", [(0, 1), (1, 0)])


contract_last = (((1,), (1,)), ((), ()))
contract_first = (((0,), (0,)), ((), ()))


def dot_last(left, right):
    return lax.dot_general(left, right, contract_last, preferred_element_type=f32)


def dot_exact(left, right, dims):
    return lax.dot_general(
        left, right, dims, precision=lax.Precision.HIGHEST, preferred_element_type=f32
    )


def group_kernel(
    index_ref, got_ref, gain_ref,
    first_ref, gain_out_ref, loss_ref, pieces_ref, scale_ref, column_ref, scaled_ref,
):
    gain = gain_ref[...]
    raw, unit, inv_norm = [], [], []
    for side in range(2):
        raw.append(got_ref[side, :, :D])
        embeds = raw[side] * gain
        square = jnp.sum(embeds * embeds, -1, keepdims=True)
        inv_norm.append(lax.rsqrt(square + epsilon))
        unit.append(embeds * inv_norm[side])
    logits = logit_scale * dot_exact(unit[0], unit[1], contract_last)
    log_total = jnp.log(jnp.sum(jnp.exp(logits), -1, keepdims=True))
    target = got_ref[0, :, AT_POS : AT_POS + 1]
    passage = lax.broadcasted_iota(jnp.int32, (GROUP, GROUP), 1).astype(f32)
    one_hot = jnp.where(passage == target, 1.0, 0.0)
    chosen = jnp.sum(logits * one_hot, -1, keepdims=True)
    loss = jnp.sum(log_total - chosen, 0, keepdims=True)
    loss_ref[...] = jnp.broadcast_to(loss, (8, 128))
    score_grad = grad_scale * (jnp.exp(logits - log_total) - one_hot)
    grads = (
        dot_exact(score_grad, unit[1], (((1,), (0,)), ((), ()))),
        dot_exact(score_grad, unit[0], contract_first),
    )
    gain_sum = jnp.zeros((1, D), f32)
    first = jnp.zeros((SLICE, D), f32)
    for side in range(2):
        grad = logit_scale * grads[side]
        along = jnp.sum(unit[side] * grad, -1, keepdims=True)
        pooled_grad = (grad - unit[side] * along) * inv_norm[side]
        gain_sum = gain_sum + jnp.sum(pooled_grad * raw[side], 0, keepdims=True)
        scaled = pooled_grad * gain
        scaled_ref[side] = scaled
        first = first + dot_exact(got_ref[side, :, AT_U:AT_LEN], scaled, contract_first)
    for block in range(NR):
        columns = slice(block * COLS, (block + 1) * COLS)
        first_ref[block] = first[:, columns]
        gain_out_ref[block] = gain_sum[:, columns]

    token = lax.broadcasted_iota(jnp.int32, (SEQ, SEQ), 0)
    lane = lax.broadcasted_iota(jnp.int32, (SEQ, SEQ), 1)
    position = lax.broadcasted_iota(jnp.int32, (SEQ, 1), 0).astype(f32)
    for pair in range(NC):
        index = index_ref[pair]
        chosen_row = lax.broadcasted_iota(jnp.int32, (GROUP, 1), 0) == index
        parts = []
        for side in range(2):
            row = jnp.sum(jnp.where(chosen_row, scaled_ref[side], 0.0), 0, keepdims=True)
            high = row.astype(bf16).astype(f32)
            mid = (row - high).astype(bf16).astype(f32)
            parts += [high, mid, row - high - mid]
            rest = jnp.where(chosen_row, got_ref[side, :, AT_RMS:WIDTH], 0.0)
            rest = jnp.sum(rest, 0, keepdims=True)
            rms_row = rest[:, :SEQ]
            count = rest[:, AT_LEN - AT_RMS : AT_LEN - AT_RMS + 1]
            rms = jnp.sum(jnp.where(token == lane, rms_row, 0.0), -1, keepdims=True)
            column = jnp.where(position < count, rms / count, 0.0)
            here = slice(side * SEQ, (side + 1) * SEQ)
            column_ref[pair, here, :] = column
            scale_ref[pair, here, :] = column * rms * rms * (1.0 / D)
        parts.append(jnp.zeros((PIECES - 6, D), f32))
        piece = jnp.concatenate(parts, 0).astype(bf16)
        for block in range(NR):
            pieces_ref[pair, block] = piece[:, block * COLS : (block + 1) * COLS]


def group_math(index, got, gain):
    spec = pl.BlockSpec(memory_space=pltpu.VMEM)
    return pl.pallas_call(
        group_kernel,
        out_shape=(
            jax.ShapeDtypeStruct((NR, SLICE, COLS), f32),
            jax.ShapeDtypeStruct((NR, 1, COLS), f32),
            jax.ShapeDtypeStruct((8, 128), f32),
            jax.ShapeDtypeStruct((NC, NR, PIECES, COLS), bf16),
            jax.ShapeDtypeStruct((NC, TOK, 1), f32),
            jax.ShapeDtypeStruct((NC, TOK, 1), f32),
        ),
        in_specs=[pl.BlockSpec(memory_space=pltpu.SMEM), spec, spec],
        out_specs=(spec,) * 6,
        scratch_shapes=[pltpu.VMEM((2, GROUP, D), f32)],
        compiler_params=pltpu.CompilerParams(vmem_limit_bytes=16 * 1024 * 1024),
        cost_estimate=pl.CostEstimate(
            flops=50 * GROUP * GROUP * D, bytes_accessed=3 * 1024 * 1024, transcendentals=4096
        ),
        name="group_math",
    )(index, got, gain)


def weight_kernel(
    own_hbm, other_hbm, keep_ref, given_ref, pieces_ref, scale_ref, out_ref, coef_ref, acc_ref,
    state_ref, stage_ref, in_sems, out_sems,
):
    loads = [
        pltpu.make_async_copy(
            source.at[block], state_ref.at[pair * NT + block], in_sems.at[pair * NT + block]
        )
        for pair, source in enumerate((own_hbm, other_hbm))
        for block in range(NT)
    ]
    for load in loads:
        load.start()
    token = lax.broadcasted_iota(jnp.int32, (TOK, PIECES), 0)
    part = lax.broadcasted_iota(jnp.int32, (TOK, PIECES), 1)
    part = part - jnp.where(token < SEQ, 0, 3)
    mask = (part >= 0) & (part < 3)
    scaled = []
    for pair, attn_ref in enumerate((keep_ref, given_ref)):
        inner = jnp.zeros((TOK, PIECES), f32)
        for block in range(NT):
            loads[pair * NT + block].wait()
            inner = inner + dot_last(state_ref[pair * NT + block], pieces_ref[pair, block])
        inner = jnp.sum(jnp.where(mask, inner, 0.0), -1, keepdims=True)
        coef = scale_ref[pair] * inner
        coef_ref[pair] = coef
        scaled.append((attn_ref[...].astype(f32) * coef).astype(bf16))
    for block in range(NT):
        acc_ref[block] = lax.dot_general(
            scaled[0], state_ref[block], contract_first, preferred_element_type=f32
        ) + lax.dot_general(
            scaled[1], state_ref[NT + block], contract_first, preferred_element_type=f32
        )
    stores = []
    for place in range(NX * NY):
        rows = [
            acc_ref[block, place * SLICE : (place + 1) * SLICE, :] for block in range(NR)
        ]
        stage_ref[place] = jnp.concatenate(rows, 0).astype(bf16)
        stores.append(
            pltpu.make_async_copy(stage_ref.at[place], out_ref.at[place], out_sems.at[place])
        )
        stores[place].start()
    for store in stores:
        store.wait()


def weight_partials(own, other, keep, given, pieces, scale):
    spec = pl.BlockSpec(memory_space=pltpu.VMEM)
    hbm = pl.BlockSpec(memory_space=pltpu.HBM)
    return pl.pallas_call(
        weight_kernel,
        out_shape=(
            jax.ShapeDtypeStruct((NX * NY, NR * SLICE, COLS), bf16),
            jax.ShapeDtypeStruct((NC, TOK, 1), f32),
        ),
        in_specs=[hbm, hbm] + [spec] * 4,
        out_specs=(hbm, spec),
        scratch_shapes=[
            pltpu.VMEM((NR, HALF, COLS), f32),
            pltpu.VMEM((NC * NT, TOK, FEAT), bf16),
            pltpu.VMEM((NX * NY, NR * SLICE, COLS), bf16),
            pltpu.SemaphoreType.DMA((NC * NT,)),
            pltpu.SemaphoreType.DMA((NX * NY,)),
        ],
        compiler_params=pltpu.CompilerParams(vmem_limit_bytes=58 * 1024 * 1024),
        cost_estimate=pl.CostEstimate(
            flops=4 * TOK * HALF * D, bytes_accessed=8 * 1024 * 1024, transcendentals=0
        ),
        name="weight_partials",
    )(own, other, keep, given, pieces, scale)


def sum_kernel(spread_ref, out_ref, acc_ref):
    step = pl.program_id(0)
    part = spread_ref[0].astype(f32)
    for place in range(1, spread_ref.shape[0]):
        part = part + spread_ref[place].astype(f32)

    @pl.when(step == 0)
    def _():
        acc_ref[...] = part

    @pl.when(step > 0)
    def _():
        acc_ref[...] += part

    @pl.when(step == NX - 1)
    def _():
        for block in range(NR):
            out_ref[block] = acc_ref[block * SLICE : (block + 1) * SLICE, :].astype(bf16)


def sum_senders(spread):
    return pl.pallas_call(
        sum_kernel,
        grid=(NX,),
        out_shape=jax.ShapeDtypeStruct((NR, SLICE, COLS), bf16),
        in_specs=[pl.BlockSpec((NY, NR * SLICE, COLS), lambda step: (step, 0, 0))],
        out_specs=pl.BlockSpec((NR, SLICE, COLS), lambda step: (0, 0, 0)),
        scratch_shapes=[pltpu.VMEM((NR * SLICE, COLS), f32)],
        compiler_params=pltpu.CompilerParams(vmem_limit_bytes=16 * 1024 * 1024),
        cost_estimate=pl.CostEstimate(
            flops=NX * NY * NR * SLICE * COLS, bytes_accessed=4 * 1024 * 1024, transcendentals=0
        ),
        name="sum_senders",
    )(spread)


def join_kernel(core_ref, mine_ref, other_ref, out_ref):
    core = core_ref[0]
    for which, ref in ((core, mine_ref), (1 - core, other_ref)):
        rows = [ref[place].astype(f32) for place in range(NX * NY)]
        out_ref[pl.ds(pl.multiple_of(which * HALF, HALF), HALF), :] = jnp.concatenate(
            rows, 0
        ).astype(bf16)


def join_halves(core, mine, other):
    spec = pl.BlockSpec(memory_space=pltpu.VMEM)
    return pl.pallas_call(
        join_kernel,
        out_shape=jax.ShapeDtypeStruct((FEAT, COLS), bf16),
        in_specs=[pl.BlockSpec(memory_space=pltpu.SMEM), spec, spec],
        out_specs=spec,
        compiler_params=pltpu.CompilerParams(vmem_limit_bytes=16 * 1024 * 1024),
        cost_estimate=pl.CostEstimate(
            flops=0, bytes_accessed=4 * 1024 * 1024, transcendentals=0
        ),
        name="join_halves",
    )(core, mine, other)


def attn_kernel(
    shift_ref, own_hbm, other_hbm, pieces_ref, w_hbm, coef_ref, first_ref, keep_ref, give_ref,
    state_ref, w_ref, state_sems, w_sems,
):
    shift = shift_ref[0]
    loads = []
    for block in range(NX):
        which = lax.rem(shift + block, NR)
        loads.append(
            [pltpu.make_async_copy(w_hbm.at[block], w_ref.at[block], w_sems.at[block])]
            + [
                pltpu.make_async_copy(
                    source.at[which],
                    state_ref.at[pair * NX + block],
                    state_sems.at[pair * NX + block],
                )
                for pair, source in enumerate((own_hbm, other_hbm))
            ]
        )
        for load in loads[block]:
            load.start()
    tokens = [jnp.zeros((TOK, HALF), f32) for pair in range(NC)]
    rows = [jnp.zeros((PIECES, HALF), f32) for pair in range(NC)]
    for block in range(NX):
        which = lax.rem(shift + block, NR)
        for load in loads[block]:
            load.wait()
        for pair in range(NC):
            tokens[pair] = tokens[pair] + dot_last(state_ref[pair * NX + block], w_ref[block])
            rows[pair] = rows[pair] + dot_last(pieces_ref[pair, which], w_ref[block])
    for pair, out_ref in enumerate((keep_ref, give_ref)):
        for side in range(2):
            at = 3 * side
            row = rows[pair][at + 2 : at + 3] + rows[pair][at + 1 : at + 2]
            row = row + rows[pair][at : at + 1]
            here = slice(side * SEQ, (side + 1) * SEQ)
            out_ref[here, :] = (
                first_ref[pair, here, :] * row - coef_ref[pair, here, :] * tokens[pair][here]
            ).astype(bf16)


def attn_grads(shift, own, other, pieces, w_all, coef, first):
    spec = pl.BlockSpec(memory_space=pltpu.VMEM)
    hbm = pl.BlockSpec(memory_space=pltpu.HBM)
    out = jax.ShapeDtypeStruct((TOK, HALF), bf16)
    return pl.pallas_call(
        attn_kernel,
        out_shape=(out, out),
        in_specs=[pl.BlockSpec(memory_space=pltpu.SMEM), hbm, hbm, spec, hbm, spec, spec],
        out_specs=(spec, spec),
        scratch_shapes=[
            pltpu.VMEM((NC * NX, TOK, FEAT), bf16),
            pltpu.VMEM((NX, HALF, COLS), bf16),
            pltpu.SemaphoreType.DMA((NC * NX,)),
            pltpu.SemaphoreType.DMA((NX,)),
        ],
        compiler_params=pltpu.CompilerParams(vmem_limit_bytes=58 * 1024 * 1024),
        cost_estimate=pl.CostEstimate(
            flops=4 * TOK * HALF * D, bytes_accessed=8 * 1024 * 1024, transcendentals=0
        ),
        name="attn_grads",
    )(shift, own, other, pieces, w_all, coef, first)


def body(hidden_state, attn_out, o_weight, norm_gain, lengths, positive):
    ix, iy, ic = lax.axis_index("x"), lax.axis_index("y"), lax.axis_index("c")
    it, ir = lax.axis_index("t"), lax.axis_index("r")
    dp_index = (ix * NY + iy) * NC + ic

    state = hidden_state.reshape(TOK, FEAT)
    attn = attn_out.reshape(TOK, FEAT)
    state_all = lax.all_gather(state, "t")
    w_start = (ic * NY + iy) * W_ROWS
    w_mine = lax.dynamic_slice(o_weight, (w_start, 0), (W_ROWS, COLS))
    w_moved = lax.ppermute(
        w_mine,
        ("x", "c", "r"),
        [
            ((i * NC + k) * NR + (j + i + 2 * k) % NR, (i * NC + k) * NR + j)
            for i in range(NX)
            for k in range(NC)
            for j in range(NR)
        ],
    )
    attn_keep = jnp.where(ic == 0, attn[:, :HALF], attn[:, HALF:])
    attn_give = jnp.where(ic == 0, attn[:, HALF:], attn[:, :HALF])
    attn_other = swap_core(attn_give)

    states = state.astype(f32).reshape(2, SEQ, FEAT)
    square = lax.psum(jnp.sum(states * states, -1), "t") / D
    inv_rms = lax.rsqrt(square + epsilon)
    token_count = lengths.reshape(2).astype(f32)
    valid = (jnp.arange(SEQ, dtype=jnp.int32)[None, :] < lengths.reshape(2)[:, None]).astype(f32)
    pool_weight = valid * inv_rms / token_count[:, None]
    pooled = jnp.sum(pool_weight[..., None] * states, 1)
    attn_pool = jnp.sum(pool_weight[..., None] * attn.astype(f32).reshape(2, SEQ, FEAT), 1)

    near = jnp.concatenate([pooled, norm_gain[None]], 0)
    near = lax.all_to_all(jnp.broadcast_to(near[None], (NT, 3, FEAT)), "t", 0, 0)
    pooled_row = near[:, :2].transpose(1, 0, 2).reshape(2, D)
    gain = near[:, 2].reshape(1, D)

    u_parts = attn_pool.reshape(2, NC, NX * NY, SLICE).transpose(2, 1, 0, 3)
    u_parts = u_parts.reshape(GROUP, 2, SLICE)
    extra = jnp.stack(
        [token_count, jnp.broadcast_to(positive.astype(f32), (2,))], -1
    )
    row = jnp.concatenate([pooled_row, inv_rms], -1)
    send = jnp.concatenate(
        [
            jnp.broadcast_to(row[None], (GROUP, 2, D + SEQ)),
            u_parts,
            jnp.broadcast_to(extra[None], (GROUP, 2, 2)),
            jnp.zeros((GROUP, 2, WIDTH - AT_POS - 1), f32),
        ],
        -1,
    )
    got = lax.all_to_all(send, DP, 0, 0)
    got, attn_other = lax.optimization_barrier((got, attn_other))

    other_index = dp_index + 1 - 2 * ic
    first, gain_part, loss_part, pieces, scale, first_col = group_math(
        jnp.stack([dp_index, other_index]), got.transpose(1, 0, 2), gain
    )

    scale, state_all = lax.optimization_barrier((scale, state_all))
    state_other = swap_core(state_all)
    scale, w_moved = lax.optimization_barrier((scale, w_moved))
    w_all = lax.all_gather(w_moved, PLANE).reshape(NX, HALF, COLS)
    partial, coef = weight_partials(
        state_all, state_other, attn_keep, attn_other, pieces, scale
    )
    partial, first = lax.optimization_barrier((partial, first))
    spread = lax.all_to_all(partial, PLANE, 0, 0)

    gain_mine = lax.dynamic_index_in_dim(gain_part, it, 0, keepdims=False)
    tail = jnp.concatenate([gain_mine, jnp.broadcast_to(loss_part[:1, :1], (1, FEAT))], 0)
    tails = [tail]
    first_sum = lax.dynamic_index_in_dim(first, ir, 0, keepdims=False)
    for step in range(1, NR):
        outgoing = lax.dynamic_index_in_dim(first, (ir + step) % NR, 0, keepdims=False)
        arrived = lax.ppermute(
            jnp.concatenate([outgoing, tail], 0),
            "r",
            [(j, (j + step) % NR) for j in range(NR)],
        )
        first_sum = first_sum + arrived[:SLICE]
        tails.append(arrived[SLICE:])
    tails = jnp.stack(tails)
    totals = jnp.zeros((2, FEAT), f32)
    for source in range(NR):
        totals = totals + lax.dynamic_index_in_dim(
            tails, (ir - source) % NR, 0, keepdims=False
        )

    spread, first_sum, totals = lax.optimization_barrier((spread, first_sum, totals))
    second = lax.all_to_all(sum_senders(spread), "r", 0, 0)

    row_here = lax.dynamic_index_in_dim(pieces[0], it, 0, keepdims=False)[:6]
    row_here = row_here.astype(f32).reshape(2, 3, FEAT)
    row_here = (row_here[:, :1] + row_here[:, 1:2]) + row_here[:, 2:]
    state_grad = first_col[0].reshape(2, SEQ, 1) * row_here - states * coef[0].reshape(2, SEQ, 1)
    grad_hidden = state_grad.astype(bf16).reshape(1, 2, SEQ, FEAT)
    keep, give = attn_grads(
        (ir + 2 * ic).reshape(1), state_all, state_other, pieces, w_all, coef, first_col
    )

    second, keep, give = lax.optimization_barrier((second, keep, give))
    second_sum = jnp.sum(second.astype(f32), 0)
    total = first_sum - second_sum
    done = jnp.broadcast_to(total.astype(bf16)[None], (NX * NY, SLICE, COLS))
    half = lax.all_to_all(done, PLANE, 0, 0)
    arrived = swap_core(give)
    grad_attn = jnp.where(
        ic == 0, jnp.concatenate([keep, arrived], 1), jnp.concatenate([arrived, keep], 1)
    ).reshape(1, 2, SEQ, FEAT)
    half, grad_attn, grad_hidden, totals = lax.optimization_barrier(
        (half, grad_attn, grad_hidden, totals)
    )
    half_other = swap_core(half)
    grad_weight = join_halves(ic.reshape(1), half, half_other)
    return (grad_hidden, grad_attn, grad_weight, totals[0], totals[1, 0])


def solution(mesh):
    fine = Mesh(mesh.devices.reshape(NX, NY, NC, NT, NR), ("x", "y", "c", "t", "r"))
    pairs = ("x", "y", "c", "r")
    placed = (
        P(pairs, None, None, "t"),
        P(pairs, None, None, "t"),
        P("t", "r"),
        P("t"),
        P(pairs, None),
        P(pairs),
    )
    return jax.shard_map(
        body,
        mesh=fine,
        in_specs=placed,
        out_specs=(
            P(pairs, None, None, "t"),
            P(pairs, None, None, "t"),
            P("t", "r"),
            P("t"),
            P(),
        ),
        check_vma=False,
    )
```

```python
import jax
import jax.numpy as jnp
from jax import lax
from jax.experimental import pallas as pl
from jax.experimental.pallas import tpu as pltpu
from jax.sharding import Mesh, PartitionSpec as P

logit_scale = 20.0
grad_scale = 256.0
epsilon = 1e-06

f32 = jnp.float32
bf16 = jnp.bfloat16

NX, NY, NC, NT, NR = 4, 4, 2, 4, 4
PLANE = ("x", "y")
DP = ("x", "y", "c")

D = 3584
FEAT = D // NT
COLS = D // NR
SEQ = 128
TOK = 2 * SEQ
HALF = FEAT // NC
SLICE = HALF // (NX * NY)
W_FIRST = 64
W_REST = HALF // NY - W_FIRST
PIECES = 16
GROUP = NX * NY * NC

AT_RMS = D
AT_U = D + SEQ
AT_LEN = AT_U + SLICE
AT_POS = AT_LEN + 1
WIDTH = D + 2 * SEQ


def swap_core(value):
    return lax.ppermute(value, "c", [(0, 1), (1, 0)])


contract_last = (((1,), (1,)), ((), ()))
contract_first = (((0,), (0,)), ((), ()))


def dot_last(left, right):
    return lax.dot_general(left, right, contract_last, preferred_element_type=f32)


def dot_exact(left, right, dims):
    return lax.dot_general(
        left, right, dims, precision=lax.Precision.HIGHEST, preferred_element_type=f32
    )


def group_kernel(
    index_ref, got_ref, gain_ref,
    first_ref, gain_out_ref, loss_ref, pieces_ref, scale_ref, column_ref, scaled_ref,
):
    gain = gain_ref[...]
    raw, unit, inv_norm = [], [], []
    for side in range(2):
        raw.append(got_ref[side, :, :D])
        embeds = raw[side] * gain
        square = jnp.sum(embeds * embeds, -1, keepdims=True)
        inv_norm.append(lax.rsqrt(square + epsilon))
        unit.append(embeds * inv_norm[side])
    logits = logit_scale * dot_exact(unit[0], unit[1], contract_last)
    log_total = jnp.log(jnp.sum(jnp.exp(logits), -1, keepdims=True))
    target = got_ref[0, :, AT_POS : AT_POS + 1]
    passage = lax.broadcasted_iota(jnp.int32, (GROUP, GROUP), 1).astype(f32)
    one_hot = jnp.where(passage == target, 1.0, 0.0)
    chosen = jnp.sum(logits * one_hot, -1, keepdims=True)
    loss = jnp.sum(log_total - chosen, 0, keepdims=True)
    loss_ref[...] = jnp.broadcast_to(loss, (8, 128))
    score_grad = grad_scale * (jnp.exp(logits - log_total) - one_hot)
    grads = (
        dot_exact(score_grad, unit[1], (((1,), (0,)), ((), ()))),
        dot_exact(score_grad, unit[0], contract_first),
    )
    gain_sum = jnp.zeros((1, D), f32)
    first = jnp.zeros((SLICE, D), f32)
    for side in range(2):
        grad = logit_scale * grads[side]
        along = jnp.sum(unit[side] * grad, -1, keepdims=True)
        pooled_grad = (grad - unit[side] * along) * inv_norm[side]
        gain_sum = gain_sum + jnp.sum(pooled_grad * raw[side], 0, keepdims=True)
        scaled = pooled_grad * gain
        scaled_ref[side] = scaled
        first = first + dot_exact(got_ref[side, :, AT_U:AT_LEN], scaled, contract_first)
    for block in range(NR):
        columns = slice(block * COLS, (block + 1) * COLS)
        first_ref[block] = first[:, columns]
        gain_out_ref[block] = gain_sum[:, columns]

    token = lax.broadcasted_iota(jnp.int32, (SEQ, SEQ), 0)
    lane = lax.broadcasted_iota(jnp.int32, (SEQ, SEQ), 1)
    position = lax.broadcasted_iota(jnp.int32, (SEQ, 1), 0).astype(f32)
    for pair in range(NC):
        index = index_ref[pair]
        chosen_row = lax.broadcasted_iota(jnp.int32, (GROUP, 1), 0) == index
        parts = []
        for side in range(2):
            row = jnp.sum(jnp.where(chosen_row, scaled_ref[side], 0.0), 0, keepdims=True)
            high = row.astype(bf16).astype(f32)
            mid = (row - high).astype(bf16).astype(f32)
            parts += [high, mid, row - high - mid]
            rest = jnp.where(chosen_row, got_ref[side, :, AT_RMS:WIDTH], 0.0)
            rest = jnp.sum(rest, 0, keepdims=True)
            rms_row = rest[:, :SEQ]
            count = rest[:, AT_LEN - AT_RMS : AT_LEN - AT_RMS + 1]
            rms = jnp.sum(jnp.where(token == lane, rms_row, 0.0), -1, keepdims=True)
            column = jnp.where(position < count, rms / count, 0.0)
            here = slice(side * SEQ, (side + 1) * SEQ)
            column_ref[pair, here, :] = column
            scale_ref[pair, here, :] = column * rms * rms * (1.0 / D)
        parts.append(jnp.zeros((PIECES - 6, D), f32))
        piece = jnp.concatenate(parts, 0).astype(bf16)
        for block in range(NR):
            pieces_ref[pair, block] = piece[:, block * COLS : (block + 1) * COLS]


def group_math(index, got, gain):
    spec = pl.BlockSpec(memory_space=pltpu.VMEM)
    return pl.pallas_call(
        group_kernel,
        out_shape=(
            jax.ShapeDtypeStruct((NR, SLICE, COLS), f32),
            jax.ShapeDtypeStruct((NR, 1, COLS), f32),
            jax.ShapeDtypeStruct((8, 128), f32),
            jax.ShapeDtypeStruct((NC, NR, PIECES, COLS), bf16),
            jax.ShapeDtypeStruct((NC, TOK, 1), f32),
            jax.ShapeDtypeStruct((NC, TOK, 1), f32),
        ),
        in_specs=[pl.BlockSpec(memory_space=pltpu.SMEM), spec, spec],
        out_specs=(spec,) * 6,
        scratch_shapes=[pltpu.VMEM((2, GROUP, D), f32)],
        compiler_params=pltpu.CompilerParams(vmem_limit_bytes=16 * 1024 * 1024),
        cost_estimate=pl.CostEstimate(
            flops=50 * GROUP * GROUP * D, bytes_accessed=3 * 1024 * 1024, transcendentals=4096
        ),
        name="group_math",
    )(index, got, gain)


def weight_kernel(
    own_ref, other_ref, keep_ref, given_ref, pieces_ref, scale_ref, out_ref, coef_ref, acc_ref
):
    token = lax.broadcasted_iota(jnp.int32, (TOK, PIECES), 0)
    part = lax.broadcasted_iota(jnp.int32, (TOK, PIECES), 1)
    part = part - jnp.where(token < SEQ, 0, 3)
    mask = (part >= 0) & (part < 3)
    scaled = []
    for pair, (state_ref, attn_ref) in enumerate(
        ((own_ref, keep_ref), (other_ref, given_ref))
    ):
        inner = jnp.zeros((TOK, PIECES), f32)
        for block in range(NT):
            inner = inner + dot_last(state_ref[block], pieces_ref[pair, block])
        inner = jnp.sum(jnp.where(mask, inner, 0.0), -1, keepdims=True)
        coef = scale_ref[pair] * inner
        coef_ref[pair] = coef
        scaled.append((attn_ref[...].astype(f32) * coef).astype(bf16))
    for block in range(NT):
        acc_ref[block] = lax.dot_general(
            scaled[0], own_ref[block], contract_first, preferred_element_type=f32
        ) + lax.dot_general(
            scaled[1], other_ref[block], contract_first, preferred_element_type=f32
        )
    for place in range(NX * NY):
        rows = [
            acc_ref[block, place * SLICE : (place + 1) * SLICE, :] for block in range(NR)
        ]
        out_ref[place] = jnp.concatenate(rows, 0).astype(bf16)


def weight_partials(own, other, keep, given, pieces, scale):
    spec = pl.BlockSpec(memory_space=pltpu.VMEM)
    return pl.pallas_call(
        weight_kernel,
        out_shape=(
            jax.ShapeDtypeStruct((NX * NY, NR * SLICE, COLS), bf16),
            jax.ShapeDtypeStruct((NC, TOK, 1), f32),
        ),
        in_specs=[spec] * 6,
        out_specs=(spec, spec),
        scratch_shapes=[pltpu.VMEM((NR, HALF, COLS), f32)],
        compiler_params=pltpu.CompilerParams(vmem_limit_bytes=24 * 1024 * 1024),
        cost_estimate=pl.CostEstimate(
            flops=4 * TOK * HALF * D, bytes_accessed=8 * 1024 * 1024, transcendentals=0
        ),
        name="weight_partials",
    )(own, other, keep, given, pieces, scale)


def sum_kernel(spread_ref, out_ref, acc_ref):
    step = pl.program_id(0)
    part = spread_ref[0].astype(f32)
    for place in range(1, spread_ref.shape[0]):
        part = part + spread_ref[place].astype(f32)

    @pl.when(step == 0)
    def _():
        acc_ref[...] = part

    @pl.when(step > 0)
    def _():
        acc_ref[...] += part

    @pl.when(step == NX - 1)
    def _():
        for block in range(NR):
            out_ref[block] = acc_ref[block * SLICE : (block + 1) * SLICE, :].astype(bf16)


def sum_senders(spread):
    return pl.pallas_call(
        sum_kernel,
        grid=(NX,),
        out_shape=jax.ShapeDtypeStruct((NR, SLICE, COLS), bf16),
        in_specs=[pl.BlockSpec((NY, NR * SLICE, COLS), lambda step: (step, 0, 0))],
        out_specs=pl.BlockSpec((NR, SLICE, COLS), lambda step: (0, 0, 0)),
        scratch_shapes=[pltpu.VMEM((NR * SLICE, COLS), f32)],
        compiler_params=pltpu.CompilerParams(vmem_limit_bytes=16 * 1024 * 1024),
        cost_estimate=pl.CostEstimate(
            flops=NX * NY * NR * SLICE * COLS, bytes_accessed=4 * 1024 * 1024, transcendentals=0
        ),
        name="sum_senders",
    )(spread)


def join_kernel(core_ref, mine_ref, other_ref, out_ref):
    core = core_ref[0]
    for which, ref in ((core, mine_ref), (1 - core, other_ref)):
        rows = [ref[place].astype(f32) for place in range(NX * NY)]
        out_ref[pl.ds(pl.multiple_of(which * HALF, HALF), HALF), :] = jnp.concatenate(
            rows, 0
        ).astype(bf16)


def join_halves(core, mine, other):
    spec = pl.BlockSpec(memory_space=pltpu.VMEM)
    return pl.pallas_call(
        join_kernel,
        out_shape=jax.ShapeDtypeStruct((FEAT, COLS), bf16),
        in_specs=[pl.BlockSpec(memory_space=pltpu.SMEM), spec, spec],
        out_specs=spec,
        compiler_params=pltpu.CompilerParams(vmem_limit_bytes=16 * 1024 * 1024),
        cost_estimate=pl.CostEstimate(
            flops=0, bytes_accessed=4 * 1024 * 1024, transcendentals=0
        ),
        name="join_halves",
    )(core, mine, other)


def attn_kernel(
    shift_ref, own_hbm, other_hbm, pieces_ref, w_hbm, coef_ref, first_ref, keep_ref, give_ref,
    state_ref, w_ref, state_sems, w_sems,
):
    shift = shift_ref[0]
    columns = w_ref.shape[1]
    loads = []
    for block in range(NX):
        which = lax.rem(shift + block, NR)
        loads.append(
            [pltpu.make_async_copy(w_hbm.at[block], w_ref.at[block], w_sems.at[block])]
            + [
                pltpu.make_async_copy(
                    source.at[which],
                    state_ref.at[pair * NX + block],
                    state_sems.at[pair * NX + block],
                )
                for pair, source in enumerate((own_hbm, other_hbm))
            ]
        )
        for load in loads[block]:
            load.start()
    tokens = [jnp.zeros((TOK, columns), f32) for pair in range(NC)]
    rows = [jnp.zeros((PIECES, columns), f32) for pair in range(NC)]
    for block in range(NX):
        which = lax.rem(shift + block, NR)
        for load in loads[block]:
            load.wait()
        for pair in range(NC):
            tokens[pair] = tokens[pair] + dot_last(state_ref[pair * NX + block], w_ref[block])
            rows[pair] = rows[pair] + dot_last(pieces_ref[pair, which], w_ref[block])
    for pair, out_ref in enumerate((keep_ref, give_ref)):
        for side in range(2):
            at = 3 * side
            row = rows[pair][at + 2 : at + 3] + rows[pair][at + 1 : at + 2]
            row = row + rows[pair][at : at + 1]
            here = slice(side * SEQ, (side + 1) * SEQ)
            out_ref[here, :] = (
                first_ref[pair, here, :] * row - coef_ref[pair, here, :] * tokens[pair][here]
            ).astype(bf16)


def attn_grads(shift, own, other, pieces, w_all, coef, first):
    spec = pl.BlockSpec(memory_space=pltpu.VMEM)
    hbm = pl.BlockSpec(memory_space=pltpu.HBM)
    columns = w_all.shape[1]
    out = jax.ShapeDtypeStruct((TOK, columns), bf16)
    return pl.pallas_call(
        attn_kernel,
        out_shape=(out, out),
        in_specs=[pl.BlockSpec(memory_space=pltpu.SMEM), hbm, hbm, spec, hbm, spec, spec],
        out_specs=(spec, spec),
        scratch_shapes=[
            pltpu.VMEM((NC * NX, TOK, FEAT), bf16),
            pltpu.VMEM((NX, columns, COLS), bf16),
            pltpu.SemaphoreType.DMA((NC * NX,)),
            pltpu.SemaphoreType.DMA((NX,)),
        ],
        compiler_params=pltpu.CompilerParams(vmem_limit_bytes=58 * 1024 * 1024),
        cost_estimate=pl.CostEstimate(
            flops=4 * TOK * columns * D, bytes_accessed=8 * 1024 * 1024, transcendentals=0
        ),
        name="attn_grads",
    )(shift, own, other, pieces, w_all, coef, first)


def body(hidden_state, attn_out, o_weight, norm_gain, lengths, positive):
    ix, iy, ic = lax.axis_index("x"), lax.axis_index("y"), lax.axis_index("c")
    it, ir = lax.axis_index("t"), lax.axis_index("r")
    dp_index = (ix * NY + iy) * NC + ic

    state = hidden_state.reshape(TOK, FEAT)
    attn = attn_out.reshape(TOK, FEAT)
    state_all = lax.all_gather(state, "t")
    w_routes = [
        ((i * NC + k) * NR + (j + i + 2 * k) % NR, (i * NC + k) * NR + j)
        for i in range(NX)
        for k in range(NC)
        for j in range(NR)
    ]
    w_first = lax.ppermute(
        lax.dynamic_slice(o_weight, (ic * HALF + iy * W_FIRST, 0), (W_FIRST, COLS)),
        ("x", "c", "r"),
        w_routes,
    )
    w_rest = lax.ppermute(
        lax.dynamic_slice(
            o_weight, (ic * HALF + NY * W_FIRST + iy * W_REST, 0), (W_REST, COLS)
        ),
        ("x", "c", "r"),
        w_routes,
    )
    attn_keep = jnp.where(ic == 0, attn[:, :HALF], attn[:, HALF:])
    attn_give = jnp.where(ic == 0, attn[:, HALF:], attn[:, :HALF])
    attn_other = swap_core(attn_give)

    states = state.astype(f32).reshape(2, SEQ, FEAT)
    square = lax.psum(jnp.sum(states * states, -1), "t") / D
    inv_rms = lax.rsqrt(square + epsilon)
    token_count = lengths.reshape(2).astype(f32)
    valid = (jnp.arange(SEQ, dtype=jnp.int32)[None, :] < lengths.reshape(2)[:, None]).astype(f32)
    pool_weight = valid * inv_rms / token_count[:, None]
    pooled = jnp.sum(pool_weight[..., None] * states, 1)
    attn_pool = jnp.sum(pool_weight[..., None] * attn.astype(f32).reshape(2, SEQ, FEAT), 1)

    near = jnp.concatenate([pooled, norm_gain[None]], 0)
    near = lax.all_to_all(jnp.broadcast_to(near[None], (NT, 3, FEAT)), "t", 0, 0)
    pooled_row = near[:, :2].transpose(1, 0, 2).reshape(2, D)
    gain = near[:, 2].reshape(1, D)

    u_parts = attn_pool.reshape(2, NC, NX * NY, SLICE).transpose(2, 1, 0, 3)
    u_parts = u_parts.reshape(GROUP, 2, SLICE)
    extra = jnp.stack(
        [token_count, jnp.broadcast_to(positive.astype(f32), (2,))], -1
    )
    row = jnp.concatenate([pooled_row, inv_rms], -1)
    send = jnp.concatenate(
        [
            jnp.broadcast_to(row[None], (GROUP, 2, D + SEQ)),
            u_parts,
            jnp.broadcast_to(extra[None], (GROUP, 2, 2)),
            jnp.zeros((GROUP, 2, WIDTH - AT_POS - 1), f32),
        ],
        -1,
    )
    got = lax.all_to_all(send, DP, 0, 0)
    got, attn_other, w_first = lax.optimization_barrier((got, attn_other, w_first))

    other_index = dp_index + 1 - 2 * ic
    got, state_all = lax.optimization_barrier((got, state_all))
    state_other = swap_core(state_all)
    w_first = lax.all_gather(w_first, PLANE).reshape(NX, NY * W_FIRST, COLS)
    first, gain_part, loss_part, pieces, scale, first_col = group_math(
        jnp.stack([dp_index, other_index]), got.transpose(1, 0, 2), gain
    )

    partial, coef = weight_partials(
        state_all, state_other, attn_keep, attn_other, pieces, scale
    )
    partial, first = lax.optimization_barrier((partial, first))
    spread = lax.all_to_all(partial, PLANE, 0, 0)

    gain_mine = lax.dynamic_index_in_dim(gain_part, it, 0, keepdims=False)
    tail = jnp.concatenate([gain_mine, jnp.broadcast_to(loss_part[:1, :1], (1, FEAT))], 0)
    tails = [tail]
    first_sum = lax.dynamic_index_in_dim(first, ir, 0, keepdims=False)
    for step in range(1, NR):
        outgoing = lax.dynamic_index_in_dim(first, (ir + step) % NR, 0, keepdims=False)
        arrived = lax.ppermute(
            jnp.concatenate([outgoing, tail], 0),
            "r",
            [(j, (j + step) % NR) for j in range(NR)],
        )
        first_sum = first_sum + arrived[:SLICE]
        tails.append(arrived[SLICE:])
    tails = jnp.stack(tails)
    totals = jnp.zeros((2, FEAT), f32)
    for source in range(NR):
        totals = totals + lax.dynamic_index_in_dim(
            tails, (ir - source) % NR, 0, keepdims=False
        )

    row_here = lax.dynamic_index_in_dim(pieces[0], it, 0, keepdims=False)[:6]
    row_here = row_here.astype(f32).reshape(2, 3, FEAT)
    row_here = (row_here[:, :1] + row_here[:, 1:2]) + row_here[:, 2:]
    state_grad = first_col[0].reshape(2, SEQ, 1) * row_here - states * coef[0].reshape(2, SEQ, 1)
    grad_hidden = state_grad.astype(bf16).reshape(1, 2, SEQ, FEAT)
    shift = (ir + 2 * ic).reshape(1)
    keep, give = attn_grads(shift, state_all, state_other, pieces, w_first, coef, first_col)
    arrived = swap_core(give)

    spread, first_sum, totals, grad_hidden, arrived, w_rest = lax.optimization_barrier(
        (spread, first_sum, totals, grad_hidden, arrived, w_rest)
    )
    w_rest = lax.all_gather(w_rest, PLANE).reshape(NX, NY * W_REST, COLS)
    second = lax.all_to_all(sum_senders(spread), "r", 0, 0)
    second_sum = jnp.sum(second.astype(f32), 0)
    total = first_sum - second_sum
    done = jnp.broadcast_to(total.astype(bf16)[None], (NX * NY, SLICE, COLS))
    half = lax.all_to_all(done, PLANE, 0, 0)
    keep_rest, give_rest = attn_grads(
        shift, state_all, state_other, pieces, w_rest, coef, first_col
    )
    half, keep_rest, give_rest = lax.optimization_barrier((half, keep_rest, give_rest))
    half_other = swap_core(half)
    arrived_rest = swap_core(give_rest)
    mine = [keep, keep_rest]
    theirs = [arrived, arrived_rest]
    grad_attn = jnp.where(
        ic == 0, jnp.concatenate(mine + theirs, 1), jnp.concatenate(theirs + mine, 1)
    ).reshape(1, 2, SEQ, FEAT)
    grad_weight = join_halves(ic.reshape(1), half, half_other)
    return (grad_hidden, grad_attn, grad_weight, totals[0], totals[1, 0])


def solution(mesh):
    fine = Mesh(mesh.devices.reshape(NX, NY, NC, NT, NR), ("x", "y", "c", "t", "r"))
    pairs = ("x", "y", "c", "r")
    placed = (
        P(pairs, None, None, "t"),
        P(pairs, None, None, "t"),
        P("t", "r"),
        P("t"),
        P(pairs, None),
        P(pairs),
    )
    return jax.shard_map(
        body,
        mesh=fine,
        in_specs=placed,
        out_specs=(
            P(pairs, None, None, "t"),
            P(pairs, None, None, "t"),
            P("t", "r"),
            P("t"),
            P(),
        ),
        check_vma=False,
    )
```

```python
import jax
import jax.numpy as jnp
from jax import lax
from jax.experimental import pallas as pl
from jax.experimental.pallas import tpu as pltpu
from jax.sharding import Mesh, PartitionSpec as P

logit_scale = 20.0
grad_scale = 256.0
epsilon = 1e-06

f32 = jnp.float32
bf16 = jnp.bfloat16

NX, NY, NC, NT, NR = 4, 4, 2, 4, 4
PLANE = ("x", "y")
DP = ("x", "y", "c")

D = 3584
FEAT = D // NT
COLS = D // NR
SEQ = 128
TOK = 2 * SEQ
HALF = FEAT // NC
SLICE = HALF // (NX * NY)
W_ROWS = HALF // NY
PIECES = 16
GROUP = NX * NY * NC

AT_RMS = D
AT_U = D + SEQ
AT_LEN = AT_U + SLICE
AT_POS = AT_LEN + 1
WIDTH = D + 2 * SEQ


def swap_core(value):
    return lax.ppermute(value, "c", [(0, 1), (1, 0)])


contract_last = (((1,), (1,)), ((), ()))
contract_first = (((0,), (0,)), ((), ()))


def dot_last(left, right):
    return lax.dot_general(left, right, contract_last, preferred_element_type=f32)


def dot_exact(left, right, dims):
    return lax.dot_general(
        left, right, dims, precision=lax.Precision.HIGHEST, preferred_element_type=f32
    )


def group_kernel(
    index_ref, got_ref, gain_ref,
    first_ref, gain_out_ref, loss_ref, pieces_ref, scale_ref, column_ref, scaled_ref,
):
    gain = gain_ref[...]
    raw, unit, inv_norm = [], [], []
    for side in range(2):
        raw.append(got_ref[side, :, :D])
        embeds = raw[side] * gain
        square = jnp.sum(embeds * embeds, -1, keepdims=True)
        inv_norm.append(lax.rsqrt(square + epsilon))
        unit.append(embeds * inv_norm[side])
    logits = logit_scale * dot_exact(unit[0], unit[1], contract_last)
    log_total = jnp.log(jnp.sum(jnp.exp(logits), -1, keepdims=True))
    target = got_ref[0, :, AT_POS : AT_POS + 1]
    passage = lax.broadcasted_iota(jnp.int32, (GROUP, GROUP), 1).astype(f32)
    one_hot = jnp.where(passage == target, 1.0, 0.0)
    chosen = jnp.sum(logits * one_hot, -1, keepdims=True)
    loss = jnp.sum(log_total - chosen, 0, keepdims=True)
    loss_ref[...] = jnp.broadcast_to(loss, (8, 128))
    score_grad = grad_scale * (jnp.exp(logits - log_total) - one_hot)
    grads = (
        dot_exact(score_grad, unit[1], (((1,), (0,)), ((), ()))),
        dot_exact(score_grad, unit[0], contract_first),
    )
    gain_sum = jnp.zeros((1, D), f32)
    first = jnp.zeros((SLICE, D), f32)
    for side in range(2):
        grad = logit_scale * grads[side]
        along = jnp.sum(unit[side] * grad, -1, keepdims=True)
        pooled_grad = (grad - unit[side] * along) * inv_norm[side]
        gain_sum = gain_sum + jnp.sum(pooled_grad * raw[side], 0, keepdims=True)
        scaled = pooled_grad * gain
        scaled_ref[side] = scaled
        first = first + dot_exact(got_ref[side, :, AT_U:AT_LEN], scaled, contract_first)
    for block in range(NR):
        columns = slice(block * COLS, (block + 1) * COLS)
        first_ref[block] = first[:, columns]
        gain_out_ref[block] = gain_sum[:, columns]

    token = lax.broadcasted_iota(jnp.int32, (SEQ, SEQ), 0)
    lane = lax.broadcasted_iota(jnp.int32, (SEQ, SEQ), 1)
    position = lax.broadcasted_iota(jnp.int32, (SEQ, 1), 0).astype(f32)
    for pair in range(NC):
        index = index_ref[pair]
        chosen_row = lax.broadcasted_iota(jnp.int32, (GROUP, 1), 0) == index
        parts = []
        for side in range(2):
            row = jnp.sum(jnp.where(chosen_row, scaled_ref[side], 0.0), 0, keepdims=True)
            high = row.astype(bf16).astype(f32)
            mid = (row - high).astype(bf16).astype(f32)
            parts += [high, mid, row - high - mid]
            rest = jnp.where(chosen_row, got_ref[side, :, AT_RMS:WIDTH], 0.0)
            rest = jnp.sum(rest, 0, keepdims=True)
            rms_row = rest[:, :SEQ]
            count = rest[:, AT_LEN - AT_RMS : AT_LEN - AT_RMS + 1]
            rms = jnp.sum(jnp.where(token == lane, rms_row, 0.0), -1, keepdims=True)
            column = jnp.where(position < count, rms / count, 0.0)
            here = slice(side * SEQ, (side + 1) * SEQ)
            column_ref[pair, here, :] = column
            scale_ref[pair, here, :] = column * rms * rms * (1.0 / D)
        parts.append(jnp.zeros((PIECES - 6, D), f32))
        piece = jnp.concatenate(parts, 0).astype(bf16)
        for block in range(NR):
            pieces_ref[pair, block] = piece[:, block * COLS : (block + 1) * COLS]


def group_math(index, got, gain):
    spec = pl.BlockSpec(memory_space=pltpu.VMEM)
    return pl.pallas_call(
        group_kernel,
        out_shape=(
            jax.ShapeDtypeStruct((NR, SLICE, COLS), f32),
            jax.ShapeDtypeStruct((NR, 1, COLS), f32),
            jax.ShapeDtypeStruct((8, 128), f32),
            jax.ShapeDtypeStruct((NC, NR, PIECES, COLS), bf16),
            jax.ShapeDtypeStruct((NC, TOK, 1), f32),
            jax.ShapeDtypeStruct((NC, TOK, 1), f32),
        ),
        in_specs=[pl.BlockSpec(memory_space=pltpu.SMEM), spec, spec],
        out_specs=(spec,) * 6,
        scratch_shapes=[pltpu.VMEM((2, GROUP, D), f32)],
        compiler_params=pltpu.CompilerParams(vmem_limit_bytes=16 * 1024 * 1024),
        cost_estimate=pl.CostEstimate(
            flops=50 * GROUP * GROUP * D, bytes_accessed=3 * 1024 * 1024, transcendentals=4096
        ),
        name="group_math",
    )(index, got, gain)


def weight_kernel(
    own_ref, other_ref, keep_ref, given_ref, pieces_ref, scale_ref, out_ref, coef_ref, acc_ref
):
    token = lax.broadcasted_iota(jnp.int32, (TOK, PIECES), 0)
    part = lax.broadcasted_iota(jnp.int32, (TOK, PIECES), 1)
    part = part - jnp.where(token < SEQ, 0, 3)
    mask = (part >= 0) & (part < 3)
    scaled = []
    for pair, (state_ref, attn_ref) in enumerate(
        ((own_ref, keep_ref), (other_ref, given_ref))
    ):
        inner = jnp.zeros((TOK, PIECES), f32)
        for block in range(NT):
            inner = inner + dot_last(state_ref[block], pieces_ref[pair, block])
        inner = jnp.sum(jnp.where(mask, inner, 0.0), -1, keepdims=True)
        coef = scale_ref[pair] * inner
        coef_ref[pair] = coef
        scaled.append((attn_ref[...].astype(f32) * coef).astype(bf16))
    for block in range(NT):
        acc_ref[block] = lax.dot_general(
            scaled[0], own_ref[block], contract_first, preferred_element_type=f32
        ) + lax.dot_general(
            scaled[1], other_ref[block], contract_first, preferred_element_type=f32
        )
    for place in range(NX * NY):
        rows = [
            acc_ref[block, place * SLICE : (place + 1) * SLICE, :] for block in range(NR)
        ]
        out_ref[place] = jnp.concatenate(rows, 0).astype(bf16)


def weight_partials(own, other, keep, given, pieces, scale):
    spec = pl.BlockSpec(memory_space=pltpu.VMEM)
    return pl.pallas_call(
        weight_kernel,
        out_shape=(
            jax.ShapeDtypeStruct((NX * NY, NR * SLICE, COLS), bf16),
            jax.ShapeDtypeStruct((NC, TOK, 1), f32),
        ),
        in_specs=[spec] * 6,
        out_specs=(spec, spec),
        scratch_shapes=[pltpu.VMEM((NR, HALF, COLS), f32)],
        compiler_params=pltpu.CompilerParams(vmem_limit_bytes=24 * 1024 * 1024),
        cost_estimate=pl.CostEstimate(
            flops=4 * TOK * HALF * D, bytes_accessed=8 * 1024 * 1024, transcendentals=0
        ),
        name="weight_partials",
    )(own, other, keep, given, pieces, scale)


def sum_kernel(spread_ref, out_ref, acc_ref):
    step = pl.program_id(0)
    part = spread_ref[0].astype(f32)
    for place in range(1, spread_ref.shape[0]):
        part = part + spread_ref[place].astype(f32)

    @pl.when(step == 0)
    def _():
        acc_ref[...] = part

    @pl.when(step > 0)
    def _():
        acc_ref[...] += part

    @pl.when(step == NX - 1)
    def _():
        for block in range(NR):
            out_ref[block] = acc_ref[block * SLICE : (block + 1) * SLICE, :].astype(bf16)


def sum_senders(spread):
    return pl.pallas_call(
        sum_kernel,
        grid=(NX,),
        out_shape=jax.ShapeDtypeStruct((NR, SLICE, COLS), bf16),
        in_specs=[pl.BlockSpec((NY, NR * SLICE, COLS), lambda step: (step, 0, 0))],
        out_specs=pl.BlockSpec((NR, SLICE, COLS), lambda step: (0, 0, 0)),
        scratch_shapes=[pltpu.VMEM((NR * SLICE, COLS), f32)],
        compiler_params=pltpu.CompilerParams(vmem_limit_bytes=16 * 1024 * 1024),
        cost_estimate=pl.CostEstimate(
            flops=NX * NY * NR * SLICE * COLS, bytes_accessed=4 * 1024 * 1024, transcendentals=0
        ),
        name="sum_senders",
    )(spread)


def join_kernel(core_ref, mine_ref, other_ref, out_ref):
    core = core_ref[0]
    for which, ref in ((core, mine_ref), (1 - core, other_ref)):
        rows = [ref[place].astype(f32) for place in range(NX * NY)]
        out_ref[pl.ds(pl.multiple_of(which * HALF, HALF), HALF), :] = jnp.concatenate(
            rows, 0
        ).astype(bf16)


def join_halves(core, mine, other):
    spec = pl.BlockSpec(memory_space=pltpu.VMEM)
    return pl.pallas_call(
        join_kernel,
        out_shape=jax.ShapeDtypeStruct((FEAT, COLS), bf16),
        in_specs=[pl.BlockSpec(memory_space=pltpu.SMEM), spec, spec],
        out_specs=spec,
        compiler_params=pltpu.CompilerParams(vmem_limit_bytes=16 * 1024 * 1024),
        cost_estimate=pl.CostEstimate(
            flops=0, bytes_accessed=4 * 1024 * 1024, transcendentals=0
        ),
        name="join_halves",
    )(core, mine, other)


def attn_kernel(
    shift_ref, own_hbm, other_hbm, pieces_ref, w_hbm, coef_ref, first_ref, keep_ref, give_ref,
    state_ref, w_ref, state_sems, w_sems,
):
    shift = shift_ref[0]
    columns = w_ref.shape[1]
    loads = []
    for block in range(NX):
        which = lax.rem(shift + block, NR)
        loads.append(
            [pltpu.make_async_copy(w_hbm.at[block], w_ref.at[block], w_sems.at[block])]
            + [
                pltpu.make_async_copy(
                    source.at[which],
                    state_ref.at[pair * NX + block],
                    state_sems.at[pair * NX + block],
                )
                for pair, source in enumerate((own_hbm, other_hbm))
            ]
        )
        for load in loads[block]:
            load.start()
    tokens = [jnp.zeros((TOK, columns), f32) for pair in range(NC)]
    rows = [jnp.zeros((PIECES, columns), f32) for pair in range(NC)]
    for block in range(NX):
        which = lax.rem(shift + block, NR)
        for load in loads[block]:
            load.wait()
        for pair in range(NC):
            tokens[pair] = tokens[pair] + dot_last(state_ref[pair * NX + block], w_ref[block])
            rows[pair] = rows[pair] + dot_last(pieces_ref[pair, which], w_ref[block])
    for pair, out_ref in enumerate((keep_ref, give_ref)):
        for side in range(2):
            at = 3 * side
            row = rows[pair][at + 2 : at + 3] + rows[pair][at + 1 : at + 2]
            row = row + rows[pair][at : at + 1]
            here = slice(side * SEQ, (side + 1) * SEQ)
            out_ref[here, :] = (
                first_ref[pair, here, :] * row - coef_ref[pair, here, :] * tokens[pair][here]
            ).astype(bf16)


def attn_grads(shift, own, other, pieces, w_all, coef, first):
    spec = pl.BlockSpec(memory_space=pltpu.VMEM)
    hbm = pl.BlockSpec(memory_space=pltpu.HBM)
    columns = w_all.shape[1]
    out = jax.ShapeDtypeStruct((TOK, columns), bf16)
    return pl.pallas_call(
        attn_kernel,
        out_shape=(out, out),
        in_specs=[pl.BlockSpec(memory_space=pltpu.SMEM), hbm, hbm, spec, hbm, spec, spec],
        out_specs=(spec, spec),
        scratch_shapes=[
            pltpu.VMEM((NC * NX, TOK, FEAT), bf16),
            pltpu.VMEM((NX, columns, COLS), bf16),
            pltpu.SemaphoreType.DMA((NC * NX,)),
            pltpu.SemaphoreType.DMA((NX,)),
        ],
        compiler_params=pltpu.CompilerParams(vmem_limit_bytes=58 * 1024 * 1024),
        cost_estimate=pl.CostEstimate(
            flops=4 * TOK * columns * D, bytes_accessed=8 * 1024 * 1024, transcendentals=0
        ),
        name="attn_grads",
    )(shift, own, other, pieces, w_all, coef, first)


def body(hidden_state, attn_out, o_weight, norm_gain, lengths, positive):
    ix, iy, ic = lax.axis_index("x"), lax.axis_index("y"), lax.axis_index("c")
    it, ir = lax.axis_index("t"), lax.axis_index("r")
    dp_index = (ix * NY + iy) * NC + ic

    state = hidden_state.reshape(TOK, FEAT)
    attn = attn_out.reshape(TOK, FEAT)
    state_all = lax.all_gather(state, "t")
    w_routes = [
        ((i * NC + k) * NR + (j + i + 2 * k) % NR, (i * NC + k) * NR + j)
        for i in range(NX)
        for k in range(NC)
        for j in range(NR)
    ]
    w_moved = lax.ppermute(
        lax.dynamic_slice(o_weight, (ic * HALF + iy * W_ROWS, 0), (W_ROWS, COLS)),
        ("x", "c", "r"),
        w_routes,
    )
    attn_keep = jnp.where(ic == 0, attn[:, :HALF], attn[:, HALF:])
    attn_give = jnp.where(ic == 0, attn[:, HALF:], attn[:, :HALF])
    attn_other = swap_core(attn_give)

    states = state.astype(f32).reshape(2, SEQ, FEAT)
    square = lax.psum(jnp.sum(states * states, -1), "t") / D
    inv_rms = lax.rsqrt(square + epsilon)
    token_count = lengths.reshape(2).astype(f32)
    valid = (jnp.arange(SEQ, dtype=jnp.int32)[None, :] < lengths.reshape(2)[:, None]).astype(f32)
    pool_weight = valid * inv_rms / token_count[:, None]
    pooled = jnp.sum(pool_weight[..., None] * states, 1)
    attn_pool = jnp.sum(pool_weight[..., None] * attn.astype(f32).reshape(2, SEQ, FEAT), 1)

    near = jnp.concatenate([pooled, norm_gain[None]], 0)
    near = lax.all_to_all(jnp.broadcast_to(near[None], (NT, 3, FEAT)), "t", 0, 0)
    pooled_row = near[:, :2].transpose(1, 0, 2).reshape(2, D)
    gain = near[:, 2].reshape(1, D)

    u_parts = attn_pool.reshape(2, NC, NX * NY, SLICE).transpose(2, 1, 0, 3)
    u_parts = u_parts.reshape(GROUP, 2, SLICE)
    extra = jnp.stack(
        [token_count, jnp.broadcast_to(positive.astype(f32), (2,))], -1
    )
    row = jnp.concatenate([pooled_row, inv_rms], -1)
    send = jnp.concatenate(
        [
            jnp.broadcast_to(row[None], (GROUP, 2, D + SEQ)),
            u_parts,
            jnp.broadcast_to(extra[None], (GROUP, 2, 2)),
            jnp.zeros((GROUP, 2, WIDTH - AT_POS - 1), f32),
        ],
        -1,
    )
    got = lax.all_to_all(send, DP, 0, 0)
    got, attn_other, w_moved = lax.optimization_barrier((got, attn_other, w_moved))

    other_index = dp_index + 1 - 2 * ic
    got, state_all = lax.optimization_barrier((got, state_all))
    state_other = swap_core(state_all)
    w_all = lax.all_gather(w_moved, PLANE).reshape(NX, HALF, COLS)
    first, gain_part, loss_part, pieces, scale, first_col = group_math(
        jnp.stack([dp_index, other_index]), got.transpose(1, 0, 2), gain
    )

    partial, coef = weight_partials(
        state_all, state_other, attn_keep, attn_other, pieces, scale
    )
    partial, first = lax.optimization_barrier((partial, first))
    spread = lax.all_to_all(partial, PLANE, 0, 0)

    gain_mine = lax.dynamic_index_in_dim(gain_part, it, 0, keepdims=False)
    tail = jnp.concatenate([gain_mine, jnp.broadcast_to(loss_part[:1, :1], (1, FEAT))], 0)
    tails = [tail]
    first_sum = lax.dynamic_index_in_dim(first, ir, 0, keepdims=False)
    for step in range(1, NR):
        outgoing = lax.dynamic_index_in_dim(first, (ir + step) % NR, 0, keepdims=False)
        arrived = lax.ppermute(
            jnp.concatenate([outgoing, tail], 0),
            "r",
            [(j, (j + step) % NR) for j in range(NR)],
        )
        first_sum = first_sum + arrived[:SLICE]
        tails.append(arrived[SLICE:])
    tails = jnp.stack(tails)
    totals = jnp.zeros((2, FEAT), f32)
    for source in range(NR):
        totals = totals + lax.dynamic_index_in_dim(
            tails, (ir - source) % NR, 0, keepdims=False
        )

    row_here = lax.dynamic_index_in_dim(pieces[0], it, 0, keepdims=False)[:6]
    row_here = row_here.astype(f32).reshape(2, 3, FEAT)
    row_here = (row_here[:, :1] + row_here[:, 1:2]) + row_here[:, 2:]
    state_grad = first_col[0].reshape(2, SEQ, 1) * row_here - states * coef[0].reshape(2, SEQ, 1)
    grad_hidden = state_grad.astype(bf16).reshape(1, 2, SEQ, FEAT)
    spread, first_sum, totals, grad_hidden = lax.optimization_barrier(
        (spread, first_sum, totals, grad_hidden)
    )
    second = lax.all_to_all(sum_senders(spread), "r", 0, 0)
    keep, give = attn_grads(
        (ir + 2 * ic).reshape(1), state_all, state_other, pieces, w_all, coef, first_col
    )
    second, keep, give = lax.optimization_barrier((second, keep, give))
    second_sum = jnp.sum(second.astype(f32), 0)
    total = first_sum - second_sum
    done = jnp.broadcast_to(total.astype(bf16)[None], (NX * NY, SLICE, COLS))
    half = lax.all_to_all(done, PLANE, 0, 0)
    arrived = swap_core(give)
    grad_attn = jnp.where(
        ic == 0, jnp.concatenate([keep, arrived], 1), jnp.concatenate([arrived, keep], 1)
    ).reshape(1, 2, SEQ, FEAT)
    half, grad_attn = lax.optimization_barrier((half, grad_attn))
    half_other = swap_core(half)
    grad_weight = join_halves(ic.reshape(1), half, half_other)
    return (grad_hidden, grad_attn, grad_weight, totals[0], totals[1, 0])


def solution(mesh):
    fine = Mesh(mesh.devices.reshape(NX, NY, NC, NT, NR), ("x", "y", "c", "t", "r"))
    pairs = ("x", "y", "c", "r")
    placed = (
        P(pairs, None, None, "t"),
        P(pairs, None, None, "t"),
        P("t", "r"),
        P("t"),
        P(pairs, None),
        P(pairs),
    )
    return jax.shard_map(
        body,
        mesh=fine,
        in_specs=placed,
        out_specs=(
            P(pairs, None, None, "t"),
            P(pairs, None, None, "t"),
            P("t", "r"),
            P("t"),
            P(),
        ),
        check_vma=False,
    )
```

```python
import jax
import jax.numpy as jnp
from jax import lax
from jax.experimental import pallas as pl
from jax.experimental.pallas import tpu as pltpu
from jax.sharding import Mesh, PartitionSpec as P

logit_scale = 20.0
grad_scale = 256.0
epsilon = 1e-06

f32 = jnp.float32
bf16 = jnp.bfloat16

NX, NY, NC, NT, NR = 4, 4, 2, 4, 4
PLANE = ("x", "y")
DP = ("x", "y", "c")

D = 3584
FEAT = D // NT
COLS = D // NR
SEQ = 128
TOK = 2 * SEQ
HALF = FEAT // NC
SLICE = HALF // (NX * NY)
W_ROWS = HALF // NY
PIECES = 16
GROUP = NX * NY * NC

AT_RMS = D
AT_U = D + SEQ
AT_LEN = AT_U + SLICE
AT_POS = AT_LEN + 1
WIDTH = D + 2 * SEQ


def swap_core(value):
    return lax.ppermute(value, "c", [(0, 1), (1, 0)])


contract_last = (((1,), (1,)), ((), ()))
contract_first = (((0,), (0,)), ((), ()))


def dot_last(left, right):
    return lax.dot_general(left, right, contract_last, preferred_element_type=f32)


def dot_exact(left, right, dims):
    return lax.dot_general(
        left, right, dims, precision=lax.Precision.HIGHEST, preferred_element_type=f32
    )


def group_kernel(
    index_ref, got_ref, gain_ref,
    first_ref, gain_out_ref, loss_ref, pieces_ref, scale_ref, column_ref, scaled_ref,
):
    gain = gain_ref[...]
    raw, unit, inv_norm = [], [], []
    for side in range(2):
        raw.append(got_ref[side, :, :D])
        embeds = raw[side] * gain
        square = jnp.sum(embeds * embeds, -1, keepdims=True)
        inv_norm.append(lax.rsqrt(square + epsilon))
        unit.append(embeds * inv_norm[side])
    logits = logit_scale * dot_exact(unit[0], unit[1], contract_last)
    log_total = jnp.log(jnp.sum(jnp.exp(logits), -1, keepdims=True))
    target = got_ref[0, :, AT_POS : AT_POS + 1]
    passage = lax.broadcasted_iota(jnp.int32, (GROUP, GROUP), 1).astype(f32)
    one_hot = jnp.where(passage == target, 1.0, 0.0)
    chosen = jnp.sum(logits * one_hot, -1, keepdims=True)
    loss = jnp.sum(log_total - chosen, 0, keepdims=True)
    loss_ref[...] = jnp.broadcast_to(loss, (8, 128))
    score_grad = grad_scale * (jnp.exp(logits - log_total) - one_hot)
    grads = (
        dot_exact(score_grad, unit[1], (((1,), (0,)), ((), ()))),
        dot_exact(score_grad, unit[0], contract_first),
    )
    gain_sum = jnp.zeros((1, D), f32)
    first = jnp.zeros((SLICE, D), f32)
    for side in range(2):
        grad = logit_scale * grads[side]
        along = jnp.sum(unit[side] * grad, -1, keepdims=True)
        pooled_grad = (grad - unit[side] * along) * inv_norm[side]
        gain_sum = gain_sum + jnp.sum(pooled_grad * raw[side], 0, keepdims=True)
        scaled = pooled_grad * gain
        scaled_ref[side] = scaled
        first = first + dot_exact(got_ref[side, :, AT_U:AT_LEN], scaled, contract_first)
    for block in range(NR):
        columns = slice(block * COLS, (block + 1) * COLS)
        first_ref[block] = first[:, columns]
        gain_out_ref[block] = gain_sum[:, columns]

    token = lax.broadcasted_iota(jnp.int32, (SEQ, SEQ), 0)
    lane = lax.broadcasted_iota(jnp.int32, (SEQ, SEQ), 1)
    position = lax.broadcasted_iota(jnp.int32, (SEQ, 1), 0).astype(f32)
    for pair in range(NC):
        index = index_ref[pair]
        chosen_row = lax.broadcasted_iota(jnp.int32, (GROUP, 1), 0) == index
        parts = []
        for side in range(2):
            row = jnp.sum(jnp.where(chosen_row, scaled_ref[side], 0.0), 0, keepdims=True)
            high = row.astype(bf16).astype(f32)
            mid = (row - high).astype(bf16).astype(f32)
            parts += [high, mid, row - high - mid]
            rest = jnp.where(chosen_row, got_ref[side, :, AT_RMS:WIDTH], 0.0)
            rest = jnp.sum(rest, 0, keepdims=True)
            rms_row = rest[:, :SEQ]
            count = rest[:, AT_LEN - AT_RMS : AT_LEN - AT_RMS + 1]
            rms = jnp.sum(jnp.where(token == lane, rms_row, 0.0), -1, keepdims=True)
            column = jnp.where(position < count, rms / count, 0.0)
            here = slice(side * SEQ, (side + 1) * SEQ)
            column_ref[pair, here, :] = column
            scale_ref[pair, here, :] = column * rms * rms * (1.0 / D)
        parts.append(jnp.zeros((PIECES - 6, D), f32))
        piece = jnp.concatenate(parts, 0).astype(bf16)
        for block in range(NR):
            pieces_ref[pair, block] = piece[:, block * COLS : (block + 1) * COLS]


def group_math(index, got, gain):
    spec = pl.BlockSpec(memory_space=pltpu.VMEM)
    return pl.pallas_call(
        group_kernel,
        out_shape=(
            jax.ShapeDtypeStruct((NR, SLICE, COLS), f32),
            jax.ShapeDtypeStruct((NR, 1, COLS), f32),
            jax.ShapeDtypeStruct((8, 128), f32),
            jax.ShapeDtypeStruct((NC, NR, PIECES, COLS), bf16),
            jax.ShapeDtypeStruct((NC, TOK, 1), f32),
            jax.ShapeDtypeStruct((NC, TOK, 1), f32),
        ),
        in_specs=[pl.BlockSpec(memory_space=pltpu.SMEM), spec, spec],
        out_specs=(spec,) * 6,
        scratch_shapes=[pltpu.VMEM((2, GROUP, D), f32)],
        compiler_params=pltpu.CompilerParams(vmem_limit_bytes=16 * 1024 * 1024),
        cost_estimate=pl.CostEstimate(
            flops=50 * GROUP * GROUP * D, bytes_accessed=3 * 1024 * 1024, transcendentals=4096
        ),
        name="group_math",
    )(index, got, gain)


def weight_kernel(
    replica_ref, own_ref, other_ref, keep_ref, given_ref, pieces_ref, scale_ref,
    far_ref, near_ref, coef_ref, acc_ref,
):
    blocks = [lax.rem(replica_ref[0] + step, NR) for step in range(NR)]
    token = lax.broadcasted_iota(jnp.int32, (TOK, PIECES), 0)
    part = lax.broadcasted_iota(jnp.int32, (TOK, PIECES), 1)
    part = part - jnp.where(token < SEQ, 0, 3)
    mask = (part >= 0) & (part < 3)
    scaled = []
    for pair, (state_ref, attn_ref) in enumerate(
        ((own_ref, keep_ref), (other_ref, given_ref))
    ):
        inner = jnp.zeros((TOK, PIECES), f32)
        for block in range(NT):
            inner = inner + dot_last(state_ref[block], pieces_ref[pair, block])
        inner = jnp.sum(jnp.where(mask, inner, 0.0), -1, keepdims=True)
        coef = scale_ref[pair] * inner
        coef_ref[pair] = coef
        scaled.append((attn_ref[...].astype(f32) * coef).astype(bf16))
    for block in range(NT):
        acc_ref[block] = lax.dot_general(
            scaled[0], own_ref[block], contract_first, preferred_element_type=f32
        ) + lax.dot_general(
            scaled[1], other_ref[block], contract_first, preferred_element_type=f32
        )
    for place in range(NX * NY):
        rows = [
            acc_ref[block, place * SLICE : (place + 1) * SLICE, :] for block in blocks
        ]
        near_ref[place] = rows[0].astype(bf16)
        far_ref[place] = jnp.concatenate(rows[1:], 0).astype(bf16)


def weight_partials(replica, own, other, keep, given, pieces, scale):
    spec = pl.BlockSpec(memory_space=pltpu.VMEM)
    return pl.pallas_call(
        weight_kernel,
        out_shape=(
            jax.ShapeDtypeStruct((NX * NY, (NR - 1) * SLICE, COLS), bf16),
            jax.ShapeDtypeStruct((NX * NY, SLICE, COLS), bf16),
            jax.ShapeDtypeStruct((NC, TOK, 1), f32),
        ),
        in_specs=[pl.BlockSpec(memory_space=pltpu.SMEM)] + [spec] * 6,
        out_specs=(spec,) * 3,
        scratch_shapes=[pltpu.VMEM((NR, HALF, COLS), f32)],
        compiler_params=pltpu.CompilerParams(vmem_limit_bytes=24 * 1024 * 1024),
        cost_estimate=pl.CostEstimate(
            flops=4 * TOK * HALF * D, bytes_accessed=8 * 1024 * 1024, transcendentals=0
        ),
        name="weight_partials",
    )(replica, own, other, keep, given, pieces, scale)


def sum_kernel(spread_ref, out_ref, acc_ref):
    step = pl.program_id(0)
    part = spread_ref[0].astype(f32)
    for place in range(1, spread_ref.shape[0]):
        part = part + spread_ref[place].astype(f32)

    @pl.when(step == 0)
    def _():
        acc_ref[...] = part

    @pl.when(step > 0)
    def _():
        acc_ref[...] += part

    @pl.when(step == NX - 1)
    def _():
        for block in range(NR - 1):
            out_ref[block] = acc_ref[block * SLICE : (block + 1) * SLICE, :].astype(bf16)


def sum_senders(spread):
    return pl.pallas_call(
        sum_kernel,
        grid=(NX,),
        out_shape=jax.ShapeDtypeStruct((NR - 1, SLICE, COLS), bf16),
        in_specs=[pl.BlockSpec((NY, (NR - 1) * SLICE, COLS), lambda step: (step, 0, 0))],
        out_specs=pl.BlockSpec((NR - 1, SLICE, COLS), lambda step: (0, 0, 0)),
        scratch_shapes=[pltpu.VMEM(((NR - 1) * SLICE, COLS), f32)],
        compiler_params=pltpu.CompilerParams(vmem_limit_bytes=16 * 1024 * 1024),
        cost_estimate=pl.CostEstimate(
            flops=NX * NY * NR * SLICE * COLS, bytes_accessed=4 * 1024 * 1024, transcendentals=0
        ),
        name="sum_senders",
    )(spread)


def join_kernel(core_ref, mine_ref, other_ref, out_ref):
    core = core_ref[0]
    for which, ref in ((core, mine_ref), (1 - core, other_ref)):
        rows = [ref[place].astype(f32) for place in range(NX * NY)]
        out_ref[pl.ds(pl.multiple_of(which * HALF, HALF), HALF), :] = jnp.concatenate(
            rows, 0
        ).astype(bf16)


def join_halves(core, mine, other):
    spec = pl.BlockSpec(memory_space=pltpu.VMEM)
    return pl.pallas_call(
        join_kernel,
        out_shape=jax.ShapeDtypeStruct((FEAT, COLS), bf16),
        in_specs=[pl.BlockSpec(memory_space=pltpu.SMEM), spec, spec],
        out_specs=spec,
        compiler_params=pltpu.CompilerParams(vmem_limit_bytes=16 * 1024 * 1024),
        cost_estimate=pl.CostEstimate(
            flops=0, bytes_accessed=4 * 1024 * 1024, transcendentals=0
        ),
        name="join_halves",
    )(core, mine, other)


def attn_kernel(
    shift_ref, own_hbm, other_hbm, pieces_ref, w_hbm, coef_ref, first_ref, keep_ref, give_ref,
    state_ref, w_ref, state_sems, w_sems,
):
    shift = shift_ref[0]
    columns = w_ref.shape[1]
    loads = []
    for block in range(NX):
        which = lax.rem(shift + block, NR)
        loads.append(
            [pltpu.make_async_copy(w_hbm.at[block], w_ref.at[block], w_sems.at[block])]
            + [
                pltpu.make_async_copy(
                    source.at[which],
                    state_ref.at[pair * NX + block],
                    state_sems.at[pair * NX + block],
                )
                for pair, source in enumerate((own_hbm, other_hbm))
            ]
        )
        for load in loads[block]:
            load.start()
    tokens = [jnp.zeros((TOK, columns), f32) for pair in range(NC)]
    rows = [jnp.zeros((PIECES, columns), f32) for pair in range(NC)]
    for block in range(NX):
        which = lax.rem(shift + block, NR)
        for load in loads[block]:
            load.wait()
        for pair in range(NC):
            tokens[pair] = tokens[pair] + dot_last(state_ref[pair * NX + block], w_ref[block])
            rows[pair] = rows[pair] + dot_last(pieces_ref[pair, which], w_ref[block])
    for pair, out_ref in enumerate((keep_ref, give_ref)):
        for side in range(2):
            at = 3 * side
            row = rows[pair][at + 2 : at + 3] + rows[pair][at + 1 : at + 2]
            row = row + rows[pair][at : at + 1]
            here = slice(side * SEQ, (side + 1) * SEQ)
            out_ref[here, :] = (
                first_ref[pair, here, :] * row - coef_ref[pair, here, :] * tokens[pair][here]
            ).astype(bf16)


def attn_grads(shift, own, other, pieces, w_all, coef, first):
    spec = pl.BlockSpec(memory_space=pltpu.VMEM)
    hbm = pl.BlockSpec(memory_space=pltpu.HBM)
    columns = w_all.shape[1]
    out = jax.ShapeDtypeStruct((TOK, columns), bf16)
    return pl.pallas_call(
        attn_kernel,
        out_shape=(out, out),
        in_specs=[pl.BlockSpec(memory_space=pltpu.SMEM), hbm, hbm, spec, hbm, spec, spec],
        out_specs=(spec, spec),
        scratch_shapes=[
            pltpu.VMEM((NC * NX, TOK, FEAT), bf16),
            pltpu.VMEM((NX, columns, COLS), bf16),
            pltpu.SemaphoreType.DMA((NC * NX,)),
            pltpu.SemaphoreType.DMA((NX,)),
        ],
        compiler_params=pltpu.CompilerParams(vmem_limit_bytes=58 * 1024 * 1024),
        cost_estimate=pl.CostEstimate(
            flops=4 * TOK * columns * D, bytes_accessed=8 * 1024 * 1024, transcendentals=0
        ),
        name="attn_grads",
    )(shift, own, other, pieces, w_all, coef, first)


def body(hidden_state, attn_out, o_weight, norm_gain, lengths, positive):
    ix, iy, ic = lax.axis_index("x"), lax.axis_index("y"), lax.axis_index("c")
    it, ir = lax.axis_index("t"), lax.axis_index("r")
    dp_index = (ix * NY + iy) * NC + ic

    state = hidden_state.reshape(TOK, FEAT)
    attn = attn_out.reshape(TOK, FEAT)
    state_all = lax.all_gather(state, "t")
    w_routes = [
        ((i * NC + k) * NR + (j + i + 2 * k) % NR, (i * NC + k) * NR + j)
        for i in range(NX)
        for k in range(NC)
        for j in range(NR)
    ]
    w_moved = lax.ppermute(
        lax.dynamic_slice(o_weight, (ic * HALF + iy * W_ROWS, 0), (W_ROWS, COLS)),
        ("x", "c", "r"),
        w_routes,
    )
    attn_keep = jnp.where(ic == 0, attn[:, :HALF], attn[:, HALF:])
    attn_give = jnp.where(ic == 0, attn[:, HALF:], attn[:, :HALF])
    attn_other = swap_core(attn_give)

    states = state.astype(f32).reshape(2, SEQ, FEAT)
    square = lax.psum(jnp.sum(states * states, -1), "t") / D
    inv_rms = lax.rsqrt(square + epsilon)
    token_count = lengths.reshape(2).astype(f32)
    valid = (jnp.arange(SEQ, dtype=jnp.int32)[None, :] < lengths.reshape(2)[:, None]).astype(f32)
    pool_weight = valid * inv_rms / token_count[:, None]
    pooled = jnp.sum(pool_weight[..., None] * states, 1)
    attn_pool = jnp.sum(pool_weight[..., None] * attn.astype(f32).reshape(2, SEQ, FEAT), 1)

    near = jnp.concatenate([pooled, norm_gain[None]], 0)
    near = lax.all_to_all(jnp.broadcast_to(near[None], (NT, 3, FEAT)), "t", 0, 0)
    pooled_row = near[:, :2].transpose(1, 0, 2).reshape(2, D)
    gain = near[:, 2].reshape(1, D)

    u_parts = attn_pool.reshape(2, NC, NX * NY, SLICE).transpose(2, 1, 0, 3)
    u_parts = u_parts.reshape(GROUP, 2, SLICE)
    extra = jnp.stack(
        [token_count, jnp.broadcast_to(positive.astype(f32), (2,))], -1
    )
    row = jnp.concatenate([pooled_row, inv_rms], -1)
    send = jnp.concatenate(
        [
            jnp.broadcast_to(row[None], (GROUP, 2, D + SEQ)),
            u_parts,
            jnp.broadcast_to(extra[None], (GROUP, 2, 2)),
            jnp.zeros((GROUP, 2, WIDTH - AT_POS - 1), f32),
        ],
        -1,
    )
    got = lax.all_to_all(send, DP, 0, 0)
    got, attn_other, w_moved = lax.optimization_barrier((got, attn_other, w_moved))

    other_index = dp_index + 1 - 2 * ic
    got, state_all = lax.optimization_barrier((got, state_all))
    state_other = swap_core(state_all)
    w_all = lax.all_gather(w_moved, PLANE).reshape(NX, HALF, COLS)
    first, gain_part, loss_part, pieces, scale, first_col = group_math(
        jnp.stack([dp_index, other_index]), got.transpose(1, 0, 2), gain
    )

    far, near_part, coef = weight_partials(
        ir.reshape(1), state_all, state_other, attn_keep, attn_other, pieces, scale
    )
    far, first = lax.optimization_barrier((far, first))
    far = lax.all_to_all(far, PLANE, 0, 0)

    gain_mine = lax.dynamic_index_in_dim(gain_part, it, 0, keepdims=False)
    tail = jnp.concatenate([gain_mine, jnp.broadcast_to(loss_part[:1, :1], (1, FEAT))], 0)
    tails = [tail]
    first_sum = lax.dynamic_index_in_dim(first, ir, 0, keepdims=False)
    for step in range(1, NR):
        outgoing = lax.dynamic_index_in_dim(first, (ir + step) % NR, 0, keepdims=False)
        arrived = lax.ppermute(
            jnp.concatenate([outgoing, tail], 0),
            "r",
            [(j, (j + step) % NR) for j in range(NR)],
        )
        first_sum = first_sum + arrived[:SLICE]
        tails.append(arrived[SLICE:])
    tails = jnp.stack(tails)
    totals = jnp.zeros((2, FEAT), f32)
    for source in range(NR):
        totals = totals + lax.dynamic_index_in_dim(
            tails, (ir - source) % NR, 0, keepdims=False
        )

    row_here = lax.dynamic_index_in_dim(pieces[0], it, 0, keepdims=False)[:6]
    row_here = row_here.astype(f32).reshape(2, 3, FEAT)
    row_here = (row_here[:, :1] + row_here[:, 1:2]) + row_here[:, 2:]
    state_grad = first_col[0].reshape(2, SEQ, 1) * row_here - states * coef[0].reshape(2, SEQ, 1)
    grad_hidden = state_grad.astype(bf16).reshape(1, 2, SEQ, FEAT)
    far, near_part, first_sum, totals, grad_hidden = lax.optimization_barrier(
        (far, near_part, first_sum, totals, grad_hidden)
    )
    near_part = lax.all_to_all(near_part, PLANE, 0, 0)
    far = sum_senders(far)
    second_sum = jnp.sum(near_part.astype(f32), 0)
    for step in range(1, NR):
        second_sum = second_sum + lax.ppermute(
            far[step - 1], "r", [(j, (j + step) % NR) for j in range(NR)]
        ).astype(f32)
    total = first_sum - second_sum
    done = jnp.broadcast_to(total.astype(bf16)[None], (NX * NY, SLICE, COLS))
    half = lax.all_to_all(done, PLANE, 0, 0)
    keep, give = attn_grads(
        (ir + 2 * ic).reshape(1), state_all, state_other, pieces, w_all, coef, first_col
    )
    half, keep, give = lax.optimization_barrier((half, keep, give))
    half_other = swap_core(half)
    arrived = swap_core(give)
    grad_attn = jnp.where(
        ic == 0, jnp.concatenate([keep, arrived], 1), jnp.concatenate([arrived, keep], 1)
    ).reshape(1, 2, SEQ, FEAT)
    grad_weight = join_halves(ic.reshape(1), half, half_other)
    return (grad_hidden, grad_attn, grad_weight, totals[0], totals[1, 0])


def solution(mesh):
    fine = Mesh(mesh.devices.reshape(NX, NY, NC, NT, NR), ("x", "y", "c", "t", "r"))
    pairs = ("x", "y", "c", "r")
    placed = (
        P(pairs, None, None, "t"),
        P(pairs, None, None, "t"),
        P("t", "r"),
        P("t"),
        P(pairs, None),
        P(pairs),
    )
    return jax.shard_map(
        body,
        mesh=fine,
        in_specs=placed,
        out_specs=(
            P(pairs, None, None, "t"),
            P(pairs, None, None, "t"),
            P("t", "r"),
            P("t"),
            P(),
        ),
        check_vma=False,
    )
```

```python
import jax
import jax.numpy as jnp
from jax import lax
from jax.experimental import pallas as pl
from jax.experimental.pallas import tpu as pltpu
from jax.sharding import Mesh, PartitionSpec as P

logit_scale = 20.0
grad_scale = 256.0
epsilon = 1e-06

f32 = jnp.float32
bf16 = jnp.bfloat16

NX, NY, NC, NT, NR = 4, 4, 2, 4, 4
PLANE = ("x", "y")
DP = ("x", "y", "c")

D = 3584
FEAT = D // NT
COLS = D // NR
SEQ = 128
TOK = 2 * SEQ
HALF = FEAT // NC
SLICE = HALF // (NX * NY)
W_ROWS = HALF // NY
PIECES = 16
GROUP = NX * NY * NC

AT_RMS = D
AT_U = D + SEQ
AT_LEN = AT_U + SLICE
AT_POS = AT_LEN + 1
WIDTH = D + 2 * SEQ


def swap_core(value):
    return lax.ppermute(value, "c", [(0, 1), (1, 0)])


contract_last = (((1,), (1,)), ((), ()))
contract_first = (((0,), (0,)), ((), ()))


def dot_last(left, right):
    return lax.dot_general(left, right, contract_last, preferred_element_type=f32)


def dot_exact(left, right, dims):
    return lax.dot_general(
        left, right, dims, precision=lax.Precision.HIGHEST, preferred_element_type=f32
    )


def group_kernel(
    index_ref, got_ref, gain_ref,
    first_ref, gain_out_ref, loss_ref, pieces_ref, scale_ref, column_ref, scaled_ref,
):
    gain = gain_ref[...]
    raw, unit, inv_norm = [], [], []
    for side in range(2):
        raw.append(got_ref[side, :, :D])
        embeds = raw[side] * gain
        square = jnp.sum(embeds * embeds, -1, keepdims=True)
        inv_norm.append(lax.rsqrt(square + epsilon))
        unit.append(embeds * inv_norm[side])
    logits = logit_scale * dot_exact(unit[0], unit[1], contract_last)
    log_total = jnp.log(jnp.sum(jnp.exp(logits), -1, keepdims=True))
    target = got_ref[0, :, AT_POS : AT_POS + 1]
    passage = lax.broadcasted_iota(jnp.int32, (GROUP, GROUP), 1).astype(f32)
    one_hot = jnp.where(passage == target, 1.0, 0.0)
    chosen = jnp.sum(logits * one_hot, -1, keepdims=True)
    loss = jnp.sum(log_total - chosen, 0, keepdims=True)
    loss_ref[...] = jnp.broadcast_to(loss, (8, 128))
    score_grad = grad_scale * (jnp.exp(logits - log_total) - one_hot)
    grads = (
        dot_exact(score_grad, unit[1], (((1,), (0,)), ((), ()))),
        dot_exact(score_grad, unit[0], contract_first),
    )
    gain_sum = jnp.zeros((1, D), f32)
    first = jnp.zeros((SLICE, D), f32)
    for side in range(2):
        grad = logit_scale * grads[side]
        along = jnp.sum(unit[side] * grad, -1, keepdims=True)
        pooled_grad = (grad - unit[side] * along) * inv_norm[side]
        gain_sum = gain_sum + jnp.sum(pooled_grad * raw[side], 0, keepdims=True)
        scaled = pooled_grad * gain
        scaled_ref[side] = scaled
        first = first + dot_exact(got_ref[side, :, AT_U:AT_LEN], scaled, contract_first)
    for block in range(NR):
        columns = slice(block * COLS, (block + 1) * COLS)
        first_ref[block] = first[:, columns]
        gain_out_ref[block] = gain_sum[:, columns]

    token = lax.broadcasted_iota(jnp.int32, (SEQ, SEQ), 0)
    lane = lax.broadcasted_iota(jnp.int32, (SEQ, SEQ), 1)
    position = lax.broadcasted_iota(jnp.int32, (SEQ, 1), 0).astype(f32)
    for pair in range(NC):
        index = index_ref[pair]
        chosen_row = lax.broadcasted_iota(jnp.int32, (GROUP, 1), 0) == index
        parts = []
        for side in range(2):
            row = jnp.sum(jnp.where(chosen_row, scaled_ref[side], 0.0), 0, keepdims=True)
            high = row.astype(bf16).astype(f32)
            mid = (row - high).astype(bf16).astype(f32)
            parts += [high, mid, row - high - mid]
            rest = jnp.where(chosen_row, got_ref[side, :, AT_RMS:WIDTH], 0.0)
            rest = jnp.sum(rest, 0, keepdims=True)
            rms_row = rest[:, :SEQ]
            count = rest[:, AT_LEN - AT_RMS : AT_LEN - AT_RMS + 1]
            rms = jnp.sum(jnp.where(token == lane, rms_row, 0.0), -1, keepdims=True)
            column = jnp.where(position < count, rms / count, 0.0)
            here = slice(side * SEQ, (side + 1) * SEQ)
            column_ref[pair, here, :] = column
            scale_ref[pair, here, :] = column * rms * rms * (1.0 / D)
        parts.append(jnp.zeros((PIECES - 6, D), f32))
        piece = jnp.concatenate(parts, 0).astype(bf16)
        for block in range(NR):
            pieces_ref[pair, block] = piece[:, block * COLS : (block + 1) * COLS]


def group_math(index, got, gain):
    spec = pl.BlockSpec(memory_space=pltpu.VMEM)
    return pl.pallas_call(
        group_kernel,
        out_shape=(
            jax.ShapeDtypeStruct((NR, SLICE, COLS), f32),
            jax.ShapeDtypeStruct((NR, 1, COLS), f32),
            jax.ShapeDtypeStruct((8, 128), f32),
            jax.ShapeDtypeStruct((NC, NR, PIECES, COLS), bf16),
            jax.ShapeDtypeStruct((NC, TOK, 1), f32),
            jax.ShapeDtypeStruct((NC, TOK, 1), f32),
        ),
        in_specs=[pl.BlockSpec(memory_space=pltpu.SMEM), spec, spec],
        out_specs=(spec,) * 6,
        scratch_shapes=[pltpu.VMEM((2, GROUP, D), f32)],
        compiler_params=pltpu.CompilerParams(vmem_limit_bytes=16 * 1024 * 1024),
        cost_estimate=pl.CostEstimate(
            flops=50 * GROUP * GROUP * D, bytes_accessed=3 * 1024 * 1024, transcendentals=4096
        ),
        name="group_math",
    )(index, got, gain)


def weight_kernel(
    own_ref, other_ref, keep_ref, given_ref, pieces_ref, scale_ref, out_ref, coef_ref, acc_ref
):
    token = lax.broadcasted_iota(jnp.int32, (TOK, PIECES), 0)
    part = lax.broadcasted_iota(jnp.int32, (TOK, PIECES), 1)
    part = part - jnp.where(token < SEQ, 0, 3)
    mask = (part >= 0) & (part < 3)
    scaled = []
    for pair, (state_ref, attn_ref) in enumerate(
        ((own_ref, keep_ref), (other_ref, given_ref))
    ):
        inner = jnp.zeros((TOK, PIECES), f32)
        for block in range(NT):
            inner = inner + dot_last(state_ref[block], pieces_ref[pair, block])
        inner = jnp.sum(jnp.where(mask, inner, 0.0), -1, keepdims=True)
        coef = scale_ref[pair] * inner
        coef_ref[pair] = coef
        scaled.append((attn_ref[...].astype(f32) * coef).astype(bf16))
    for block in range(NT):
        acc_ref[block] = lax.dot_general(
            scaled[0], own_ref[block], contract_first, preferred_element_type=f32
        ) + lax.dot_general(
            scaled[1], other_ref[block], contract_first, preferred_element_type=f32
        )
    for place in range(NX * NY):
        rows = [
            acc_ref[block, place * SLICE : (place + 1) * SLICE, :] for block in range(NR)
        ]
        out_ref[place] = jnp.concatenate(rows, 0).astype(bf16)


def weight_partials(own, other, keep, given, pieces, scale):
    spec = pl.BlockSpec(memory_space=pltpu.VMEM)
    return pl.pallas_call(
        weight_kernel,
        out_shape=(
            jax.ShapeDtypeStruct((NX * NY, NR * SLICE, COLS), bf16),
            jax.ShapeDtypeStruct((NC, TOK, 1), f32),
        ),
        in_specs=[spec] * 6,
        out_specs=(spec, spec),
        scratch_shapes=[pltpu.VMEM((NR, HALF, COLS), f32)],
        compiler_params=pltpu.CompilerParams(vmem_limit_bytes=24 * 1024 * 1024),
        cost_estimate=pl.CostEstimate(
            flops=4 * TOK * HALF * D, bytes_accessed=8 * 1024 * 1024, transcendentals=0
        ),
        name="weight_partials",
    )(own, other, keep, given, pieces, scale)


def sum_kernel(spread_ref, out_ref, acc_ref):
    step = pl.program_id(0)
    part = spread_ref[0].astype(f32)
    for place in range(1, spread_ref.shape[0]):
        part = part + spread_ref[place].astype(f32)

    @pl.when(step == 0)
    def _():
        acc_ref[...] = part

    @pl.when(step > 0)
    def _():
        acc_ref[...] += part

    @pl.when(step == NX - 1)
    def _():
        for block in range(NR):
            out_ref[block] = acc_ref[block * SLICE : (block + 1) * SLICE, :].astype(bf16)


def sum_senders(spread):
    return pl.pallas_call(
        sum_kernel,
        grid=(NX,),
        out_shape=jax.ShapeDtypeStruct((NR, SLICE, COLS), bf16),
        in_specs=[pl.BlockSpec((NY, NR * SLICE, COLS), lambda step: (step, 0, 0))],
        out_specs=pl.BlockSpec((NR, SLICE, COLS), lambda step: (0, 0, 0)),
        scratch_shapes=[pltpu.VMEM((NR * SLICE, COLS), f32)],
        compiler_params=pltpu.CompilerParams(vmem_limit_bytes=16 * 1024 * 1024),
        cost_estimate=pl.CostEstimate(
            flops=NX * NY * NR * SLICE * COLS, bytes_accessed=4 * 1024 * 1024, transcendentals=0
        ),
        name="sum_senders",
    )(spread)


def join_kernel(core_ref, mine_ref, other_ref, out_ref):
    core = core_ref[0]
    for which, ref in ((core, mine_ref), (1 - core, other_ref)):
        rows = [ref[place].astype(f32) for place in range(NX * NY)]
        out_ref[pl.ds(pl.multiple_of(which * HALF, HALF), HALF), :] = jnp.concatenate(
            rows, 0
        ).astype(bf16)


def join_halves(core, mine, other):
    spec = pl.BlockSpec(memory_space=pltpu.VMEM)
    return pl.pallas_call(
        join_kernel,
        out_shape=jax.ShapeDtypeStruct((FEAT, COLS), bf16),
        in_specs=[pl.BlockSpec(memory_space=pltpu.SMEM), spec, spec],
        out_specs=spec,
        compiler_params=pltpu.CompilerParams(vmem_limit_bytes=16 * 1024 * 1024),
        cost_estimate=pl.CostEstimate(
            flops=0, bytes_accessed=4 * 1024 * 1024, transcendentals=0
        ),
        name="join_halves",
    )(core, mine, other)


def attn_kernel(
    shift_ref, own_hbm, other_hbm, pieces_ref, w_hbm, coef_ref, first_ref, keep_ref, give_ref,
    state_ref, w_ref, state_sems, w_sems,
):
    shift = shift_ref[0]
    columns = w_ref.shape[1]
    loads = []
    for block in range(NX):
        which = lax.rem(shift + block, NR)
        loads.append(
            [pltpu.make_async_copy(w_hbm.at[block], w_ref.at[block], w_sems.at[block])]
            + [
                pltpu.make_async_copy(
                    source.at[which],
                    state_ref.at[pair * NX + block],
                    state_sems.at[pair * NX + block],
                )
                for pair, source in enumerate((own_hbm, other_hbm))
            ]
        )
        for load in loads[block]:
            load.start()
    tokens = [jnp.zeros((TOK, columns), f32) for pair in range(NC)]
    rows = [jnp.zeros((PIECES, columns), f32) for pair in range(NC)]
    for block in range(NX):
        which = lax.rem(shift + block, NR)
        for load in loads[block]:
            load.wait()
        for pair in range(NC):
            tokens[pair] = tokens[pair] + dot_last(state_ref[pair * NX + block], w_ref[block])
            rows[pair] = rows[pair] + dot_last(pieces_ref[pair, which], w_ref[block])
    for pair, out_ref in enumerate((keep_ref, give_ref)):
        for side in range(2):
            at = 3 * side
            row = rows[pair][at + 2 : at + 3] + rows[pair][at + 1 : at + 2]
            row = row + rows[pair][at : at + 1]
            here = slice(side * SEQ, (side + 1) * SEQ)
            out_ref[here, :] = (
                first_ref[pair, here, :] * row - coef_ref[pair, here, :] * tokens[pair][here]
            ).astype(bf16)


def attn_grads(shift, own, other, pieces, w_all, coef, first):
    spec = pl.BlockSpec(memory_space=pltpu.VMEM)
    hbm = pl.BlockSpec(memory_space=pltpu.HBM)
    columns = w_all.shape[1]
    out = jax.ShapeDtypeStruct((TOK, columns), bf16)
    return pl.pallas_call(
        attn_kernel,
        out_shape=(out, out),
        in_specs=[pl.BlockSpec(memory_space=pltpu.SMEM), hbm, hbm, spec, hbm, spec, spec],
        out_specs=(spec, spec),
        scratch_shapes=[
            pltpu.VMEM((NC * NX, TOK, FEAT), bf16),
            pltpu.VMEM((NX, columns, COLS), bf16),
            pltpu.SemaphoreType.DMA((NC * NX,)),
            pltpu.SemaphoreType.DMA((NX,)),
        ],
        compiler_params=pltpu.CompilerParams(vmem_limit_bytes=58 * 1024 * 1024),
        cost_estimate=pl.CostEstimate(
            flops=4 * TOK * columns * D, bytes_accessed=8 * 1024 * 1024, transcendentals=0
        ),
        name="attn_grads",
    )(shift, own, other, pieces, w_all, coef, first)


def body(hidden_state, attn_out, o_weight, norm_gain, lengths, positive):
    ix, iy, ic = lax.axis_index("x"), lax.axis_index("y"), lax.axis_index("c")
    it, ir = lax.axis_index("t"), lax.axis_index("r")
    dp_index = (ix * NY + iy) * NC + ic

    state = hidden_state.reshape(TOK, FEAT)
    attn = attn_out.reshape(TOK, FEAT)
    state_all = lax.all_gather(state, "t")
    w_routes = [
        ((i * NC + k) * NR + (j + i + 2 * k) % NR, (i * NC + k) * NR + j)
        for i in range(NX)
        for k in range(NC)
        for j in range(NR)
    ]
    w_moved = lax.ppermute(
        lax.dynamic_slice(o_weight, (ic * HALF + iy * W_ROWS, 0), (W_ROWS, COLS)),
        ("x", "c", "r"),
        w_routes,
    )
    attn_keep = jnp.where(ic == 0, attn[:, :HALF], attn[:, HALF:])
    attn_give = jnp.where(ic == 0, attn[:, HALF:], attn[:, :HALF])
    attn_other = swap_core(attn_give)

    states = state.astype(f32).reshape(2, SEQ, FEAT)
    square = lax.psum(jnp.sum(states * states, -1), "t") / D
    inv_rms = lax.rsqrt(square + epsilon)
    token_count = lengths.reshape(2).astype(f32)
    valid = (jnp.arange(SEQ, dtype=jnp.int32)[None, :] < lengths.reshape(2)[:, None]).astype(f32)
    pool_weight = valid * inv_rms / token_count[:, None]
    pooled = jnp.sum(pool_weight[..., None] * states, 1)
    attn_pool = jnp.sum(pool_weight[..., None] * attn.astype(f32).reshape(2, SEQ, FEAT), 1)

    near = jnp.concatenate([pooled, norm_gain[None]], 0)
    near = lax.all_to_all(jnp.broadcast_to(near[None], (NT, 3, FEAT)), "t", 0, 0)
    pooled_row = near[:, :2].transpose(1, 0, 2).reshape(2, D)
    gain = near[:, 2].reshape(1, D)

    u_parts = attn_pool.reshape(2, NC, NX * NY, SLICE).transpose(2, 1, 0, 3)
    u_parts = u_parts.reshape(GROUP, 2, SLICE)
    extra = jnp.stack(
        [token_count, jnp.broadcast_to(positive.astype(f32), (2,))], -1
    )
    row = jnp.concatenate([pooled_row, inv_rms], -1)
    send = jnp.concatenate(
        [
            jnp.broadcast_to(row[None], (GROUP, 2, D + SEQ)),
            u_parts,
            jnp.broadcast_to(extra[None], (GROUP, 2, 2)),
            jnp.zeros((GROUP, 2, WIDTH - AT_POS - 1), f32),
        ],
        -1,
    )
    got = lax.all_to_all(send, DP, 0, 0)
    got, attn_other = lax.optimization_barrier((got, attn_other))

    other_index = dp_index + 1 - 2 * ic
    got, state_all = lax.optimization_barrier((got, state_all))
    state_other = swap_core(state_all)
    first, gain_part, loss_part, pieces, scale, first_col = group_math(
        jnp.stack([dp_index, other_index]), got.transpose(1, 0, 2), gain
    )

    partial, coef = weight_partials(
        state_all, state_other, attn_keep, attn_other, pieces, scale
    )
    partial, first, w_moved = lax.optimization_barrier((partial, first, w_moved))
    w_all = lax.all_gather(w_moved, PLANE).reshape(NX, HALF, COLS)
    spread = lax.all_to_all(partial, PLANE, 0, 0)

    gain_mine = lax.dynamic_index_in_dim(gain_part, it, 0, keepdims=False)
    tail = jnp.concatenate([gain_mine, jnp.broadcast_to(loss_part[:1, :1], (1, FEAT))], 0)
    tails = [tail]
    first_sum = lax.dynamic_index_in_dim(first, ir, 0, keepdims=False)
    for step in range(1, NR):
        outgoing = lax.dynamic_index_in_dim(first, (ir + step) % NR, 0, keepdims=False)
        arrived = lax.ppermute(
            jnp.concatenate([outgoing, tail], 0),
            "r",
            [(j, (j + step) % NR) for j in range(NR)],
        )
        first_sum = first_sum + arrived[:SLICE]
        tails.append(arrived[SLICE:])
    tails = jnp.stack(tails)
    totals = jnp.zeros((2, FEAT), f32)
    for source in range(NR):
        totals = totals + lax.dynamic_index_in_dim(
            tails, (ir - source) % NR, 0, keepdims=False
        )

    row_here = lax.dynamic_index_in_dim(pieces[0], it, 0, keepdims=False)[:6]
    row_here = row_here.astype(f32).reshape(2, 3, FEAT)
    row_here = (row_here[:, :1] + row_here[:, 1:2]) + row_here[:, 2:]
    state_grad = first_col[0].reshape(2, SEQ, 1) * row_here - states * coef[0].reshape(2, SEQ, 1)
    grad_hidden = state_grad.astype(bf16).reshape(1, 2, SEQ, FEAT)
    spread, first_sum, totals, grad_hidden = lax.optimization_barrier(
        (spread, first_sum, totals, grad_hidden)
    )
    second = lax.all_to_all(sum_senders(spread), "r", 0, 0)
    second_sum = jnp.sum(second.astype(f32), 0)
    total = first_sum - second_sum
    done = jnp.broadcast_to(total.astype(bf16)[None], (NX * NY, SLICE, COLS))
    half = lax.all_to_all(done, PLANE, 0, 0)
    keep, give = attn_grads(
        (ir + 2 * ic).reshape(1), state_all, state_other, pieces, w_all, coef, first_col
    )
    half, keep, give = lax.optimization_barrier((half, keep, give))
    half_other = swap_core(half)
    arrived = swap_core(give)
    grad_attn = jnp.where(
        ic == 0, jnp.concatenate([keep, arrived], 1), jnp.concatenate([arrived, keep], 1)
    ).reshape(1, 2, SEQ, FEAT)
    grad_weight = join_halves(ic.reshape(1), half, half_other)
    return (grad_hidden, grad_attn, grad_weight, totals[0], totals[1, 0])


def solution(mesh):
    fine = Mesh(mesh.devices.reshape(NX, NY, NC, NT, NR), ("x", "y", "c", "t", "r"))
    pairs = ("x", "y", "c", "r")
    placed = (
        P(pairs, None, None, "t"),
        P(pairs, None, None, "t"),
        P("t", "r"),
        P("t"),
        P(pairs, None),
        P(pairs),
    )
    return jax.shard_map(
        body,
        mesh=fine,
        in_specs=placed,
        out_specs=(
            P(pairs, None, None, "t"),
            P(pairs, None, None, "t"),
            P("t", "r"),
            P("t"),
            P(),
        ),
        check_vma=False,
    )
```

```python
import jax
import jax.numpy as jnp
from jax import lax
from jax.experimental import pallas as pl
from jax.experimental.pallas import tpu as pltpu
from jax.sharding import Mesh, PartitionSpec as P

logit_scale = 20.0
grad_scale = 256.0
epsilon = 1e-06

f32 = jnp.float32
bf16 = jnp.bfloat16

NX, NY, NC, NT, NR = 4, 4, 2, 4, 4
PLANE = ("x", "y")
DP = ("x", "y", "c")

D = 3584
FEAT = D // NT
COLS = D // NR
SEQ = 128
TOK = 2 * SEQ
HALF = FEAT // NC
SLICE = HALF // (NX * NY)
W_ROWS = HALF // NY
PIECES = 16
GROUP = NX * NY * NC

AT_RMS = D
AT_U = D + SEQ
AT_LEN = AT_U + SLICE
AT_POS = AT_LEN + 1
WIDTH = D + 2 * SEQ


def swap_core(value):
    return lax.ppermute(value, "c", [(0, 1), (1, 0)])


contract_last = (((1,), (1,)), ((), ()))
contract_first = (((0,), (0,)), ((), ()))


def dot_last(left, right):
    return lax.dot_general(left, right, contract_last, preferred_element_type=f32)


def dot_exact(left, right, dims):
    return lax.dot_general(
        left, right, dims, precision=lax.Precision.HIGHEST, preferred_element_type=f32
    )


def group_kernel(
    index_ref, got_ref, gain_ref,
    first_ref, gain_out_ref, loss_ref, pieces_ref, scale_ref, column_ref, scaled_ref,
):
    gain = gain_ref[...]
    raw, unit, inv_norm = [], [], []
    for side in range(2):
        raw.append(got_ref[side, :, :D])
        embeds = raw[side] * gain
        square = jnp.sum(embeds * embeds, -1, keepdims=True)
        inv_norm.append(lax.rsqrt(square + epsilon))
        unit.append(embeds * inv_norm[side])
    logits = logit_scale * dot_exact(unit[0], unit[1], contract_last)
    log_total = jnp.log(jnp.sum(jnp.exp(logits), -1, keepdims=True))
    target = got_ref[0, :, AT_POS : AT_POS + 1]
    passage = lax.broadcasted_iota(jnp.int32, (GROUP, GROUP), 1).astype(f32)
    one_hot = jnp.where(passage == target, 1.0, 0.0)
    chosen = jnp.sum(logits * one_hot, -1, keepdims=True)
    loss = jnp.sum(log_total - chosen, 0, keepdims=True)
    loss_ref[...] = jnp.broadcast_to(loss, (8, 128))
    score_grad = grad_scale * (jnp.exp(logits - log_total) - one_hot)
    grads = (
        dot_exact(score_grad, unit[1], (((1,), (0,)), ((), ()))),
        dot_exact(score_grad, unit[0], contract_first),
    )
    gain_sum = jnp.zeros((1, D), f32)
    first = jnp.zeros((SLICE, D), f32)
    for side in range(2):
        grad = logit_scale * grads[side]
        along = jnp.sum(unit[side] * grad, -1, keepdims=True)
        pooled_grad = (grad - unit[side] * along) * inv_norm[side]
        gain_sum = gain_sum + jnp.sum(pooled_grad * raw[side], 0, keepdims=True)
        scaled = pooled_grad * gain
        scaled_ref[side] = scaled
        first = first + dot_exact(got_ref[side, :, AT_U:AT_LEN], scaled, contract_first)
    for block in range(NR):
        columns = slice(block * COLS, (block + 1) * COLS)
        first_ref[block] = first[:, columns]
        gain_out_ref[block] = gain_sum[:, columns]

    token = lax.broadcasted_iota(jnp.int32, (SEQ, SEQ), 0)
    lane = lax.broadcasted_iota(jnp.int32, (SEQ, SEQ), 1)
    position = lax.broadcasted_iota(jnp.int32, (SEQ, 1), 0).astype(f32)
    for pair in range(NC):
        index = index_ref[pair]
        chosen_row = lax.broadcasted_iota(jnp.int32, (GROUP, 1), 0) == index
        parts = []
        for side in range(2):
            row = jnp.sum(jnp.where(chosen_row, scaled_ref[side], 0.0), 0, keepdims=True)
            high = row.astype(bf16).astype(f32)
            mid = (row - high).astype(bf16).astype(f32)
            parts += [high, mid, row - high - mid]
            rest = jnp.where(chosen_row, got_ref[side, :, AT_RMS:WIDTH], 0.0)
            rest = jnp.sum(rest, 0, keepdims=True)
            rms_row = rest[:, :SEQ]
            count = rest[:, AT_LEN - AT_RMS : AT_LEN - AT_RMS + 1]
            rms = jnp.sum(jnp.where(token == lane, rms_row, 0.0), -1, keepdims=True)
            column = jnp.where(position < count, rms / count, 0.0)
            here = slice(side * SEQ, (side + 1) * SEQ)
            column_ref[pair, here, :] = column
            scale_ref[pair, here, :] = column * rms * rms * (1.0 / D)
        parts.append(jnp.zeros((PIECES - 6, D), f32))
        piece = jnp.concatenate(parts, 0).astype(bf16)
        for block in range(NR):
            pieces_ref[pair, block] = piece[:, block * COLS : (block + 1) * COLS]


def group_math(index, got, gain):
    spec = pl.BlockSpec(memory_space=pltpu.VMEM)
    return pl.pallas_call(
        group_kernel,
        out_shape=(
            jax.ShapeDtypeStruct((NR, SLICE, COLS), f32),
            jax.ShapeDtypeStruct((NR, 1, COLS), f32),
            jax.ShapeDtypeStruct((8, 128), f32),
            jax.ShapeDtypeStruct((NC, NR, PIECES, COLS), bf16),
            jax.ShapeDtypeStruct((NC, TOK, 1), f32),
            jax.ShapeDtypeStruct((NC, TOK, 1), f32),
        ),
        in_specs=[pl.BlockSpec(memory_space=pltpu.SMEM), spec, spec],
        out_specs=(spec,) * 6,
        scratch_shapes=[pltpu.VMEM((2, GROUP, D), f32)],
        compiler_params=pltpu.CompilerParams(vmem_limit_bytes=16 * 1024 * 1024),
        cost_estimate=pl.CostEstimate(
            flops=50 * GROUP * GROUP * D, bytes_accessed=3 * 1024 * 1024, transcendentals=4096
        ),
        name="group_math",
    )(index, got, gain)


def weight_kernel(
    own_ref, other_ref, keep_ref, given_ref, pieces_ref, scale_ref, out_ref, coef_ref, acc_ref
):
    token = lax.broadcasted_iota(jnp.int32, (TOK, PIECES), 0)
    part = lax.broadcasted_iota(jnp.int32, (TOK, PIECES), 1)
    part = part - jnp.where(token < SEQ, 0, 3)
    mask = (part >= 0) & (part < 3)
    scaled = []
    for pair, (state_ref, attn_ref) in enumerate(
        ((own_ref, keep_ref), (other_ref, given_ref))
    ):
        inner = jnp.zeros((TOK, PIECES), f32)
        for block in range(NT):
            inner = inner + dot_last(state_ref[block], pieces_ref[pair, block])
        inner = jnp.sum(jnp.where(mask, inner, 0.0), -1, keepdims=True)
        coef = scale_ref[pair] * inner
        coef_ref[pair] = coef
        scaled.append((attn_ref[...].astype(f32) * coef).astype(bf16))
    for block in range(NT):
        acc_ref[block] = lax.dot_general(
            scaled[0], own_ref[block], contract_first, preferred_element_type=f32
        ) + lax.dot_general(
            scaled[1], other_ref[block], contract_first, preferred_element_type=f32
        )
    for place in range(NX * NY):
        rows = [
            acc_ref[block, place * SLICE : (place + 1) * SLICE, :] for block in range(NR)
        ]
        out_ref[place] = jnp.concatenate(rows, 0).astype(bf16)


def weight_partials(own, other, keep, given, pieces, scale):
    spec = pl.BlockSpec(memory_space=pltpu.VMEM)
    return pl.pallas_call(
        weight_kernel,
        out_shape=(
            jax.ShapeDtypeStruct((NX * NY, NR * SLICE, COLS), bf16),
            jax.ShapeDtypeStruct((NC, TOK, 1), f32),
        ),
        in_specs=[spec] * 6,
        out_specs=(spec, spec),
        scratch_shapes=[pltpu.VMEM((NR, HALF, COLS), f32)],
        compiler_params=pltpu.CompilerParams(vmem_limit_bytes=24 * 1024 * 1024),
        cost_estimate=pl.CostEstimate(
            flops=4 * TOK * HALF * D, bytes_accessed=8 * 1024 * 1024, transcendentals=0
        ),
        name="weight_partials",
    )(own, other, keep, given, pieces, scale)


def sum_kernel(spread_ref, out_ref, acc_ref):
    step = pl.program_id(0)
    part = spread_ref[0].astype(f32)
    for place in range(1, spread_ref.shape[0]):
        part = part + spread_ref[place].astype(f32)

    @pl.when(step == 0)
    def _():
        acc_ref[...] = part

    @pl.when(step > 0)
    def _():
        acc_ref[...] += part

    @pl.when(step == NX - 1)
    def _():
        for block in range(NR):
            out_ref[block] = acc_ref[block * SLICE : (block + 1) * SLICE, :].astype(bf16)


def sum_senders(spread):
    return pl.pallas_call(
        sum_kernel,
        grid=(NX,),
        out_shape=jax.ShapeDtypeStruct((NR, SLICE, COLS), bf16),
        in_specs=[pl.BlockSpec((NY, NR * SLICE, COLS), lambda step: (step, 0, 0))],
        out_specs=pl.BlockSpec((NR, SLICE, COLS), lambda step: (0, 0, 0)),
        scratch_shapes=[pltpu.VMEM((NR * SLICE, COLS), f32)],
        compiler_params=pltpu.CompilerParams(vmem_limit_bytes=16 * 1024 * 1024),
        cost_estimate=pl.CostEstimate(
            flops=NX * NY * NR * SLICE * COLS, bytes_accessed=4 * 1024 * 1024, transcendentals=0
        ),
        name="sum_senders",
    )(spread)


def join_kernel(whole_ref, out_ref):
    for core in range(NC):
        rows = [whole_ref[place * NC + core].astype(f32) for place in range(NX * NY)]
        out_ref[core * HALF : (core + 1) * HALF, :] = jnp.concatenate(rows, 0).astype(bf16)


def join_slices(whole):
    spec = pl.BlockSpec(memory_space=pltpu.VMEM)
    return pl.pallas_call(
        join_kernel,
        out_shape=jax.ShapeDtypeStruct((FEAT, COLS), bf16),
        in_specs=[spec],
        out_specs=spec,
        compiler_params=pltpu.CompilerParams(vmem_limit_bytes=16 * 1024 * 1024),
        cost_estimate=pl.CostEstimate(
            flops=0, bytes_accessed=4 * 1024 * 1024, transcendentals=0
        ),
        name="join_slices",
    )(whole)


def attn_kernel(
    shift_ref, own_hbm, other_hbm, pieces_ref, w_hbm, coef_ref, first_ref, keep_ref, give_ref,
    state_ref, w_ref, state_sems, w_sems,
):
    shift = shift_ref[0]
    columns = w_ref.shape[1]
    loads = []
    for block in range(NX):
        which = lax.rem(shift + block, NR)
        loads.append(
            [pltpu.make_async_copy(w_hbm.at[block], w_ref.at[block], w_sems.at[block])]
            + [
                pltpu.make_async_copy(
                    source.at[which],
                    state_ref.at[pair * NX + block],
                    state_sems.at[pair * NX + block],
                )
                for pair, source in enumerate((own_hbm, other_hbm))
            ]
        )
        for load in loads[block]:
            load.start()
    tokens = [jnp.zeros((TOK, columns), f32) for pair in range(NC)]
    rows = [jnp.zeros((PIECES, columns), f32) for pair in range(NC)]
    for block in range(NX):
        which = lax.rem(shift + block, NR)
        for load in loads[block]:
            load.wait()
        for pair in range(NC):
            tokens[pair] = tokens[pair] + dot_last(state_ref[pair * NX + block], w_ref[block])
            rows[pair] = rows[pair] + dot_last(pieces_ref[pair, which], w_ref[block])
    for pair, out_ref in enumerate((keep_ref, give_ref)):
        for side in range(2):
            at = 3 * side
            row = rows[pair][at + 2 : at + 3] + rows[pair][at + 1 : at + 2]
            row = row + rows[pair][at : at + 1]
            here = slice(side * SEQ, (side + 1) * SEQ)
            out_ref[here, :] = (
                first_ref[pair, here, :] * row - coef_ref[pair, here, :] * tokens[pair][here]
            ).astype(bf16)


def attn_grads(shift, own, other, pieces, w_all, coef, first):
    spec = pl.BlockSpec(memory_space=pltpu.VMEM)
    hbm = pl.BlockSpec(memory_space=pltpu.HBM)
    columns = w_all.shape[1]
    out = jax.ShapeDtypeStruct((TOK, columns), bf16)
    return pl.pallas_call(
        attn_kernel,
        out_shape=(out, out),
        in_specs=[pl.BlockSpec(memory_space=pltpu.SMEM), hbm, hbm, spec, hbm, spec, spec],
        out_specs=(spec, spec),
        scratch_shapes=[
            pltpu.VMEM((NC * NX, TOK, FEAT), bf16),
            pltpu.VMEM((NX, columns, COLS), bf16),
            pltpu.SemaphoreType.DMA((NC * NX,)),
            pltpu.SemaphoreType.DMA((NX,)),
        ],
        compiler_params=pltpu.CompilerParams(vmem_limit_bytes=58 * 1024 * 1024),
        cost_estimate=pl.CostEstimate(
            flops=4 * TOK * columns * D, bytes_accessed=8 * 1024 * 1024, transcendentals=0
        ),
        name="attn_grads",
    )(shift, own, other, pieces, w_all, coef, first)


def body(hidden_state, attn_out, o_weight, norm_gain, lengths, positive):
    ix, iy, ic = lax.axis_index("x"), lax.axis_index("y"), lax.axis_index("c")
    it, ir = lax.axis_index("t"), lax.axis_index("r")
    dp_index = (ix * NY + iy) * NC + ic

    state = hidden_state.reshape(TOK, FEAT)
    attn = attn_out.reshape(TOK, FEAT)
    state_all = lax.all_gather(state, "t")
    w_routes = [
        ((i * NC + k) * NR + (j + i + 2 * k) % NR, (i * NC + k) * NR + j)
        for i in range(NX)
        for k in range(NC)
        for j in range(NR)
    ]
    w_moved = lax.ppermute(
        lax.dynamic_slice(o_weight, (ic * HALF + iy * W_ROWS, 0), (W_ROWS, COLS)),
        ("x", "c", "r"),
        w_routes,
    )
    attn_keep = jnp.where(ic == 0, attn[:, :HALF], attn[:, HALF:])
    attn_give = jnp.where(ic == 0, attn[:, HALF:], attn[:, :HALF])
    attn_other = swap_core(attn_give)

    states = state.astype(f32).reshape(2, SEQ, FEAT)
    square = lax.psum(jnp.sum(states * states, -1), "t") / D
    inv_rms = lax.rsqrt(square + epsilon)
    token_count = lengths.reshape(2).astype(f32)
    valid = (jnp.arange(SEQ, dtype=jnp.int32)[None, :] < lengths.reshape(2)[:, None]).astype(f32)
    pool_weight = valid * inv_rms / token_count[:, None]
    pooled = jnp.sum(pool_weight[..., None] * states, 1)
    attn_pool = jnp.sum(pool_weight[..., None] * attn.astype(f32).reshape(2, SEQ, FEAT), 1)

    near = jnp.concatenate([pooled, norm_gain[None]], 0)
    near = lax.all_to_all(jnp.broadcast_to(near[None], (NT, 3, FEAT)), "t", 0, 0)
    pooled_row = near[:, :2].transpose(1, 0, 2).reshape(2, D)
    gain = near[:, 2].reshape(1, D)

    u_parts = attn_pool.reshape(2, NC, NX * NY, SLICE).transpose(2, 1, 0, 3)
    u_parts = u_parts.reshape(GROUP, 2, SLICE)
    extra = jnp.stack(
        [token_count, jnp.broadcast_to(positive.astype(f32), (2,))], -1
    )
    row = jnp.concatenate([pooled_row, inv_rms], -1)
    send = jnp.concatenate(
        [
            jnp.broadcast_to(row[None], (GROUP, 2, D + SEQ)),
            u_parts,
            jnp.broadcast_to(extra[None], (GROUP, 2, 2)),
            jnp.zeros((GROUP, 2, WIDTH - AT_POS - 1), f32),
        ],
        -1,
    )
    got = lax.all_to_all(send, DP, 0, 0)
    got, attn_other = lax.optimization_barrier((got, attn_other))

    other_index = dp_index + 1 - 2 * ic
    got, state_all = lax.optimization_barrier((got, state_all))
    state_other = swap_core(state_all)
    first, gain_part, loss_part, pieces, scale, first_col = group_math(
        jnp.stack([dp_index, other_index]), got.transpose(1, 0, 2), gain
    )

    partial, coef = weight_partials(
        state_all, state_other, attn_keep, attn_other, pieces, scale
    )
    partial, first, w_moved = lax.optimization_barrier((partial, first, w_moved))
    w_all = lax.all_gather(w_moved, PLANE).reshape(NX, HALF, COLS)
    spread = lax.all_to_all(partial, PLANE, 0, 0)

    gain_mine = lax.dynamic_index_in_dim(gain_part, it, 0, keepdims=False)
    tail = jnp.concatenate([gain_mine, jnp.broadcast_to(loss_part[:1, :1], (1, FEAT))], 0)
    tails = [tail]
    first_sum = lax.dynamic_index_in_dim(first, ir, 0, keepdims=False)
    for step in range(1, NR):
        outgoing = lax.dynamic_index_in_dim(first, (ir + step) % NR, 0, keepdims=False)
        arrived = lax.ppermute(
            jnp.concatenate([outgoing, tail], 0),
            "r",
            [(j, (j + step) % NR) for j in range(NR)],
        )
        first_sum = first_sum + arrived[:SLICE]
        tails.append(arrived[SLICE:])
    tails = jnp.stack(tails)
    totals = jnp.zeros((2, FEAT), f32)
    for source in range(NR):
        totals = totals + lax.dynamic_index_in_dim(
            tails, (ir - source) % NR, 0, keepdims=False
        )

    row_here = lax.dynamic_index_in_dim(pieces[0], it, 0, keepdims=False)[:6]
    row_here = row_here.astype(f32).reshape(2, 3, FEAT)
    row_here = (row_here[:, :1] + row_here[:, 1:2]) + row_here[:, 2:]
    state_grad = first_col[0].reshape(2, SEQ, 1) * row_here - states * coef[0].reshape(2, SEQ, 1)
    grad_hidden = state_grad.astype(bf16).reshape(1, 2, SEQ, FEAT)
    spread, first_sum, totals, grad_hidden = lax.optimization_barrier(
        (spread, first_sum, totals, grad_hidden)
    )
    second = lax.all_to_all(sum_senders(spread), "r", 0, 0)
    second_sum = jnp.sum(second.astype(f32), 0)
    total = first_sum - second_sum
    done = jnp.broadcast_to(total.astype(bf16)[None], (GROUP, SLICE, COLS))
    whole = lax.all_to_all(done, DP, 0, 0)
    keep, give = attn_grads(
        (ir + 2 * ic).reshape(1), state_all, state_other, pieces, w_all, coef, first_col
    )
    arrived = swap_core(give)
    grad_attn = jnp.where(
        ic == 0, jnp.concatenate([keep, arrived], 1), jnp.concatenate([arrived, keep], 1)
    ).reshape(1, 2, SEQ, FEAT)
    whole, grad_attn = lax.optimization_barrier((whole, grad_attn))
    grad_weight = join_slices(whole)
    return (grad_hidden, grad_attn, grad_weight, totals[0], totals[1, 0])


def solution(mesh):
    fine = Mesh(mesh.devices.reshape(NX, NY, NC, NT, NR), ("x", "y", "c", "t", "r"))
    pairs = ("x", "y", "c", "r")
    placed = (
        P(pairs, None, None, "t"),
        P(pairs, None, None, "t"),
        P("t", "r"),
        P("t"),
        P(pairs, None),
        P(pairs),
    )
    return jax.shard_map(
        body,
        mesh=fine,
        in_specs=placed,
        out_specs=(
            P(pairs, None, None, "t"),
            P(pairs, None, None, "t"),
            P("t", "r"),
            P("t"),
            P(),
        ),
        check_vma=False,
    )
```
